512 devices in a mesh: region: 8 (over z_hi, x), blk: 64 (over z_lo, y, core).
Axes of the slice: x: 4, y: 4, z: 16 (z_hi: 2, z_lo: 8; z = z_hi * 8 + z_lo), core: 2. Of those that a mesh axis runs over, the one named last changes fastest.
Arguments:
- archive: bfloat16 [65536, 6, 1024], P(('region', 'blk')), may hold values from -6 to 6
- unit_of: int32 [65536], P(('region', 'blk')), may hold values from 0 to 4095, as said below
- row_counts: int32 [512], P(('region', 'blk')), may hold values from 0 to 128, as said below
Outputs:
- cycle_stack: bfloat16 [1024, 4, 2, 9, 2048], P(('region', 'blk'))
- region_stack: bfloat16 [1024, 2, 9, 2048], P(('region', 'blk'))
The draws below stay inside these ranges and needn't reach their ends.
Inputs may be any that keep to these rules, and one draw needn't show every extreme that they name: `unit_of`: the first row_counts slots of each archive shard are live; over the live slots of a region's 64 shards every unit 0 .. 4095 appears exactly once. A shard holds at most 2 live units of one owner block (unit // 64), and some shard holds exactly 2 of some owner. Slots past the count hold arbitrary unit numbers. `row_counts`: the counts of one region's shards sum to 4096; in every region some shard has 128 live slots and some has none.
All inputs are finite; a program needn't handle non-finite values.
Results may differ from the reference program's by a relative error of at most 0.0068.
Values may be sent and summed in bfloat16 or wider, within the bound.
No kernel may reach another device: no remote copies, remote signals or barrier semaphores. Data moves between devices by JAX's collectives and lax.ppermute only.
A program may use at most 64 MiB of HBM per device.

```python
import math
import jax
import jax.numpy as jnp
from jax import lax

SB = 2
SEGS = 32
F = 1024
LAGS = 2048
HALF = 24
STEPS = 4
REGIONS = 8
BLOCKS = 64
UNITS = 64
CAP = 128
SLOT = 2
ROWS_ALL = 65536


def shuffled_rows(base_key, count, length):

    def one_shuffle(row_key):
        return jax.random.permutation(row_key, length)
    return jax.vmap(one_shuffle)(jax.random.split(base_key, count))


def one_region(region_key):
    keys = jax.random.split(region_key, 6)
    shard_order = jax.random.permutation(keys[0], BLOCKS)
    levels = jax.random.randint(keys[1], (BLOCKS // 2,), 0, 5).at[0].set(4)
    coins = jax.random.randint(keys[2], (BLOCKS // 2, BLOCKS), 0, 4)
    heavy = (coins < levels[:, None]).astype(jnp.int32)
    share = UNITS // BLOCKS
    paired = jnp.stack([share * (1 + heavy), share * (1 - heavy)], axis=1).reshape(BLOCKS, BLOCKS)
    loads = jnp.zeros((BLOCKS, BLOCKS), jnp.int32).at[shard_order].set(paired)
    counts = jnp.sum(loads, axis=1)
    place = jnp.arange(SLOT, dtype=jnp.int32)
    occupied = place[None, None, :] < loads[:, :, None]
    first = jnp.cumsum(loads, axis=0) - loads
    order_in_owner = jnp.minimum(first[:, :, None] + place[None, None, :], UNITS - 1)
    shuffles = shuffled_rows(keys[3], BLOCKS, UNITS)
    owner_index = jnp.broadcast_to(jnp.arange(BLOCKS, dtype=jnp.int32)[None, :, None], (BLOCKS, BLOCKS, SLOT))
    picked = shuffles[owner_index, order_in_owner]
    units = (owner_index * UNITS + picked).reshape(BLOCKS, CAP)
    occupied = occupied.reshape(BLOCKS, CAP).astype(jnp.int32)
    priority = shuffled_rows(keys[4], BLOCKS, CAP)
    sort_key = (1 - occupied) * CAP + priority
    arranged = jnp.take_along_axis(units, jnp.argsort(sort_key, axis=1), axis=1)
    filler = jax.random.randint(keys[5], (BLOCKS, CAP), 0, UNITS * BLOCKS)
    cap_index = jnp.arange(CAP, dtype=jnp.int32)
    result = jnp.where(cap_index[None, :] < counts[:, None], arranged, filler)
    return (result.astype(jnp.int32), counts.astype(jnp.int32))


def route_plan(base_key):

    def region_key_of(region_number):
        return jax.random.fold_in(base_key, region_number)
    region_keys = jax.vmap(region_key_of)(jnp.arange(REGIONS, dtype=jnp.int32))
    return jax.vmap(one_region)(region_keys)


def draw_unit_of(key, part):
    planned = route_plan(key)
    return planned[0].reshape(-1)


def draw_row_counts(key, part):
    planned = route_plan(key)
    return planned[1].reshape(-1)


def level_of(key, shape, pieces, least, largest):
    gain, own = 1.0, jax.random.fold_in(key, 6)
    for position, blocks in pieces:
        draws = jnp.exp(jax.random.uniform(jax.random.fold_in(own, position), (blocks,), jnp.float32, least / len(pieces), largest / len(pieces)))
        gain = gain * jnp.repeat(draws, shape[position] // blocks).reshape([-1 if axis == position else 1 for axis in range(len(shape))])
    return gain


def scatter_about(own_key, extent, width, most, cuts=(), kind=jnp.bfloat16):
    values = jax.random.normal(own_key, extent, jnp.float32) * width
    if len(cuts) > 0:
        values = level_of(own_key, extent, cuts, -0.22, 0.18) * values
    return jnp.clip(values, min=-most, max=most).astype(kind)


def setup_inputs(seed: int = 0) -> dict:
    key_list = jax.random.split(jax.random.key(seed), 4)
    archive = scatter_about(key_list[0], (ROWS_ALL, 6, F), 1.0, 6.0, ((0, 512),))
    unit_of = draw_unit_of(jax.random.fold_in(key_list[3], 71), 0)
    row_counts = draw_row_counts(jax.random.fold_in(key_list[3], 71), 0)
    return dict(archive=archive, unit_of=unit_of, row_counts=row_counts)


epsilon = 1e-05

def make_table():
    bin_index = jnp.arange(F, dtype=jnp.int32)
    lag_index = jnp.arange(LAGS, dtype=jnp.int32) - LAGS // 2
    phase = bin_index[:, None] * lag_index[None, :] % (2 * F)
    angle = phase.astype(jnp.float32) * (math.pi / F)
    return jnp.concatenate([jnp.cos(angle), -jnp.sin(angle)], axis=0).astype(jnp.bfloat16)

def whiten(placed):
    spectra = placed.astype(jnp.float32).reshape(UNITS, 3, 2, F)
    magnitude = lax.optimization_barrier(jnp.mean(jnp.sqrt(spectra[:, :, 0] * spectra[:, :, 0] + spectra[:, :, 1] * spectra[:, :, 1]), axis=1))
    padded = jnp.pad(magnitude, ((0, 0), (HALF, HALF)))
    window_sum = padded[:, 0:F]
    for offset in range(1, 2 * HALF + 1):
        window_sum = window_sum + padded[:, offset:offset + F]
    bin_index = jnp.arange(F, dtype=jnp.int32)
    bin_count = (jnp.minimum(bin_index + HALF, F - 1) - jnp.maximum(bin_index - HALF, 0) + 1).astype(jnp.float32)
    level_mean = window_sum / bin_count + epsilon
    return (spectra / level_mean[:, None, None, :]).reshape(UNITS, 6, F).astype(jnp.bfloat16)

def cross_lags(mine_block, other_block, lag_table):
    mine_parts = mine_block.astype(jnp.float32).reshape(SB, SEGS, 3, 2, F)
    other_parts = other_block.astype(jnp.float32).reshape(SB, SEGS, 3, 2, F)
    mine_real, mine_imag = (mine_parts[:, :, :, 0], mine_parts[:, :, :, 1])
    other_real, other_imag = (other_parts[:, :, :, 0], other_parts[:, :, :, 1])
    form = 'iscf,jsdf->ijcdf'
    real_part = jnp.einsum(form, mine_real, other_real) + jnp.einsum(form, mine_imag, other_imag)
    imag_part = jnp.einsum(form, mine_imag, other_real) - jnp.einsum(form, mine_real, other_imag)
    stacked = jnp.concatenate([real_part, imag_part], axis=-1).astype(jnp.bfloat16).reshape(SB * SB * 9, 2 * F)
    series = jnp.dot(stacked, lag_table, preferred_element_type=jnp.float32) * (1.0 / math.sqrt(F * SEGS))
    return series.astype(jnp.bfloat16).reshape(SB, SB, 9, LAGS)

def reference(archive, unit_of, row_counts):
    shard_total = REGIONS * BLOCKS
    slot_index = jnp.arange(CAP, dtype=jnp.int32)
    live_slot = slot_index[None, :] < row_counts[:, None]
    region_base = (jnp.arange(shard_total, dtype=jnp.int32) // BLOCKS)[:, None] * (UNITS * BLOCKS)
    target = jnp.where(live_slot, region_base + unit_of.reshape(shard_total, CAP), shard_total * UNITS)
    routed = jnp.zeros((shard_total * UNITS, 6, F), jnp.bfloat16).at[target.reshape(-1)].set(archive, mode='drop')
    whitened = lax.map(whiten, routed.reshape(shard_total, UNITS, 6, F))
    lag_table = make_table()

    def one_device(device):
        region_at = device // BLOCKS
        block_at = device % BLOCKS
        mine = whitened[device]
        cycle_list = []
        for offset in range(1, STEPS + 1):
            partner = region_at * BLOCKS + (block_at - offset) % BLOCKS
            cycle_list.append(cross_lags(mine, whitened[partner], lag_table))
        neighbour = (region_at - 1) % REGIONS * BLOCKS + block_at
        across = cross_lags(mine, whitened[neighbour], lag_table)
        return (jnp.stack(cycle_list, axis=1), across)
    cycle_all, across_all = lax.map(one_device, jnp.arange(shard_total, dtype=jnp.int32))
    return (cycle_all.reshape(shard_total * SB, STEPS, SB, 9, LAGS), across_all.reshape(shard_total * SB, SB, 9, LAGS))
```

```python
import functools
import math

import jax
import jax.numpy as jnp
from jax import lax
from jax.experimental import pallas as pl
from jax.experimental.pallas import tpu as pltpu
from jax.sharding import PartitionSpec as P

SB = 2
SEGS = 32
F = 1024
LAGS = 2048
HALF = 24
STEPS = 4
UNITS = 64
CAP = 128
LANES = 128
FH = F // LANES
TILE = 2 * FH
epsilon = 1e-05

CHUNKS = ((0, 1, 2),)
GROUP = 32
VMEM = pl.BlockSpec(memory_space=pltpu.VMEM)
SMEM = pl.BlockSpec(memory_space=pltpu.SMEM)


def pairs_of(chunk):
    before = [c for part in CHUNKS[:chunk] for c in part]
    now = before + list(CHUNKS[chunk])
    return [(c, d) for c in now for d in now if not (c in before and d in before)]


def place_of(component):
    for chunk, part in enumerate(CHUNKS):
        if component in part:
            return chunk, part.index(component)


def whiten_kernel(source_ref, band_ref, inverse_ref, archive_ref, *rest):
    outs, (level_ref,) = rest[:-1], rest[-1:]
    base = pl.program_id(0) * GROUP
    rows = GROUP * FH

    def slab_of(position):
        return archive_ref[source_ref[base + position]].astype(jnp.float32)

    def magnitude(position, carry):
        slab = slab_of(position)
        total = None
        for c in range(3):
            real = slab[c * TILE : c * TILE + FH]
            imag = slab[c * TILE + FH : (c + 1) * TILE]
            size = jnp.sqrt(real * real + imag * imag)
            total = size if total is None else total + size
        level_ref[pl.ds(pl.multiple_of(FH + position * FH, FH), FH), :] = total * (1.0 / 3.0)
        return carry

    lax.fori_loop(0, GROUP, magnitude, 0, unroll=4)
    here = level_ref[FH : FH + rows, :]
    before = level_ref[FH - 1 : FH - 1 + rows, :]
    after = level_ref[FH + 1 : FH + 1 + rows, :]
    lane = lax.broadcasted_iota(jnp.int32, (rows, LANES), 1)
    row = lax.broadcasted_iota(jnp.int32, (rows, LANES), 0) % FH
    edge = jnp.where(
        lane >= LANES // 2,
        jnp.where(row == 0, 0.0, before),
        jnp.where(row == FH - 1, 0.0, after),
    )
    spread = jnp.concatenate([here, edge], axis=1)
    high = spread.astype(jnp.bfloat16)
    low = (spread - high.astype(jnp.float32)).astype(jnp.bfloat16)
    band = band_ref[...]
    window = jnp.dot(high, band, preferred_element_type=jnp.float32) + jnp.dot(
        low, band, preferred_element_type=jnp.float32
    )
    level = window.reshape(GROUP, FH, LANES) * inverse_ref[...][None] + epsilon
    level_ref[FH : FH + rows, :] = (1.0 / level).reshape(rows, LANES)

    def divide(position, carry):
        slab = slab_of(position)
        gain = level_ref[pl.ds(pl.multiple_of(FH + position * FH, FH), FH), :]
        for out, part in zip(outs, CHUNKS):
            pieces = []
            for c in part:
                for half in range(2):
                    start = c * TILE + half * FH
                    pieces.append(slab[start : start + FH] * gain)
            out[position] = jnp.concatenate(pieces, axis=0).astype(jnp.bfloat16)
        return carry

    lax.fori_loop(0, GROUP, divide, 0, unroll=4)


def whiten(source, archive):
    low = jnp.arange(LANES, dtype=jnp.int32)
    gap = jnp.abs(low[:, None] - low[None, :])
    band = jnp.concatenate([gap <= HALF, gap >= LANES - HALF], axis=0).astype(jnp.bfloat16)
    bin_index = jnp.arange(F, dtype=jnp.int32)
    bin_count = (
        jnp.minimum(bin_index + HALF, F - 1) - jnp.maximum(bin_index - HALF, 0) + 1
    ).astype(jnp.float32)
    inverse = (1.0 / bin_count).reshape(FH, LANES)
    sizes = [len(part) * TILE for part in CHUNKS]
    return pl.pallas_call(
        whiten_kernel,
        grid=(CAP // GROUP,),
        in_specs=[SMEM, VMEM, VMEM, VMEM],
        out_specs=[pl.BlockSpec((GROUP, size, LANES), lambda g: (g, 0, 0)) for size in sizes],
        out_shape=[jax.ShapeDtypeStruct((CAP, size, LANES), jnp.bfloat16) for size in sizes],
        scratch_shapes=[pltpu.VMEM((GROUP * FH + 2 * FH, LANES), jnp.float32)],
        compiler_params=pltpu.CompilerParams(vmem_limit_bytes=16 * 1024 * 1024),
        cost_estimate=pl.CostEstimate(flops=200_000_000, bytes_accessed=4_000_000, transcendentals=0),
        name="whiten",
    )(source, band, inverse, archive)


def sort_kernel(source_ref, got_ref, out_ref):
    def move(unit, carry):
        out_ref[unit] = got_ref[source_ref[unit]]
        return carry

    lax.fori_loop(0, UNITS, move, 0, unroll=8)


def sort_units(source, got):
    return pl.pallas_call(
        sort_kernel,
        in_specs=[SMEM, VMEM],
        out_specs=VMEM,
        out_shape=jax.ShapeDtypeStruct((UNITS,) + got.shape[1:], jnp.bfloat16),
        compiler_params=pltpu.CompilerParams(vmem_limit_bytes=16 * 1024 * 1024),
        cost_estimate=pl.CostEstimate(flops=0, bytes_accessed=3_000_000, transcendentals=0),
        name="sort_units",
    )(source, got)


def products(mine, other, chunk, store):
    pairs = pairs_of(chunk)

    def load(refs, unit, component):
        which, at = place_of(component)
        tile = refs[which][unit, at * TILE : (at + 1) * TILE, :].astype(jnp.float32)
        return tile[:FH], tile[FH:]

    firsts = sorted({c for c, _ in pairs})
    seconds = sorted({d for _, d in pairs})
    for i in range(SB):
        for j in range(SB):

            def step(m, sums):
                left = {c: load(mine, i * SEGS + m, c) for c in firsts}
                right = {d: load(other, j * SEGS + m, d) for d in seconds}
                new = []
                for n, (c, d) in enumerate(pairs):
                    real, imag = sums[n]
                    (ar, ai), (br, bi) = left[c], right[d]
                    new.append((real + ar * br + ai * bi, imag + ai * br - ar * bi))
                return tuple(new)

            zero = jnp.zeros((FH, LANES), jnp.float32)
            sums = lax.fori_loop(
                0, SEGS, step, tuple((zero, zero) for _ in pairs), unroll=2
            )
            for n, (real, imag) in enumerate(sums):
                store(i, j, n, jnp.concatenate([real, imag], axis=0).astype(jnp.bfloat16))


def cross_kernel(chunk, plan, flag_ref, *refs):
    depth = chunk + 1
    blocks = [refs[n : n + depth] for n in range(0, len(refs) - len(plan), depth)]
    outs = refs[len(refs) - len(plan) :]
    for out, (left, when_zero, when_one) in zip(outs, plan):

        def store(i, j, n, tile, out=out):
            out[i * SB + j, n] = tile

        if when_zero == when_one:
            products(blocks[left], blocks[when_zero], chunk, store)
        else:
            for value, right in ((0, when_zero), (1, when_one)):

                @pl.when(flag_ref[0] == value)
                def _(right=right, left=left, store=store):
                    products(blocks[left], blocks[right], chunk, store)


def cross(chunk, plan, flag, *blocks):
    count = len(pairs_of(chunk))
    shape = (SB * SB, count, TILE, LANES)
    flat = [part for block in blocks for part in block[: chunk + 1]]
    return pl.pallas_call(
        functools.partial(cross_kernel, chunk, plan),
        in_specs=[SMEM] + [VMEM] * len(flat),
        out_specs=[VMEM] * len(plan),
        out_shape=[jax.ShapeDtypeStruct(shape, jnp.bfloat16)] * len(plan),
        compiler_params=pltpu.CompilerParams(vmem_limit_bytes=24 * 1024 * 1024),
        cost_estimate=pl.CostEstimate(
            flops=len(plan) * 40_000_000, bytes_accessed=len(plan) * 1_500_000, transcendentals=0
        ),
        name="cross",
    )(flag.reshape(1), *flat)


COLUMNS = 256
CYCLE_ROWS = SB * STEPS * 9 * SB
ALL_ROWS = CYCLE_ROWS + SB * 9 * SB


def series_kernel(table_ref, *refs):
    chunks = len(CHUNKS)
    sources = refs[: (STEPS + 1) * chunks]
    cycle_ref, region_ref, wide_ref, rows_ref = refs[(STEPS + 1) * chunks :]

    @pl.when(pl.program_id(0) == 0)
    def _():
        for k in range(STEPS + 1):
            for chunk in range(chunks):
                source = sources[k * chunks + chunk]
                for i in range(SB):
                    for j in range(SB):
                        for n, (c, d) in enumerate(pairs_of(chunk)):
                            if k < STEPS:
                                row = ((i * STEPS + k) * 9 + 3 * c + d) * SB + j
                            else:
                                row = CYCLE_ROWS + (i * 9 + 3 * c + d) * SB + j
                            wide_ref[row * TILE : (row + 1) * TILE, :] = source[
                                i * SB + j, n
                            ].astype(jnp.float32)
        for piece in range(TILE):
            rows_ref[:, piece * LANES : (piece + 1) * LANES] = wide_ref[
                pl.ds(piece, ALL_ROWS, stride=TILE), :
            ].astype(jnp.bfloat16)

    series = jnp.dot(rows_ref[...], table_ref[...], preferred_element_type=jnp.float32)
    series = (series * (1.0 / math.sqrt(F * SEGS))).astype(jnp.bfloat16)
    for i in range(SB):
        for k in range(STEPS):
            for n in range(9):
                row = ((i * STEPS + k) * 9 + n) * SB
                cycle_ref[i, k, n] = series[row : row + SB]
        for n in range(9):
            row = CYCLE_ROWS + (i * 9 + n) * SB
            region_ref[i, n] = series[row : row + SB]


def lag_series(table, sources):
    return pl.pallas_call(
        series_kernel,
        grid=(LAGS // COLUMNS,),
        in_specs=[pl.BlockSpec((2 * F, COLUMNS), lambda n: (0, n))] + [VMEM] * len(sources),
        out_specs=[
            pl.BlockSpec((SB, STEPS, 9, SB, COLUMNS), lambda n: (0, 0, 0, 0, n)),
            pl.BlockSpec((SB, 9, SB, COLUMNS), lambda n: (0, 0, 0, n)),
        ],
        out_shape=[
            jax.ShapeDtypeStruct((SB, STEPS, 9, SB, LAGS), jnp.bfloat16),
            jax.ShapeDtypeStruct((SB, 9, SB, LAGS), jnp.bfloat16),
        ],
        scratch_shapes=[
            pltpu.VMEM((ALL_ROWS * TILE, LANES), jnp.float32),
            pltpu.VMEM((ALL_ROWS, 2 * F), jnp.bfloat16),
        ],
        compiler_params=pltpu.CompilerParams(vmem_limit_bytes=32 * 1024 * 1024),
        cost_estimate=pl.CostEstimate(
            flops=2 * ALL_ROWS * 2 * F * LAGS, bytes_accessed=12_000_000, transcendentals=0
        ),
        name="lag_series",
    )(table, *sources)


def table_kernel(fine_ref, coarse_ref, out_ref):
    step = pl.program_id(0)
    for high in range(FH):
        cos_high = coarse_ref[0, high : high + 1, :]
        sin_high = coarse_ref[1, high : high + 1, :]
        cos_low, sin_low = fine_ref[0], fine_ref[1]

        @pl.when(step == 0)
        def _(high=high):
            out_ref[high * LANES : (high + 1) * LANES, :] = (
                cos_low * cos_high - sin_low * sin_high
            ).astype(jnp.bfloat16)

        @pl.when(step == 1)
        def _(high=high):
            out_ref[high * LANES : (high + 1) * LANES, :] = (
                -(sin_low * cos_high + cos_low * sin_high)
            ).astype(jnp.bfloat16)


def make_table():
    lag_index = jnp.arange(LAGS, dtype=jnp.int32) - LAGS // 2

    def angles(bins):
        phase = bins[:, None] * lag_index[None, :] % (2 * F)
        angle = phase.astype(jnp.float32) * (math.pi / F)
        return jnp.stack([jnp.cos(angle), jnp.sin(angle)])

    fine = angles(jnp.arange(LANES, dtype=jnp.int32))
    coarse = angles(LANES * jnp.arange(FH, dtype=jnp.int32))
    width = 512
    return pl.pallas_call(
        table_kernel,
        grid=(2, LAGS // width),
        in_specs=[
            pl.BlockSpec((2, LANES, width), lambda s, n: (0, 0, n)),
            pl.BlockSpec((2, FH, width), lambda s, n: (0, 0, n)),
        ],
        out_specs=pl.BlockSpec((F, width), lambda s, n: (s, n)),
        out_shape=jax.ShapeDtypeStruct((2 * F, LAGS), jnp.bfloat16),
        compiler_params=pltpu.CompilerParams(vmem_limit_bytes=16 * 1024 * 1024),
        cost_estimate=pl.CostEstimate(flops=16_000_000, bytes_accessed=12_000_000, transcendentals=0),
        name="lag_table",
    )(fine, coarse)


def shifted(block, axis, by):
    size = lax.axis_size(axis)
    return lax.ppermute(block, axis, [(i, (i + by) % size) for i in range(size)])


def swapped(block):
    return lax.ppermute(block, "blk", [(i, i ^ 1) for i in range(lax.axis_size("blk"))])


def from_previous_region(block, planes, crossing):
    regions = lax.axis_size("region")
    groups = [list(range(n, n + planes)) for n in range(0, regions, planes)]
    near = lax.ppermute(
        block, "region", [(i, i + 1) for i in range(regions) if (i + 1) % planes]
    )
    rows = block.shape[0] // planes
    parts = lax.all_to_all(
        block, "region", split_axis=0, concat_axis=0, tiled=True, axis_index_groups=groups
    )
    part = lax.ppermute(
        parts[(planes - 1) * rows :],
        "region",
        [(i, (i + planes) % regions) for i in range(regions)],
    )
    far = lax.all_gather(part, "region", axis=0, tiled=True, axis_index_groups=groups)
    return near, far


def body(archive, unit_of, row_counts):
    blocks = lax.axis_size("blk")
    slot = jnp.arange(CAP, dtype=jnp.int32)
    ids = jnp.where(slot < row_counts[0], unit_of, -1)
    ids_all = lax.all_gather(ids, "blk")

    owners = jnp.arange(blocks, dtype=jnp.int32)
    sent = (ids >> 6)[None, :] == owners[:, None]
    first = jnp.min(jnp.where(sent, slot, CAP - 1), axis=1)
    last = jnp.max(jnp.where(sent, slot, 0), axis=1)
    source = jnp.stack([first, last], axis=1).reshape(2 * blocks)
    send = whiten(source, archive.reshape(CAP, 3 * TILE, LANES))

    got = []
    for part in send:
        rows = part.shape[1]
        moved = lax.all_to_all(
            part.reshape(blocks, 2 * rows, LANES), "blk", split_axis=0, concat_axis=0, tiled=True
        )
        got.append(moved.reshape(2 * blocks, rows, LANES))

    table = make_table()
    index = lax.axis_index("blk")
    mine = (ids_all >> 6) == index
    key = slot[None, :] * UNITS + (ids_all & (UNITS - 1))
    none = CAP * UNITS
    low = jnp.min(jnp.where(mine, key, none), axis=1)
    high = jnp.max(jnp.where(mine, key, -1), axis=1)
    units = jnp.arange(UNITS, dtype=jnp.int32)[:, None]
    in_first = (low < none)[None, :] & ((low & (UNITS - 1))[None, :] == units)
    in_second = (high > low)[None, :] & ((high & (UNITS - 1))[None, :] == units)
    place = jnp.sum(
        jnp.where(in_first, 2 * owners[None, :], 0)
        + jnp.where(in_second, 2 * owners[None, :] + 1, 0),
        axis=1,
    )
    place = jnp.clip(place, 0, 2 * blocks - 1)

    core = index & 1
    planes = 4
    edge = (lax.axis_index("region") % planes == 0).astype(jnp.int32)
    own, twin, two, four, near, far = [], [], [], [], [], []
    cycle = [[], [], [], []]
    region = []
    for chunk in range(len(CHUNKS)):
        block = sort_units(place, got[chunk])
        own.append(block)
        closer, further = from_previous_region(block, planes, edge)
        two.append(shifted(block, "blk", 2))
        twin.append(swapped(block))
        four.append(shifted(block, "blk", 4))
        near.append(closer)
        far.append(further)
        by_two, for_one = cross(
            chunk, ((0, 2, 2), (1, 0, 2)), core, own, twin, two
        )
        by_four, for_three = cross(
            chunk, ((0, 3, 3), (1, 2, 3)), core, own, twin, two, four
        )
        by_one, by_three = swapped(for_one), swapped(for_three)
        for k, result in enumerate((by_one, by_two, by_three, by_four)):
            cycle[k].append(result)
        region.extend(cross(chunk, ((0, 1, 2),), edge, own, near, far))

    sources = [result for k in range(STEPS) for result in cycle[k]] + region
    cycle_series, region_series = lag_series(table, sources)
    return jnp.swapaxes(cycle_series, 2, 3), jnp.swapaxes(region_series, 1, 2)


def solution(mesh):
    placed = (P(("region", "blk"), None, None), P(("region", "blk")), P(("region", "blk")))
    return jax.shard_map(
        body,
        mesh=mesh,
        in_specs=placed,
        out_specs=(
            P(("region", "blk"), None, None, None, None),
            P(("region", "blk"), None, None, None),
        ),
        check_vma=False,
    )
```

```python
import functools
import math

import jax
import jax.numpy as jnp
from jax import lax
from jax.experimental import pallas as pl
from jax.experimental.pallas import tpu as pltpu
from jax.sharding import PartitionSpec as P

SB = 2
SEGS = 32
F = 1024
LAGS = 2048
HALF = 24
STEPS = 4
UNITS = 64
CAP = 128
LANES = 128
FH = F // LANES
TILE = 2 * FH
epsilon = 1e-05

CHUNKS = ((0, 1, 2),)
GROUP = 32
MARK = 8
PIECE = 16
VMEM = pl.BlockSpec(memory_space=pltpu.VMEM)
SMEM = pl.BlockSpec(memory_space=pltpu.SMEM)


def pairs_of(chunk):
    before = [c for part in CHUNKS[:chunk] for c in part]
    now = before + list(CHUNKS[chunk])
    return [(c, d) for c in now for d in now if not (c in before and d in before)]


def place_of(component):
    for chunk, part in enumerate(CHUNKS):
        if component in part:
            return chunk, part.index(component)


def whiten_kernel(source_ref, band_ref, inverse_ref, archive_ref, mark_ref, *rest):
    outs, (level_ref,) = rest[:-1], rest[-1:]
    base = pl.program_id(0) * GROUP
    rows = GROUP * FH

    def slab_of(position):
        return archive_ref[source_ref[base + position]].astype(jnp.float32)

    def magnitude(position, carry):
        slab = slab_of(position)
        total = None
        for c in range(3):
            real = slab[c * TILE : c * TILE + FH]
            imag = slab[c * TILE + FH : (c + 1) * TILE]
            size = jnp.sqrt(real * real + imag * imag)
            total = size if total is None else total + size
        level_ref[pl.ds(pl.multiple_of(FH + position * FH, FH), FH), :] = total * (1.0 / 3.0)
        return carry

    lax.fori_loop(0, GROUP, magnitude, 0, unroll=4)
    here = level_ref[FH : FH + rows, :]
    before = level_ref[FH - 1 : FH - 1 + rows, :]
    after = level_ref[FH + 1 : FH + 1 + rows, :]
    lane = lax.broadcasted_iota(jnp.int32, (rows, LANES), 1)
    row = lax.broadcasted_iota(jnp.int32, (rows, LANES), 0) % FH
    edge = jnp.where(
        lane >= LANES // 2,
        jnp.where(row == 0, 0.0, before),
        jnp.where(row == FH - 1, 0.0, after),
    )
    spread = jnp.concatenate([here, edge], axis=1)
    high = spread.astype(jnp.bfloat16)
    low = (spread - high.astype(jnp.float32)).astype(jnp.bfloat16)
    band = band_ref[...]
    window = jnp.dot(high, band, preferred_element_type=jnp.float32) + jnp.dot(
        low, band, preferred_element_type=jnp.float32
    )
    level = window.reshape(GROUP, FH, LANES) * inverse_ref[...][None] + epsilon
    level_ref[FH : FH + rows, :] = (1.0 / level).reshape(rows, LANES)

    def divide(position, carry):
        slab = slab_of(position)
        gain = level_ref[pl.ds(pl.multiple_of(FH + position * FH, FH), FH), :]
        for out, part in zip(outs, CHUNKS):
            pieces = []
            for c in part:
                for half in range(2):
                    start = c * TILE + half * FH
                    pieces.append(slab[start : start + FH] * gain)
            size = len(part) * TILE
            start = pl.multiple_of((position % 2) * size, TILE)
            out[position // 2, pl.ds(start, size), :] = jnp.concatenate(pieces, axis=0).astype(
                jnp.bfloat16
            )
        return carry

    lax.fori_loop(0, GROUP, divide, 0, unroll=4)
    outs[0][:, 2 * len(CHUNKS[0]) * TILE :, :] = mark_ref[...]


def whiten(source, archive, marks):
    low = jnp.arange(LANES, dtype=jnp.int32)
    gap = jnp.abs(low[:, None] - low[None, :])
    band = jnp.concatenate([gap <= HALF, gap >= LANES - HALF], axis=0).astype(jnp.bfloat16)
    bin_index = jnp.arange(F, dtype=jnp.int32)
    bin_count = (
        jnp.minimum(bin_index + HALF, F - 1) - jnp.maximum(bin_index - HALF, 0) + 1
    ).astype(jnp.float32)
    inverse = (1.0 / bin_count).reshape(FH, LANES)
    sizes = [2 * len(part) * TILE for part in CHUNKS]
    sizes[0] += MARK
    return pl.pallas_call(
        whiten_kernel,
        grid=(CAP // GROUP,),
        in_specs=[SMEM, VMEM, VMEM, VMEM]
        + [pl.BlockSpec((GROUP // 2, MARK, LANES), lambda g: (g, 0, 0))],
        out_specs=[
            pl.BlockSpec((GROUP // 2, size, LANES), lambda g: (g, 0, 0)) for size in sizes
        ],
        out_shape=[
            jax.ShapeDtypeStruct((marks.shape[0], size, LANES), jnp.bfloat16) for size in sizes
        ],
        scratch_shapes=[pltpu.VMEM((GROUP * FH + 2 * FH, LANES), jnp.float32)],
        compiler_params=pltpu.CompilerParams(vmem_limit_bytes=16 * 1024 * 1024),
        cost_estimate=pl.CostEstimate(flops=200_000_000, bytes_accessed=4_000_000, transcendentals=0),
        name="whiten",
    )(source, band, inverse, archive, marks)


def sort_kernel(source_ref, got_ref, *rest):
    out_ref = rest[-1]
    rows = out_ref.shape[1]

    def move(unit, carry):
        place = source_ref[unit]
        start = pl.multiple_of((place & 1) * rows, TILE)
        out_ref[unit] = got_ref[place >> 1, pl.ds(start, rows), :]
        return carry

    lax.fori_loop(0, UNITS, move, 0, unroll=8)


def sort_units(source, got, rows, *after):
    return pl.pallas_call(
        sort_kernel,
        in_specs=[SMEM, VMEM] + [pl.BlockSpec(memory_space=pl.ANY)] * len(after),
        out_specs=VMEM,
        out_shape=jax.ShapeDtypeStruct((UNITS, rows, LANES), jnp.bfloat16),
        compiler_params=pltpu.CompilerParams(vmem_limit_bytes=16 * 1024 * 1024),
        cost_estimate=pl.CostEstimate(flops=0, bytes_accessed=3_000_000, transcendentals=0),
        name="sort_units",
    )(source, got, *after)


def products(left_block, right_block, chunk, store):
    pairs = pairs_of(chunk)

    def load(block, base, m, component):
        which, at = place_of(component)
        pieces = block[which]
        if len(pieces) > 1:
            ref, unit = pieces[base // PIECE], m
        else:
            ref, unit = pieces[0], base + m
        tile = ref[unit, at * TILE : (at + 1) * TILE, :].astype(jnp.float32)
        return tile[:FH], tile[FH:]

    firsts = sorted({c for c, _ in pairs})
    seconds = sorted({d for _, d in pairs})
    for i in range(SB):
        for j in range(SB):
            zero = jnp.zeros((FH, LANES), jnp.float32)
            sums = tuple((zero, zero) for _ in pairs)
            for start in range(0, SEGS, PIECE):

                def step(m, sums, start=start):
                    left = {c: load(left_block, i * SEGS + start, m, c) for c in firsts}
                    right = {d: load(right_block, j * SEGS + start, m, d) for d in seconds}
                    new = []
                    for n, (c, d) in enumerate(pairs):
                        real, imag = sums[n]
                        (ar, ai), (br, bi) = left[c], right[d]
                        new.append((real + ar * br + ai * bi, imag + ai * br - ar * bi))
                    return tuple(new)

                sums = lax.fori_loop(0, PIECE, step, sums, unroll=2)
            for n, (real, imag) in enumerate(sums):
                store(i, j, n, jnp.concatenate([real, imag], axis=0).astype(jnp.bfloat16))


def cross_kernel(chunk, plan, counts, flag_ref, *refs):
    blocks, at = [], 0
    for count in counts:
        block = []
        for _ in range(chunk + 1):
            block.append(refs[at : at + count])
            at += count
        blocks.append(block)
    out = refs[at]
    for slot, (left, when_zero, when_one) in enumerate(plan):

        def store(i, j, n, tile, slot=slot):
            out[(slot * SB + i) * SB + j, n] = tile

        if when_zero == when_one:
            products(blocks[left], blocks[when_zero], chunk, store)
        else:
            for value, right in ((0, when_zero), (1, when_one)):

                @pl.when(flag_ref[0] == value)
                def _(right=right, left=left, store=store):
                    products(blocks[left], blocks[right], chunk, store)


def cross(chunk, plan, flag, *blocks):
    count = len(pairs_of(chunk))
    shape = (len(plan) * SB * SB, count, TILE, LANES)
    flat = [piece for block in blocks for part in block[: chunk + 1] for piece in part]
    return pl.pallas_call(
        functools.partial(cross_kernel, chunk, plan, tuple(len(block[0]) for block in blocks)),
        in_specs=[SMEM] + [VMEM] * len(flat),
        out_specs=VMEM,
        out_shape=jax.ShapeDtypeStruct(shape, jnp.bfloat16),
        compiler_params=pltpu.CompilerParams(vmem_limit_bytes=24 * 1024 * 1024),
        cost_estimate=pl.CostEstimate(
            flops=len(plan) * 40_000_000, bytes_accessed=len(plan) * 1_500_000, transcendentals=0
        ),
        name="cross",
    )(flag.reshape(1), *flat)


COLUMNS = 256
CYCLE_ROWS = SB * STEPS * 9 * SB
ALL_ROWS = CYCLE_ROWS + SB * 9 * SB


def series_kernel(table_ref, *refs):
    chunks = len(CHUNKS)
    sources = refs[: 3 * chunks]
    cycle_ref, region_ref, wide_ref, rows_ref = refs[3 * chunks :]

    @pl.when(pl.program_id(0) == 0)
    def _():
        for k in range(STEPS + 1):
            for chunk in range(chunks):
                source = sources[(k // 2) * chunks + chunk]
                first = (k % 2) * SB * SB
                for i in range(SB):
                    for j in range(SB):
                        for n, (c, d) in enumerate(pairs_of(chunk)):
                            if k < STEPS:
                                row = ((i * STEPS + k) * 9 + 3 * c + d) * SB + j
                            else:
                                row = CYCLE_ROWS + (i * 9 + 3 * c + d) * SB + j
                            wide_ref[row * TILE : (row + 1) * TILE, :] = source[
                                first + i * SB + j, n
                            ].astype(jnp.float32)
        for piece in range(TILE):
            rows_ref[:, piece * LANES : (piece + 1) * LANES] = wide_ref[
                pl.ds(piece, ALL_ROWS, stride=TILE), :
            ].astype(jnp.bfloat16)

    series = jnp.dot(rows_ref[...], table_ref[...], preferred_element_type=jnp.float32)
    series = (series * (1.0 / math.sqrt(F * SEGS))).astype(jnp.bfloat16)
    for i in range(SB):
        for k in range(STEPS):
            for n in range(9):
                row = ((i * STEPS + k) * 9 + n) * SB
                cycle_ref[i, k, n] = series[row : row + SB]
        for n in range(9):
            row = CYCLE_ROWS + (i * 9 + n) * SB
            region_ref[i, n] = series[row : row + SB]


def lag_series(table, sources):
    return pl.pallas_call(
        series_kernel,
        grid=(LAGS // COLUMNS,),
        in_specs=[pl.BlockSpec((2 * F, COLUMNS), lambda n: (0, n))] + [VMEM] * len(sources),
        out_specs=[
            pl.BlockSpec((SB, STEPS, 9, SB, COLUMNS), lambda n: (0, 0, 0, 0, n)),
            pl.BlockSpec((SB, 9, SB, COLUMNS), lambda n: (0, 0, 0, n)),
        ],
        out_shape=[
            jax.ShapeDtypeStruct((SB, STEPS, 9, SB, LAGS), jnp.bfloat16),
            jax.ShapeDtypeStruct((SB, 9, SB, LAGS), jnp.bfloat16),
        ],
        scratch_shapes=[
            pltpu.VMEM((ALL_ROWS * TILE, LANES), jnp.float32),
            pltpu.VMEM((ALL_ROWS, 2 * F), jnp.bfloat16),
        ],
        compiler_params=pltpu.CompilerParams(vmem_limit_bytes=32 * 1024 * 1024),
        cost_estimate=pl.CostEstimate(
            flops=2 * ALL_ROWS * 2 * F * LAGS, bytes_accessed=12_000_000, transcendentals=0
        ),
        name="lag_series",
    )(table, *sources)


def table_kernel(fine_ref, coarse_ref, out_ref):
    step = pl.program_id(0)
    for high in range(FH):
        cos_high = coarse_ref[0, high : high + 1, :]
        sin_high = coarse_ref[1, high : high + 1, :]
        cos_low, sin_low = fine_ref[0], fine_ref[1]

        @pl.when(step == 0)
        def _(high=high):
            out_ref[high * LANES : (high + 1) * LANES, :] = (
                cos_low * cos_high - sin_low * sin_high
            ).astype(jnp.bfloat16)

        @pl.when(step == 1)
        def _(high=high):
            out_ref[high * LANES : (high + 1) * LANES, :] = (
                -(sin_low * cos_high + cos_low * sin_high)
            ).astype(jnp.bfloat16)


def make_table():
    lag_index = jnp.arange(LAGS, dtype=jnp.int32) - LAGS // 2

    def angles(bins):
        phase = bins[:, None] * lag_index[None, :] % (2 * F)
        angle = phase.astype(jnp.float32) * (math.pi / F)
        return jnp.stack([jnp.cos(angle), jnp.sin(angle)])

    fine = angles(jnp.arange(LANES, dtype=jnp.int32))
    coarse = angles(LANES * jnp.arange(FH, dtype=jnp.int32))
    width = 512
    return pl.pallas_call(
        table_kernel,
        grid=(2, LAGS // width),
        in_specs=[
            pl.BlockSpec((2, LANES, width), lambda s, n: (0, 0, n)),
            pl.BlockSpec((2, FH, width), lambda s, n: (0, 0, n)),
        ],
        out_specs=pl.BlockSpec((F, width), lambda s, n: (s, n)),
        out_shape=pltpu.HBM((2 * F, LAGS), jnp.bfloat16),
        compiler_params=pltpu.CompilerParams(vmem_limit_bytes=16 * 1024 * 1024),
        cost_estimate=pl.CostEstimate(flops=16_000_000, bytes_accessed=12_000_000, transcendentals=0),
        name="lag_table",
    )(fine, coarse)


def shifted(block, axis, by):
    size = lax.axis_size(axis)
    return lax.ppermute(block, axis, [(i, (i + by) % size) for i in range(size)])


def spread(block, planes):
    regions = lax.axis_size("region")
    groups = [list(range(n, n + planes)) for n in range(0, regions, planes)]
    parts = lax.all_to_all(
        block, "region", split_axis=0, concat_axis=0, tiled=True, axis_index_groups=groups
    )
    return parts[(planes - 1) * PIECE :]


def from_previous_region(block, piece, planes):
    regions = lax.axis_size("region")
    near = lax.ppermute(
        block, "region", [(i, i + 1) for i in range(regions) if (i + 1) % planes]
    )
    piece = lax.ppermute(piece, "region", [(i, (i + planes) % regions) for i in range(regions)])
    far = [piece]
    for plane in range(1, planes):
        far.append(
            lax.ppermute(piece, "region", [(n + plane, n) for n in range(0, regions, planes)])
        )
    return near, far


def body(archive, unit_of, row_counts):
    blocks = lax.axis_size("blk")
    slot = jnp.arange(CAP, dtype=jnp.int32)
    ids = jnp.where(slot < row_counts[0], unit_of, -1)
    owners = jnp.arange(blocks, dtype=jnp.int32)
    sent = (ids >> 6)[None, :] == owners[:, None]
    key = slot * UNITS + (ids & (UNITS - 1))
    none = CAP * UNITS
    first = jnp.min(jnp.where(sent, key, none), axis=1)
    last = jnp.max(jnp.where(sent, key, -1), axis=1)
    source = jnp.clip(jnp.stack([first, last], axis=1) >> 6, 0, CAP - 1).reshape(2 * blocks)
    first_id = jnp.where(first < none, first & (UNITS - 1), -1).astype(jnp.bfloat16)
    last_id = jnp.where(last > first, last & (UNITS - 1), -1).astype(jnp.bfloat16)
    lane = jnp.arange(LANES, dtype=jnp.int32)
    marks = jnp.broadcast_to(
        jnp.where(lane[None, :] < LANES // 2, first_id[:, None], last_id[:, None])[:, None, :],
        (blocks, MARK, LANES),
    )
    send = whiten(source, archive.reshape(CAP, 3 * TILE, LANES), marks)
    got = [
        lax.all_to_all(part, "blk", split_axis=0, concat_axis=0, tiled=True) for part in send
    ]

    table = make_table()
    got[0], table = lax.optimization_barrier((got[0], table))
    found = got[0][:, 2 * len(CHUNKS[0]) * TILE, :].astype(jnp.int32)
    units = jnp.arange(UNITS, dtype=jnp.int32)[:, None]
    place = jnp.sum(
        jnp.where(found[:, 0][None, :] == units, 2 * owners[None, :], 0)
        + jnp.where(found[:, LANES - 1][None, :] == units, 2 * owners[None, :] + 1, 0),
        axis=1,
    )
    place = jnp.clip(place, 0, 2 * blocks - 1)

    planes = 4
    edge = (lax.axis_index("region") % planes == 0).astype(jnp.int32)
    own, one, two, ahead, near, far = [], [], [], [], [], []
    lower, upper, across = [], [], []
    for chunk, part in enumerate(CHUNKS):
        rows = len(part) * TILE
        early = sort_units(place, got[chunk], rows)
        piece = spread(early, planes)
        closer, further = from_previous_region(early, piece, planes)
        block = sort_units(place, got[chunk], rows, piece)
        own.append([block])
        one.append([shifted(block, "blk", 1)])
        two.append([shifted(block, "blk", 2)])
        ahead.append([shifted(block, "blk", -2)])
        near.append([closer])
        far.append(further)
        lower.append(cross(chunk, ((0, 1, 1), (0, 2, 2)), edge, own, one, two))
        later = cross(chunk, ((0, 1, 1), (0, 2, 2)), edge, ahead, one, two)
        upper.append(shifted(later, "blk", 2))
        across.append(cross(chunk, ((0, 1, 2),), edge, own, near, far))

    cycle_series, region_series = lag_series(table, lower + upper + across)
    return jnp.swapaxes(cycle_series, 2, 3), jnp.swapaxes(region_series, 1, 2)


def solution(mesh):
    placed = (P(("region", "blk"), None, None), P(("region", "blk")), P(("region", "blk")))
    return jax.shard_map(
        body,
        mesh=mesh,
        in_specs=placed,
        out_specs=(
            P(("region", "blk"), None, None, None, None),
            P(("region", "blk"), None, None, None),
        ),
        check_vma=False,
    )
```

```python
import functools
import math

import jax
import jax.numpy as jnp
from jax import lax
from jax.experimental import pallas as pl
from jax.experimental.pallas import tpu as pltpu
from jax.sharding import PartitionSpec as P

SB = 2
SEGS = 32
F = 1024
LAGS = 2048
HALF = 24
STEPS = 4
UNITS = 64
CAP = 128
LANES = 128
FH = F // LANES
TILE = 2 * FH
epsilon = 1e-05

CHUNKS = ((0, 1, 2),)
GROUP = 32
MARK = 8
PIECE = 16
VMEM = pl.BlockSpec(memory_space=pltpu.VMEM)
SMEM = pl.BlockSpec(memory_space=pltpu.SMEM)


def pairs_of(chunk):
    before = [c for part in CHUNKS[:chunk] for c in part]
    now = before + list(CHUNKS[chunk])
    return [(c, d) for c in now for d in now if not (c in before and d in before)]


def place_of(component):
    for chunk, part in enumerate(CHUNKS):
        if component in part:
            return chunk, part.index(component)


def whiten_kernel(source_ref, band_ref, inverse_ref, archive_ref, mark_ref, *rest):
    outs, (level_ref,) = rest[:-1], rest[-1:]
    base = pl.program_id(0) * GROUP
    rows = GROUP * FH

    def slab_of(position):
        return archive_ref[source_ref[base + position]].astype(jnp.float32)

    def magnitude(position, carry):
        slab = slab_of(position)
        total = None
        for c in range(3):
            real = slab[c * TILE : c * TILE + FH]
            imag = slab[c * TILE + FH : (c + 1) * TILE]
            size = jnp.sqrt(real * real + imag * imag)
            total = size if total is None else total + size
        level_ref[pl.ds(pl.multiple_of(FH + position * FH, FH), FH), :] = total * (1.0 / 3.0)
        return carry

    lax.fori_loop(0, GROUP, magnitude, 0, unroll=4)
    here = level_ref[FH : FH + rows, :]
    before = level_ref[FH - 1 : FH - 1 + rows, :]
    after = level_ref[FH + 1 : FH + 1 + rows, :]
    lane = lax.broadcasted_iota(jnp.int32, (rows, LANES), 1)
    row = lax.broadcasted_iota(jnp.int32, (rows, LANES), 0) % FH
    edge = jnp.where(
        lane >= LANES // 2,
        jnp.where(row == 0, 0.0, before),
        jnp.where(row == FH - 1, 0.0, after),
    )
    spread = jnp.concatenate([here, edge], axis=1)
    high = spread.astype(jnp.bfloat16)
    low = (spread - high.astype(jnp.float32)).astype(jnp.bfloat16)
    band = band_ref[...]
    window = jnp.dot(high, band, preferred_element_type=jnp.float32) + jnp.dot(
        low, band, preferred_element_type=jnp.float32
    )
    level = window.reshape(GROUP, FH, LANES) * inverse_ref[...][None] + epsilon
    level_ref[FH : FH + rows, :] = (1.0 / level).reshape(rows, LANES)

    def divide(position, carry):
        slab = slab_of(position)
        gain = level_ref[pl.ds(pl.multiple_of(FH + position * FH, FH), FH), :]
        for out, part in zip(outs, CHUNKS):
            pieces = []
            for c in part:
                for half in range(2):
                    start = c * TILE + half * FH
                    pieces.append(slab[start : start + FH] * gain)
            size = len(part) * TILE
            start = pl.multiple_of((position % 2) * size, TILE)
            out[position // 2, pl.ds(start, size), :] = jnp.concatenate(pieces, axis=0).astype(
                jnp.bfloat16
            )
        return carry

    lax.fori_loop(0, GROUP, divide, 0, unroll=4)
    outs[0][:, 2 * len(CHUNKS[0]) * TILE :, :] = mark_ref[...]


def whiten(source, archive, marks):
    low = jnp.arange(LANES, dtype=jnp.int32)
    gap = jnp.abs(low[:, None] - low[None, :])
    band = jnp.concatenate([gap <= HALF, gap >= LANES - HALF], axis=0).astype(jnp.bfloat16)
    bin_index = jnp.arange(F, dtype=jnp.int32)
    bin_count = (
        jnp.minimum(bin_index + HALF, F - 1) - jnp.maximum(bin_index - HALF, 0) + 1
    ).astype(jnp.float32)
    inverse = (1.0 / bin_count).reshape(FH, LANES)
    sizes = [2 * len(part) * TILE for part in CHUNKS]
    sizes[0] += MARK
    return pl.pallas_call(
        whiten_kernel,
        grid=(CAP // GROUP,),
        in_specs=[SMEM, VMEM, VMEM, VMEM]
        + [pl.BlockSpec((GROUP // 2, MARK, LANES), lambda g: (g, 0, 0))],
        out_specs=[
            pl.BlockSpec((GROUP // 2, size, LANES), lambda g: (g, 0, 0)) for size in sizes
        ],
        out_shape=[
            jax.ShapeDtypeStruct((marks.shape[0], size, LANES), jnp.bfloat16) for size in sizes
        ],
        scratch_shapes=[pltpu.VMEM((GROUP * FH + 2 * FH, LANES), jnp.float32)],
        compiler_params=pltpu.CompilerParams(vmem_limit_bytes=16 * 1024 * 1024),
        cost_estimate=pl.CostEstimate(flops=200_000_000, bytes_accessed=4_000_000, transcendentals=0),
        name="whiten",
    )(source, band, inverse, archive, marks)


def sort_kernel(source_ref, got_ref, out_ref):
    rows = out_ref.shape[1]

    def move(unit, carry):
        place = source_ref[unit]
        start = pl.multiple_of((place & 1) * rows, TILE)
        out_ref[unit] = got_ref[place >> 1, pl.ds(start, rows), :]
        return carry

    lax.fori_loop(0, UNITS, move, 0, unroll=8)


def sort_units(source, got, rows):
    return pl.pallas_call(
        sort_kernel,
        in_specs=[SMEM, VMEM],
        out_specs=VMEM,
        out_shape=jax.ShapeDtypeStruct((UNITS, rows, LANES), jnp.bfloat16),
        compiler_params=pltpu.CompilerParams(vmem_limit_bytes=16 * 1024 * 1024),
        cost_estimate=pl.CostEstimate(flops=0, bytes_accessed=3_000_000, transcendentals=0),
        name="sort_units",
    )(source, got)


def choose_kernel(plane_ref, block_ref, *refs):
    pieces, (piece_ref, out_ref) = refs[:-2], refs[-2:]
    last = len(pieces)
    out_ref[...] = block_ref[...]
    for plane, ref in enumerate(pieces):

        @pl.when(plane_ref[0] == plane)
        def _(ref=ref):
            piece_ref[...] = ref[...]

    @pl.when(plane_ref[0] == last)
    def _():
        piece_ref[...] = block_ref[last * PIECE :]


def choose(plane, block, pieces):
    return pl.pallas_call(
        choose_kernel,
        in_specs=[SMEM] + [VMEM] * (1 + len(pieces)),
        out_specs=[VMEM, VMEM],
        out_shape=[
            jax.ShapeDtypeStruct(pieces[0].shape, jnp.bfloat16),
            jax.ShapeDtypeStruct(block.shape, jnp.bfloat16),
        ],
        compiler_params=pltpu.CompilerParams(vmem_limit_bytes=16 * 1024 * 1024),
        cost_estimate=pl.CostEstimate(flops=0, bytes_accessed=2_000_000, transcendentals=0),
        name="choose_piece",
    )(plane.reshape(1), block, *pieces)


def products(left_block, right_block, chunk, store):
    pairs = pairs_of(chunk)

    def load(block, base, m, component):
        which, at = place_of(component)
        pieces = block[which]
        if len(pieces) > 1:
            ref, unit = pieces[base // PIECE], m
        else:
            ref, unit = pieces[0], base + m
        tile = ref[unit, at * TILE : (at + 1) * TILE, :].astype(jnp.float32)
        return tile[:FH], tile[FH:]

    firsts = sorted({c for c, _ in pairs})
    seconds = sorted({d for _, d in pairs})
    for i in range(SB):
        for j in range(SB):
            zero = jnp.zeros((FH, LANES), jnp.float32)
            sums = tuple((zero, zero) for _ in pairs)
            for start in range(0, SEGS, PIECE):

                def step(m, sums, start=start):
                    left = {c: load(left_block, i * SEGS + start, m, c) for c in firsts}
                    right = {d: load(right_block, j * SEGS + start, m, d) for d in seconds}
                    new = []
                    for n, (c, d) in enumerate(pairs):
                        real, imag = sums[n]
                        (ar, ai), (br, bi) = left[c], right[d]
                        new.append((real + ar * br + ai * bi, imag + ai * br - ar * bi))
                    return tuple(new)

                sums = lax.fori_loop(0, PIECE, step, sums, unroll=2)
            for n, (real, imag) in enumerate(sums):
                store(i, j, n, jnp.concatenate([real, imag], axis=0).astype(jnp.bfloat16))


def cross_kernel(chunk, plan, counts, flag_ref, *refs):
    blocks, at = [], 0
    for count in counts:
        block = []
        for _ in range(chunk + 1):
            block.append(refs[at : at + count])
            at += count
        blocks.append(block)
    outs = refs[len(refs) - len(plan) :]
    for out, (left, when_zero, when_one) in zip(outs, plan):

        def store(i, j, n, tile, out=out):
            out[i * SB + j, n] = tile

        if when_zero == when_one:
            products(blocks[left], blocks[when_zero], chunk, store)
        else:
            for value, right in ((0, when_zero), (1, when_one)):

                @pl.when(flag_ref[0] == value)
                def _(right=right, left=left, store=store):
                    products(blocks[left], blocks[right], chunk, store)


def cross(chunk, plan, flag, blocks, after=()):
    count = len(pairs_of(chunk))
    shape = (SB * SB, count, TILE, LANES)
    flat = [piece for block in blocks for part in block[: chunk + 1] for piece in part]
    return pl.pallas_call(
        functools.partial(cross_kernel, chunk, plan, tuple(len(block[0]) for block in blocks)),
        in_specs=[SMEM]
        + [VMEM] * len(flat)
        + [pl.BlockSpec(memory_space=pl.ANY)] * len(after),
        out_specs=[VMEM] * len(plan),
        out_shape=[jax.ShapeDtypeStruct(shape, jnp.bfloat16)] * len(plan),
        compiler_params=pltpu.CompilerParams(vmem_limit_bytes=24 * 1024 * 1024),
        cost_estimate=pl.CostEstimate(
            flops=len(plan) * 40_000_000, bytes_accessed=len(plan) * 1_500_000, transcendentals=0
        ),
        name="cross",
    )(flag.reshape(1), *flat, *after)


COLUMNS = 256
CYCLE_ROWS = SB * STEPS * 9 * SB
ALL_ROWS = CYCLE_ROWS + SB * 9 * SB


def series_kernel(table_ref, *refs):
    chunks = len(CHUNKS)
    sources = refs[: (STEPS + 1) * chunks]
    cycle_ref, region_ref, wide_ref, rows_ref, held_ref, sems = refs[(STEPS + 1) * chunks :]
    step = pl.program_id(0)

    def fetch(n):
        return pltpu.make_async_copy(table_ref.at[n], held_ref.at[n], sems.at[n])

    @pl.when(step == 0)
    def _():
        for n in range(LAGS // COLUMNS):
            fetch(n).start()
        for k in range(STEPS + 1):
            for chunk in range(chunks):
                source = sources[k * chunks + chunk]
                for i in range(SB):
                    for j in range(SB):
                        for n, (c, d) in enumerate(pairs_of(chunk)):
                            if k < STEPS:
                                row = ((i * STEPS + k) * 9 + 3 * c + d) * SB + j
                            else:
                                row = CYCLE_ROWS + (i * 9 + 3 * c + d) * SB + j
                            wide_ref[row * TILE : (row + 1) * TILE, :] = source[
                                i * SB + j, n
                            ].astype(jnp.float32)
        for piece in range(TILE):
            rows_ref[:, piece * LANES : (piece + 1) * LANES] = wide_ref[
                pl.ds(piece, ALL_ROWS, stride=TILE), :
            ].astype(jnp.bfloat16)

    fetch(step).wait()
    series = jnp.dot(rows_ref[...], held_ref[step], preferred_element_type=jnp.float32)
    series = (series * (1.0 / math.sqrt(F * SEGS))).astype(jnp.bfloat16)
    for i in range(SB):
        for k in range(STEPS):
            for n in range(9):
                row = ((i * STEPS + k) * 9 + n) * SB
                cycle_ref[i, k, n] = series[row : row + SB]
        for n in range(9):
            row = CYCLE_ROWS + (i * 9 + n) * SB
            region_ref[i, n] = series[row : row + SB]


def lag_series(table, sources):
    return pl.pallas_call(
        series_kernel,
        grid=(LAGS // COLUMNS,),
        in_specs=[pl.BlockSpec(memory_space=pl.ANY)] + [VMEM] * len(sources),
        out_specs=[
            pl.BlockSpec((SB, STEPS, 9, SB, COLUMNS), lambda n: (0, 0, 0, 0, n)),
            pl.BlockSpec((SB, 9, SB, COLUMNS), lambda n: (0, 0, 0, n)),
        ],
        out_shape=[
            jax.ShapeDtypeStruct((SB, STEPS, 9, SB, LAGS), jnp.bfloat16),
            jax.ShapeDtypeStruct((SB, 9, SB, LAGS), jnp.bfloat16),
        ],
        scratch_shapes=[
            pltpu.VMEM((ALL_ROWS * TILE, LANES), jnp.float32),
            pltpu.VMEM((ALL_ROWS, 2 * F), jnp.bfloat16),
            pltpu.VMEM((LAGS // COLUMNS, 2 * F, COLUMNS), jnp.bfloat16),
            pltpu.SemaphoreType.DMA((LAGS // COLUMNS,)),
        ],
        compiler_params=pltpu.CompilerParams(vmem_limit_bytes=32 * 1024 * 1024),
        cost_estimate=pl.CostEstimate(
            flops=2 * ALL_ROWS * 2 * F * LAGS, bytes_accessed=12_000_000, transcendentals=0
        ),
        name="lag_series",
    )(pltpu.with_memory_space_constraint(table, pltpu.HBM), *sources)


def table_kernel(fine_ref, coarse_ref, out_ref):
    step = pl.program_id(0)
    for high in range(FH):
        cos_high = coarse_ref[0, high : high + 1, :]
        sin_high = coarse_ref[1, high : high + 1, :]
        cos_low, sin_low = fine_ref[0], fine_ref[1]

        @pl.when(step == 0)
        def _(high=high):
            out_ref[0, high * LANES : (high + 1) * LANES, :] = (
                cos_low * cos_high - sin_low * sin_high
            ).astype(jnp.bfloat16)

        @pl.when(step == 1)
        def _(high=high):
            out_ref[0, high * LANES : (high + 1) * LANES, :] = (
                -(sin_low * cos_high + cos_low * sin_high)
            ).astype(jnp.bfloat16)


def make_table():
    lag_index = jnp.arange(LAGS, dtype=jnp.int32) - LAGS // 2

    def angles(bins):
        phase = bins[:, None] * lag_index[None, :] % (2 * F)
        angle = phase.astype(jnp.float32) * (math.pi / F)
        return jnp.stack([jnp.cos(angle), jnp.sin(angle)])

    fine = angles(jnp.arange(LANES, dtype=jnp.int32))
    coarse = angles(LANES * jnp.arange(FH, dtype=jnp.int32))
    return pl.pallas_call(
        table_kernel,
        grid=(2, LAGS // COLUMNS),
        in_specs=[
            pl.BlockSpec((2, LANES, COLUMNS), lambda s, n: (0, 0, n)),
            pl.BlockSpec((2, FH, COLUMNS), lambda s, n: (0, 0, n)),
        ],
        out_specs=pl.BlockSpec((1, F, COLUMNS), lambda s, n: (n, s, 0)),
        out_shape=pltpu.HBM((LAGS // COLUMNS, 2 * F, COLUMNS), jnp.bfloat16),
        compiler_params=pltpu.CompilerParams(vmem_limit_bytes=16 * 1024 * 1024),
        cost_estimate=pl.CostEstimate(flops=16_000_000, bytes_accessed=12_000_000, transcendentals=0),
        name="lag_table",
    )(fine, coarse)


def shifted(block, axis, by):
    size = lax.axis_size(axis)
    return lax.ppermute(block, axis, [(i, (i + by) % size) for i in range(size)])


def swapped(block):
    return lax.ppermute(block, "blk", [(i, i ^ 1) for i in range(lax.axis_size("blk"))])


def spread(block, planes):
    starts = range(0, lax.axis_size("region"), planes)
    return [
        lax.ppermute(
            block[plane * PIECE : (plane + 1) * PIECE],
            "region",
            [(n + planes - 1, n + plane) for n in starts],
        )
        for plane in range(planes - 1)
    ]


def from_previous_region(block, piece, planes):
    regions = lax.axis_size("region")
    near = lax.ppermute(
        block, "region", [(i, i + 1) for i in range(regions) if (i + 1) % planes]
    )
    piece = lax.ppermute(piece, "region", [(i, (i + planes) % regions) for i in range(regions)])
    far = [piece]
    for plane in range(1, planes):
        far.append(
            lax.ppermute(piece, "region", [(n + plane, n) for n in range(0, regions, planes)])
        )
    return near, far


def body(archive, unit_of, row_counts):
    blocks = lax.axis_size("blk")
    slot = jnp.arange(CAP, dtype=jnp.int32)
    ids = jnp.where(slot < row_counts[0], unit_of, -1)
    owners = jnp.arange(blocks, dtype=jnp.int32)
    sent = (ids >> 6)[None, :] == owners[:, None]
    key = slot * UNITS + (ids & (UNITS - 1))
    none = CAP * UNITS
    first = jnp.min(jnp.where(sent, key, none), axis=1)
    last = jnp.max(jnp.where(sent, key, -1), axis=1)
    source = jnp.clip(jnp.stack([first, last], axis=1) >> 6, 0, CAP - 1).reshape(2 * blocks)
    first_id = jnp.where(first < none, first & (UNITS - 1), -1).astype(jnp.bfloat16)
    last_id = jnp.where(last > first, last & (UNITS - 1), -1).astype(jnp.bfloat16)
    lane = jnp.arange(LANES, dtype=jnp.int32)
    marks = jnp.broadcast_to(
        jnp.where(lane[None, :] < LANES // 2, first_id[:, None], last_id[:, None])[:, None, :],
        (blocks, MARK, LANES),
    )
    send = whiten(source, archive.reshape(CAP, 3 * TILE, LANES), marks)
    got = [
        lax.all_to_all(part, "blk", split_axis=0, concat_axis=0, tiled=True) for part in send
    ]

    table = make_table()
    got[0], table = lax.optimization_barrier((got[0], table))
    found = got[0][:, 2 * len(CHUNKS[0]) * TILE, :].astype(jnp.int32)
    units = jnp.arange(UNITS, dtype=jnp.int32)[:, None]
    place = jnp.sum(
        jnp.where(found[:, 0][None, :] == units, 2 * owners[None, :], 0)
        + jnp.where(found[:, LANES - 1][None, :] == units, 2 * owners[None, :] + 1, 0),
        axis=1,
    )
    place = jnp.clip(place, 0, 2 * blocks - 1)

    planes = 4
    plane = lax.axis_index("region") % planes
    edge = (plane == 0).astype(jnp.int32)
    core = lax.axis_index("blk") & 1
    own, twin, two, four, near, far = [], [], [], [], [], []
    results = [[] for _ in range(STEPS + 1)]
    for chunk, part in enumerate(CHUNKS):
        early = sort_units(place, got[chunk], len(part) * TILE)
        piece, block = choose(plane, early, spread(early, planes))
        closer, further = from_previous_region(block, piece, planes)
        own.append([block])
        four.append([shifted(block, "blk", 4)])
        two.append([shifted(block, "blk", 2)])
        twin.append([swapped(block)])
        near.append([closer])
        far.append(further)
        by_two, for_one = cross(chunk, ((0, 2, 2), (1, 0, 2)), core, (own, twin, two))
        (for_three,) = cross(
            chunk, ((0, 1, 2),), core, (twin, two, four), (for_one,)
        )
        (by_four,) = cross(chunk, ((0, 1, 1),), core, (own, four), (for_three,))
        (by_region,) = cross(chunk, ((0, 1, 2),), edge, (own, near, far), (by_four,))
        every = (swapped(for_one), by_two, swapped(for_three), by_four, by_region)
        for k, result in enumerate(every):
            results[k].append(result)

    cycle_series, region_series = lag_series(table, [r for result in results for r in result])
    return jnp.swapaxes(cycle_series, 2, 3), jnp.swapaxes(region_series, 1, 2)


def solution(mesh):
    placed = (P(("region", "blk"), None, None), P(("region", "blk")), P(("region", "blk")))
    return jax.shard_map(
        body,
        mesh=mesh,
        in_specs=placed,
        out_specs=(
            P(("region", "blk"), None, None, None, None),
            P(("region", "blk"), None, None, None),
        ),
        check_vma=False,
    )
```

```python
import functools
import math

import jax
import jax.numpy as jnp
from jax import lax
from jax.experimental import pallas as pl
from jax.experimental.pallas import tpu as pltpu
from jax.sharding import PartitionSpec as P

SB = 2
SEGS = 32
F = 1024
LAGS = 2048
HALF = 24
STEPS = 4
UNITS = 64
CAP = 128
LANES = 128
FH = F // LANES
TILE = 2 * FH
epsilon = 1e-05

CHUNKS = ((0, 1, 2),)
GROUP = 32
MARK = 8
PIECE = 16
VMEM = pl.BlockSpec(memory_space=pltpu.VMEM)
SMEM = pl.BlockSpec(memory_space=pltpu.SMEM)


def pairs_of(chunk):
    before = [c for part in CHUNKS[:chunk] for c in part]
    now = before + list(CHUNKS[chunk])
    return [(c, d) for c in now for d in now if not (c in before and d in before)]


def place_of(component):
    for chunk, part in enumerate(CHUNKS):
        if component in part:
            return chunk, part.index(component)


def whiten_kernel(source_ref, band_ref, inverse_ref, archive_ref, mark_ref, *rest):
    outs, (level_ref,) = rest[:-1], rest[-1:]
    base = pl.program_id(0) * GROUP
    rows = GROUP * FH

    def slab_of(position):
        return archive_ref[source_ref[base + position]].astype(jnp.float32)

    def magnitude(position, carry):
        slab = slab_of(position)
        total = None
        for c in range(3):
            real = slab[c * TILE : c * TILE + FH]
            imag = slab[c * TILE + FH : (c + 1) * TILE]
            size = jnp.sqrt(real * real + imag * imag)
            total = size if total is None else total + size
        level_ref[pl.ds(pl.multiple_of(FH + position * FH, FH), FH), :] = total * (1.0 / 3.0)
        return carry

    lax.fori_loop(0, GROUP, magnitude, 0, unroll=4)
    here = level_ref[FH : FH + rows, :]
    before = level_ref[FH - 1 : FH - 1 + rows, :]
    after = level_ref[FH + 1 : FH + 1 + rows, :]
    lane = lax.broadcasted_iota(jnp.int32, (rows, LANES), 1)
    row = lax.broadcasted_iota(jnp.int32, (rows, LANES), 0) % FH
    edge = jnp.where(
        lane >= LANES // 2,
        jnp.where(row == 0, 0.0, before),
        jnp.where(row == FH - 1, 0.0, after),
    )
    spread = jnp.concatenate([here, edge], axis=1)
    high = spread.astype(jnp.bfloat16)
    low = (spread - high.astype(jnp.float32)).astype(jnp.bfloat16)
    band = band_ref[...]
    window = jnp.dot(high, band, preferred_element_type=jnp.float32) + jnp.dot(
        low, band, preferred_element_type=jnp.float32
    )
    level = window.reshape(GROUP, FH, LANES) * inverse_ref[...][None] + epsilon
    level_ref[FH : FH + rows, :] = (1.0 / level).reshape(rows, LANES)

    def divide(position, carry):
        slab = slab_of(position)
        gain = level_ref[pl.ds(pl.multiple_of(FH + position * FH, FH), FH), :]
        for out, part in zip(outs, CHUNKS):
            pieces = []
            for c in part:
                for half in range(2):
                    start = c * TILE + half * FH
                    pieces.append(slab[start : start + FH] * gain)
            size = len(part) * TILE
            start = pl.multiple_of((position % 2) * size, TILE)
            out[position // 2, pl.ds(start, size), :] = jnp.concatenate(pieces, axis=0).astype(
                jnp.bfloat16
            )
        return carry

    lax.fori_loop(0, GROUP, divide, 0, unroll=4)
    outs[0][:, 2 * len(CHUNKS[0]) * TILE :, :] = mark_ref[...]


def whiten(source, archive, marks):
    low = jnp.arange(LANES, dtype=jnp.int32)
    gap = jnp.abs(low[:, None] - low[None, :])
    band = jnp.concatenate([gap <= HALF, gap >= LANES - HALF], axis=0).astype(jnp.bfloat16)
    bin_index = jnp.arange(F, dtype=jnp.int32)
    bin_count = (
        jnp.minimum(bin_index + HALF, F - 1) - jnp.maximum(bin_index - HALF, 0) + 1
    ).astype(jnp.float32)
    inverse = (1.0 / bin_count).reshape(FH, LANES)
    sizes = [2 * len(part) * TILE for part in CHUNKS]
    sizes[0] += MARK
    return pl.pallas_call(
        whiten_kernel,
        grid=(CAP // GROUP,),
        in_specs=[SMEM, VMEM, VMEM, VMEM]
        + [pl.BlockSpec((GROUP // 2, MARK, LANES), lambda g: (g, 0, 0))],
        out_specs=[
            pl.BlockSpec((GROUP // 2, size, LANES), lambda g: (g, 0, 0)) for size in sizes
        ],
        out_shape=[
            jax.ShapeDtypeStruct((marks.shape[0], size, LANES), jnp.bfloat16) for size in sizes
        ],
        scratch_shapes=[pltpu.VMEM((GROUP * FH + 2 * FH, LANES), jnp.float32)],
        compiler_params=pltpu.CompilerParams(vmem_limit_bytes=16 * 1024 * 1024),
        cost_estimate=pl.CostEstimate(flops=200_000_000, bytes_accessed=4_000_000, transcendentals=0),
        name="whiten",
    )(source, band, inverse, archive, marks)


def sort_kernel(source_ref, got_ref, out_ref):
    rows = out_ref.shape[1]

    def move(unit, carry):
        place = source_ref[unit]
        start = pl.multiple_of((place & 1) * rows, TILE)
        out_ref[unit] = got_ref[place >> 1, pl.ds(start, rows), :]
        return carry

    lax.fori_loop(0, UNITS, move, 0, unroll=8)


def sort_units(source, got, rows):
    return pl.pallas_call(
        sort_kernel,
        in_specs=[SMEM, VMEM],
        out_specs=VMEM,
        out_shape=jax.ShapeDtypeStruct((UNITS, rows, LANES), jnp.bfloat16),
        compiler_params=pltpu.CompilerParams(vmem_limit_bytes=16 * 1024 * 1024),
        cost_estimate=pl.CostEstimate(flops=0, bytes_accessed=3_000_000, transcendentals=0),
        name="sort_units",
    )(source, got)


def choose_kernel(plane_ref, block_ref, *refs):
    pieces, (piece_ref, out_ref) = refs[:-2], refs[-2:]
    last = len(pieces)
    out_ref[...] = block_ref[...]
    for plane, ref in enumerate(pieces):

        @pl.when(plane_ref[0] == plane)
        def _(ref=ref):
            piece_ref[...] = ref[...]

    @pl.when(plane_ref[0] == last)
    def _():
        piece_ref[...] = block_ref[last * PIECE :]


def choose(plane, block, pieces):
    return pl.pallas_call(
        choose_kernel,
        in_specs=[SMEM] + [VMEM] * (1 + len(pieces)),
        out_specs=[VMEM, VMEM],
        out_shape=[
            jax.ShapeDtypeStruct(pieces[0].shape, jnp.bfloat16),
            jax.ShapeDtypeStruct(block.shape, jnp.bfloat16),
        ],
        compiler_params=pltpu.CompilerParams(vmem_limit_bytes=16 * 1024 * 1024),
        cost_estimate=pl.CostEstimate(flops=0, bytes_accessed=2_000_000, transcendentals=0),
        name="choose_piece",
    )(plane.reshape(1), block, *pieces)


def relay_kernel(piece_ref, *refs):
    refs[-1][...] = piece_ref[...]


def relay(piece, *after):
    return pl.pallas_call(
        relay_kernel,
        in_specs=[VMEM] + [pl.BlockSpec(memory_space=pl.ANY)] * len(after),
        out_specs=VMEM,
        out_shape=jax.ShapeDtypeStruct(piece.shape, jnp.bfloat16),
        compiler_params=pltpu.CompilerParams(vmem_limit_bytes=8 * 1024 * 1024),
        cost_estimate=pl.CostEstimate(flops=20_000_000_000, bytes_accessed=400_000, transcendentals=0),
        name="relay_piece",
    )(piece, *after)


def products(left_block, right_block, chunk, store):
    pairs = pairs_of(chunk)

    def load(block, base, m, component):
        which, at = place_of(component)
        pieces = block[which]
        if len(pieces) > 1:
            ref, unit = pieces[base // PIECE], m
        else:
            ref, unit = pieces[0], base + m
        tile = ref[unit, at * TILE : (at + 1) * TILE, :].astype(jnp.float32)
        return tile[:FH], tile[FH:]

    firsts = sorted({c for c, _ in pairs})
    seconds = sorted({d for _, d in pairs})
    for i in range(SB):
        for j in range(SB):
            zero = jnp.zeros((FH, LANES), jnp.float32)
            sums = tuple((zero, zero) for _ in pairs)
            for start in range(0, SEGS, PIECE):

                def step(m, sums, start=start):
                    left = {c: load(left_block, i * SEGS + start, m, c) for c in firsts}
                    right = {d: load(right_block, j * SEGS + start, m, d) for d in seconds}
                    new = []
                    for n, (c, d) in enumerate(pairs):
                        real, imag = sums[n]
                        (ar, ai), (br, bi) = left[c], right[d]
                        new.append((real + ar * br + ai * bi, imag + ai * br - ar * bi))
                    return tuple(new)

                sums = lax.fori_loop(0, PIECE, step, sums, unroll=2)
            for n, (real, imag) in enumerate(sums):
                store(i, j, n, jnp.concatenate([real, imag], axis=0).astype(jnp.bfloat16))


def cross_kernel(chunk, plan, counts, flag_ref, *refs):
    blocks, at = [], 0
    for count in counts:
        block = []
        for _ in range(chunk + 1):
            block.append(refs[at : at + count])
            at += count
        blocks.append(block)
    outs = refs[len(refs) - len(plan) :]
    for out, (left, when_zero, when_one) in zip(outs, plan):

        def store(i, j, n, tile, out=out):
            out[i * SB + j, n] = tile

        if when_zero == when_one:
            products(blocks[left], blocks[when_zero], chunk, store)
        else:
            for value, right in ((0, when_zero), (1, when_one)):

                @pl.when(flag_ref[0] == value)
                def _(right=right, left=left, store=store):
                    products(blocks[left], blocks[right], chunk, store)


def cross(chunk, plan, flag, blocks, after=()):
    count = len(pairs_of(chunk))
    shape = (SB * SB, count, TILE, LANES)
    flat = [piece for block in blocks for part in block[: chunk + 1] for piece in part]
    return pl.pallas_call(
        functools.partial(cross_kernel, chunk, plan, tuple(len(block[0]) for block in blocks)),
        in_specs=[SMEM]
        + [VMEM] * len(flat)
        + [pl.BlockSpec(memory_space=pl.ANY)] * len(after),
        out_specs=[VMEM] * len(plan),
        out_shape=[jax.ShapeDtypeStruct(shape, jnp.bfloat16)] * len(plan),
        compiler_params=pltpu.CompilerParams(vmem_limit_bytes=24 * 1024 * 1024),
        cost_estimate=pl.CostEstimate(
            flops=len(plan) * 40_000_000, bytes_accessed=len(plan) * 1_500_000, transcendentals=0
        ),
        name="cross",
    )(flag.reshape(1), *flat, *after)


COLUMNS = 256
CYCLE_ROWS = SB * STEPS * 9 * SB
ALL_ROWS = CYCLE_ROWS + SB * 9 * SB


def series_kernel(table_ref, *refs):
    chunks = len(CHUNKS)
    sources = refs[: (STEPS + 1) * chunks]
    cycle_ref, region_ref, wide_ref, rows_ref, held_ref, sems = refs[(STEPS + 1) * chunks :]
    step = pl.program_id(0)

    def fetch(n):
        return pltpu.make_async_copy(table_ref.at[n], held_ref.at[n], sems.at[n])

    @pl.when(step == 0)
    def _():
        for n in range(LAGS // COLUMNS):
            fetch(n).start()
        for k in range(STEPS + 1):
            for chunk in range(chunks):
                source = sources[k * chunks + chunk]
                for i in range(SB):
                    for j in range(SB):
                        for n, (c, d) in enumerate(pairs_of(chunk)):
                            if k < STEPS:
                                row = ((i * STEPS + k) * 9 + 3 * c + d) * SB + j
                            else:
                                row = CYCLE_ROWS + (i * 9 + 3 * c + d) * SB + j
                            wide_ref[row * TILE : (row + 1) * TILE, :] = source[
                                i * SB + j, n
                            ].astype(jnp.float32)
        for piece in range(TILE):
            rows_ref[:, piece * LANES : (piece + 1) * LANES] = wide_ref[
                pl.ds(piece, ALL_ROWS, stride=TILE), :
            ].astype(jnp.bfloat16)

    fetch(step).wait()
    series = jnp.dot(rows_ref[...], held_ref[step], preferred_element_type=jnp.float32)
    series = (series * (1.0 / math.sqrt(F * SEGS))).astype(jnp.bfloat16)
    for i in range(SB):
        for k in range(STEPS):
            for n in range(9):
                row = ((i * STEPS + k) * 9 + n) * SB
                cycle_ref[i, k, n] = series[row : row + SB]
        for n in range(9):
            row = CYCLE_ROWS + (i * 9 + n) * SB
            region_ref[i, n] = series[row : row + SB]


def lag_series(table, sources):
    return pl.pallas_call(
        series_kernel,
        grid=(LAGS // COLUMNS,),
        in_specs=[pl.BlockSpec(memory_space=pl.ANY)] + [VMEM] * len(sources),
        out_specs=[
            pl.BlockSpec((SB, STEPS, 9, SB, COLUMNS), lambda n: (0, 0, 0, 0, n)),
            pl.BlockSpec((SB, 9, SB, COLUMNS), lambda n: (0, 0, 0, n)),
        ],
        out_shape=[
            jax.ShapeDtypeStruct((SB, STEPS, 9, SB, LAGS), jnp.bfloat16),
            jax.ShapeDtypeStruct((SB, 9, SB, LAGS), jnp.bfloat16),
        ],
        scratch_shapes=[
            pltpu.VMEM((ALL_ROWS * TILE, LANES), jnp.float32),
            pltpu.VMEM((ALL_ROWS, 2 * F), jnp.bfloat16),
            pltpu.VMEM((LAGS // COLUMNS, 2 * F, COLUMNS), jnp.bfloat16),
            pltpu.SemaphoreType.DMA((LAGS // COLUMNS,)),
        ],
        compiler_params=pltpu.CompilerParams(vmem_limit_bytes=32 * 1024 * 1024),
        cost_estimate=pl.CostEstimate(
            flops=2 * ALL_ROWS * 2 * F * LAGS, bytes_accessed=12_000_000, transcendentals=0
        ),
        name="lag_series",
    )(pltpu.with_memory_space_constraint(table, pltpu.HBM), *sources)


def table_kernel(fine_ref, coarse_ref, out_ref):
    step = pl.program_id(0)
    for high in range(FH):
        cos_high = coarse_ref[0, high : high + 1, :]
        sin_high = coarse_ref[1, high : high + 1, :]
        cos_low, sin_low = fine_ref[0], fine_ref[1]

        @pl.when(step == 0)
        def _(high=high):
            out_ref[0, high * LANES : (high + 1) * LANES, :] = (
                cos_low * cos_high - sin_low * sin_high
            ).astype(jnp.bfloat16)

        @pl.when(step == 1)
        def _(high=high):
            out_ref[0, high * LANES : (high + 1) * LANES, :] = (
                -(sin_low * cos_high + cos_low * sin_high)
            ).astype(jnp.bfloat16)


def make_table():
    lag_index = jnp.arange(LAGS, dtype=jnp.int32) - LAGS // 2

    def angles(bins):
        phase = bins[:, None] * lag_index[None, :] % (2 * F)
        angle = phase.astype(jnp.float32) * (math.pi / F)
        return jnp.stack([jnp.cos(angle), jnp.sin(angle)])

    fine = angles(jnp.arange(LANES, dtype=jnp.int32))
    coarse = angles(LANES * jnp.arange(FH, dtype=jnp.int32))
    return pl.pallas_call(
        table_kernel,
        grid=(2, LAGS // COLUMNS),
        in_specs=[
            pl.BlockSpec((2, LANES, COLUMNS), lambda s, n: (0, 0, n)),
            pl.BlockSpec((2, FH, COLUMNS), lambda s, n: (0, 0, n)),
        ],
        out_specs=pl.BlockSpec((1, F, COLUMNS), lambda s, n: (n, s, 0)),
        out_shape=pltpu.HBM((LAGS // COLUMNS, 2 * F, COLUMNS), jnp.bfloat16),
        compiler_params=pltpu.CompilerParams(vmem_limit_bytes=16 * 1024 * 1024),
        cost_estimate=pl.CostEstimate(flops=16_000_000, bytes_accessed=12_000_000, transcendentals=0),
        name="lag_table",
    )(fine, coarse)


def shifted(block, axis, by):
    size = lax.axis_size(axis)
    return lax.ppermute(block, axis, [(i, (i + by) % size) for i in range(size)])


def swapped(block):
    return lax.ppermute(block, "blk", [(i, i ^ 1) for i in range(lax.axis_size("blk"))])


def spread(block, planes):
    starts = range(0, lax.axis_size("region"), planes)
    return [
        lax.ppermute(
            block[plane * PIECE : (plane + 1) * PIECE],
            "region",
            [(n + planes - 1, n + plane) for n in starts],
        )
        for plane in range(planes - 1)
    ]


def from_previous_region(block, piece, planes, *after):
    regions = lax.axis_size("region")
    near = lax.ppermute(
        block, "region", [(i, i + 1) for i in range(regions) if (i + 1) % planes]
    )
    piece = lax.ppermute(piece, "region", [(i, (i + planes) % regions) for i in range(regions)])
    far = [piece]
    piece = relay(piece, near, *after)
    for plane in range(1, planes):
        far.append(
            lax.ppermute(piece, "region", [(n + plane, n) for n in range(0, regions, planes)])
        )
    return near, far


def body(archive, unit_of, row_counts):
    blocks = lax.axis_size("blk")
    slot = jnp.arange(CAP, dtype=jnp.int32)
    ids = jnp.where(slot < row_counts[0], unit_of, -1)
    owners = jnp.arange(blocks, dtype=jnp.int32)
    sent = (ids >> 6)[None, :] == owners[:, None]
    key = slot * UNITS + (ids & (UNITS - 1))
    none = CAP * UNITS
    first = jnp.min(jnp.where(sent, key, none), axis=1)
    last = jnp.max(jnp.where(sent, key, -1), axis=1)
    source = jnp.clip(jnp.stack([first, last], axis=1) >> 6, 0, CAP - 1).reshape(2 * blocks)
    first_id = jnp.where(first < none, first & (UNITS - 1), -1).astype(jnp.bfloat16)
    last_id = jnp.where(last > first, last & (UNITS - 1), -1).astype(jnp.bfloat16)
    lane = jnp.arange(LANES, dtype=jnp.int32)
    marks = jnp.broadcast_to(
        jnp.where(lane[None, :] < LANES // 2, first_id[:, None], last_id[:, None])[:, None, :],
        (blocks, MARK, LANES),
    )
    send = whiten(source, archive.reshape(CAP, 3 * TILE, LANES), marks)
    got = [
        lax.all_to_all(part, "blk", split_axis=0, concat_axis=0, tiled=True) for part in send
    ]

    table = make_table()
    got[0], table = lax.optimization_barrier((got[0], table))
    found = got[0][:, 2 * len(CHUNKS[0]) * TILE, :].astype(jnp.int32)
    units = jnp.arange(UNITS, dtype=jnp.int32)[:, None]
    place = jnp.sum(
        jnp.where(found[:, 0][None, :] == units, 2 * owners[None, :], 0)
        + jnp.where(found[:, LANES - 1][None, :] == units, 2 * owners[None, :] + 1, 0),
        axis=1,
    )
    place = jnp.clip(place, 0, 2 * blocks - 1)

    planes = 4
    plane = lax.axis_index("region") % planes
    edge = (plane == 0).astype(jnp.int32)
    core = lax.axis_index("blk") & 1
    own, twin, two, four, near, far = [], [], [], [], [], []
    results = [[] for _ in range(STEPS + 1)]
    for chunk, part in enumerate(CHUNKS):
        early = sort_units(place, got[chunk], len(part) * TILE)
        piece, block = choose(plane, early, spread(early, planes))
        twin.append([swapped(block)])
        closer, further = from_previous_region(block, piece, planes, twin[chunk][0])
        own.append([block])
        four.append([shifted(block, "blk", 4)])
        two.append([shifted(block, "blk", 2)])
        near.append([closer])
        far.append(further)
        (by_region,) = cross(chunk, ((0, 1, 2),), edge, (own, near, far))
        by_two, for_one = cross(
            chunk, ((0, 2, 2), (1, 0, 2)), core, (own, twin, two), (by_region,)
        )
        (for_three,) = cross(chunk, ((0, 1, 2),), core, (twin, two, four), (for_one,))
        (by_four,) = cross(chunk, ((0, 1, 1),), core, (own, four), (for_three,))
        every = (swapped(for_one), by_two, swapped(for_three), by_four, by_region)
        for k, result in enumerate(every):
            results[k].append(result)

    cycle_series, region_series = lag_series(table, [r for result in results for r in result])
    return jnp.swapaxes(cycle_series, 2, 3), jnp.swapaxes(region_series, 1, 2)


def solution(mesh):
    placed = (P(("region", "blk"), None, None), P(("region", "blk")), P(("region", "blk")))
    return jax.shard_map(
        body,
        mesh=mesh,
        in_specs=placed,
        out_specs=(
            P(("region", "blk"), None, None, None, None),
            P(("region", "blk"), None, None, None),
        ),
        check_vma=False,
    )
```

```python
import functools
import math

import jax
import jax.numpy as jnp
from jax import lax
from jax.experimental import pallas as pl
from jax.experimental.pallas import tpu as pltpu
from jax.sharding import PartitionSpec as P

SB = 2
SEGS = 32
F = 1024
LAGS = 2048
HALF = 24
STEPS = 4
UNITS = 64
CAP = 128
LANES = 128
FH = F // LANES
TILE = 2 * FH
epsilon = 1e-05

CHUNKS = ((0, 1, 2),)
GROUP = 32
MARK = 8
PIECE = 16
VMEM = pl.BlockSpec(memory_space=pltpu.VMEM)
SMEM = pl.BlockSpec(memory_space=pltpu.SMEM)


def pairs_of(chunk):
    before = [c for part in CHUNKS[:chunk] for c in part]
    now = before + list(CHUNKS[chunk])
    return [(c, d) for c in now for d in now if not (c in before and d in before)]


def place_of(component):
    for chunk, part in enumerate(CHUNKS):
        if component in part:
            return chunk, part.index(component)


def whiten_kernel(source_ref, band_ref, inverse_ref, archive_ref, mark_ref, *rest):
    outs, (level_ref,) = rest[:-1], rest[-1:]
    base = pl.program_id(0) * GROUP
    rows = GROUP * FH

    def slab_of(position):
        return archive_ref[source_ref[base + position]].astype(jnp.float32)

    def magnitude(position, carry):
        slab = slab_of(position)
        total = None
        for c in range(3):
            real = slab[c * TILE : c * TILE + FH]
            imag = slab[c * TILE + FH : (c + 1) * TILE]
            size = jnp.sqrt(real * real + imag * imag)
            total = size if total is None else total + size
        level_ref[pl.ds(pl.multiple_of(FH + position * FH, FH), FH), :] = total * (1.0 / 3.0)
        return carry

    lax.fori_loop(0, GROUP, magnitude, 0, unroll=4)
    here = level_ref[FH : FH + rows, :]
    before = level_ref[FH - 1 : FH - 1 + rows, :]
    after = level_ref[FH + 1 : FH + 1 + rows, :]
    lane = lax.broadcasted_iota(jnp.int32, (rows, LANES), 1)
    row = lax.broadcasted_iota(jnp.int32, (rows, LANES), 0) % FH
    edge = jnp.where(
        lane >= LANES // 2,
        jnp.where(row == 0, 0.0, before),
        jnp.where(row == FH - 1, 0.0, after),
    )
    spread = jnp.concatenate([here, edge], axis=1)
    high = spread.astype(jnp.bfloat16)
    low = (spread - high.astype(jnp.float32)).astype(jnp.bfloat16)
    band = band_ref[...]
    window = jnp.dot(high, band, preferred_element_type=jnp.float32) + jnp.dot(
        low, band, preferred_element_type=jnp.float32
    )
    level = window.reshape(GROUP, FH, LANES) * inverse_ref[...][None] + epsilon
    level_ref[FH : FH + rows, :] = (1.0 / level).reshape(rows, LANES)

    def divide(position, carry):
        slab = slab_of(position)
        gain = level_ref[pl.ds(pl.multiple_of(FH + position * FH, FH), FH), :]
        for out, part in zip(outs, CHUNKS):
            pieces = []
            for c in part:
                for half in range(2):
                    start = c * TILE + half * FH
                    pieces.append(slab[start : start + FH] * gain)
            size = len(part) * TILE
            start = pl.multiple_of((position % 2) * size, TILE)
            out[position // 2, pl.ds(start, size), :] = jnp.concatenate(pieces, axis=0).astype(
                jnp.bfloat16
            )
        return carry

    lax.fori_loop(0, GROUP, divide, 0, unroll=4)
    outs[0][:, 2 * len(CHUNKS[0]) * TILE :, :] = mark_ref[...]


def whiten(source, archive, marks):
    low = jnp.arange(LANES, dtype=jnp.int32)
    gap = jnp.abs(low[:, None] - low[None, :])
    band = jnp.concatenate([gap <= HALF, gap >= LANES - HALF], axis=0).astype(jnp.bfloat16)
    bin_index = jnp.arange(F, dtype=jnp.int32)
    bin_count = (
        jnp.minimum(bin_index + HALF, F - 1) - jnp.maximum(bin_index - HALF, 0) + 1
    ).astype(jnp.float32)
    inverse = (1.0 / bin_count).reshape(FH, LANES)
    sizes = [2 * len(part) * TILE for part in CHUNKS]
    sizes[0] += MARK
    return pl.pallas_call(
        whiten_kernel,
        grid=(CAP // GROUP,),
        in_specs=[SMEM, VMEM, VMEM, VMEM]
        + [pl.BlockSpec((GROUP // 2, MARK, LANES), lambda g: (g, 0, 0))],
        out_specs=[
            pl.BlockSpec((GROUP // 2, size, LANES), lambda g: (g, 0, 0)) for size in sizes
        ],
        out_shape=[
            jax.ShapeDtypeStruct((marks.shape[0], size, LANES), jnp.bfloat16) for size in sizes
        ],
        scratch_shapes=[pltpu.VMEM((GROUP * FH + 2 * FH, LANES), jnp.float32)],
        compiler_params=pltpu.CompilerParams(vmem_limit_bytes=16 * 1024 * 1024),
        cost_estimate=pl.CostEstimate(flops=200_000_000, bytes_accessed=4_000_000, transcendentals=0),
        name="whiten",
    )(source, band, inverse, archive, marks)


def sort_kernel(source_ref, got_ref, out_ref):
    rows = out_ref.shape[1]

    def move(unit, carry):
        place = source_ref[unit]
        start = pl.multiple_of((place & 1) * rows, TILE)
        out_ref[unit] = got_ref[place >> 1, pl.ds(start, rows), :]
        return carry

    lax.fori_loop(0, UNITS, move, 0, unroll=8)


def sort_units(source, got, rows):
    return pl.pallas_call(
        sort_kernel,
        in_specs=[SMEM, VMEM],
        out_specs=VMEM,
        out_shape=jax.ShapeDtypeStruct((UNITS, rows, LANES), jnp.bfloat16),
        compiler_params=pltpu.CompilerParams(vmem_limit_bytes=16 * 1024 * 1024),
        cost_estimate=pl.CostEstimate(flops=0, bytes_accessed=3_000_000, transcendentals=0),
        name="sort_units",
    )(source, got)


def choose_kernel(plane_ref, block_ref, *refs):
    pieces, (piece_ref, out_ref) = refs[:-2], refs[-2:]
    last = len(pieces)
    out_ref[...] = block_ref[...]
    for plane, ref in enumerate(pieces):

        @pl.when(plane_ref[0] == plane)
        def _(ref=ref):
            piece_ref[...] = ref[...]

    @pl.when(plane_ref[0] == last)
    def _():
        piece_ref[...] = block_ref[last * PIECE :]


def choose(plane, block, pieces):
    return pl.pallas_call(
        choose_kernel,
        in_specs=[SMEM] + [VMEM] * (1 + len(pieces)),
        out_specs=[VMEM, VMEM],
        out_shape=[
            jax.ShapeDtypeStruct(pieces[0].shape, jnp.bfloat16),
            jax.ShapeDtypeStruct(block.shape, jnp.bfloat16),
        ],
        compiler_params=pltpu.CompilerParams(vmem_limit_bytes=16 * 1024 * 1024),
        cost_estimate=pl.CostEstimate(flops=0, bytes_accessed=2_000_000, transcendentals=0),
        name="choose_piece",
    )(plane.reshape(1), block, *pieces)


def relay_kernel(piece_ref, *refs):
    refs[-1][...] = piece_ref[...]


def relay(piece, *after):
    return pl.pallas_call(
        relay_kernel,
        in_specs=[VMEM] + [pl.BlockSpec(memory_space=pl.ANY)] * len(after),
        out_specs=VMEM,
        out_shape=jax.ShapeDtypeStruct(piece.shape, jnp.bfloat16),
        compiler_params=pltpu.CompilerParams(vmem_limit_bytes=8 * 1024 * 1024),
        cost_estimate=pl.CostEstimate(flops=20_000_000_000, bytes_accessed=400_000, transcendentals=0),
        name="relay_piece",
    )(piece, *after)


def products(left_block, right_block, chunk, store):
    pairs = pairs_of(chunk)

    def load(block, base, m, component):
        which, at = place_of(component)
        pieces = block[which]
        if len(pieces) > 1:
            ref, unit = pieces[base // PIECE], m
        else:
            ref, unit = pieces[0], base + m
        tile = ref[unit, at * TILE : (at + 1) * TILE, :].astype(jnp.float32)
        return tile[:FH], tile[FH:]

    firsts = sorted({c for c, _ in pairs})
    seconds = sorted({d for _, d in pairs})
    for i in range(SB):
        for j in range(SB):
            zero = jnp.zeros((FH, LANES), jnp.float32)
            sums = tuple((zero, zero) for _ in pairs)
            for start in range(0, SEGS, PIECE):

                def step(m, sums, start=start):
                    left = {c: load(left_block, i * SEGS + start, m, c) for c in firsts}
                    right = {d: load(right_block, j * SEGS + start, m, d) for d in seconds}
                    new = []
                    for n, (c, d) in enumerate(pairs):
                        real, imag = sums[n]
                        (ar, ai), (br, bi) = left[c], right[d]
                        new.append((real + ar * br + ai * bi, imag + ai * br - ar * bi))
                    return tuple(new)

                sums = lax.fori_loop(0, PIECE, step, sums, unroll=2)
            for n, (real, imag) in enumerate(sums):
                store(i, j, n, jnp.concatenate([real, imag], axis=0).astype(jnp.bfloat16))


def cross_kernel(chunk, plan, counts, carried, flag_ref, *refs):
    blocks, at = [], 0
    for count in counts:
        block = []
        for _ in range(chunk + 1):
            block.append(refs[at : at + count])
            at += count
        blocks.append(block)
    out = refs[-1]
    size = SB * SB
    for slot in range(carried):
        out[slot * size : (slot + 1) * size] = refs[at + slot][...]
    for slot, (when_zero, when_one) in enumerate(plan, carried):

        def store(i, j, n, tile, slot=slot):
            out[slot * size + i * SB + j, n] = tile

        if when_zero == when_one:
            products(blocks[when_zero[0]], blocks[when_zero[1]], chunk, store)
        else:
            for value, (left, right) in ((0, when_zero), (1, when_one)):

                @pl.when(flag_ref[0] == value)
                def _(right=right, left=left, store=store):
                    products(blocks[left], blocks[right], chunk, store)


def cross(chunk, plan, flag, blocks, carried=(), after=()):
    count = len(pairs_of(chunk))
    shape = ((len(carried) + len(plan)) * SB * SB, count, TILE, LANES)
    flat = [piece for block in blocks for part in block[: chunk + 1] for piece in part]
    flat += carried
    return pl.pallas_call(
        functools.partial(
            cross_kernel, chunk, plan, tuple(len(block[0]) for block in blocks), len(carried)
        ),
        in_specs=[SMEM]
        + [VMEM] * len(flat)
        + [pl.BlockSpec(memory_space=pl.ANY)] * len(after),
        out_specs=VMEM,
        out_shape=jax.ShapeDtypeStruct(shape, jnp.bfloat16),
        compiler_params=pltpu.CompilerParams(vmem_limit_bytes=24 * 1024 * 1024),
        cost_estimate=pl.CostEstimate(
            flops=len(plan) * 40_000_000, bytes_accessed=len(plan) * 1_500_000, transcendentals=0
        ),
        name="cross",
    )(flag.reshape(1), *flat, *after)


COLUMNS = 256
CYCLE_ROWS = SB * STEPS * 9 * SB
ALL_ROWS = CYCLE_ROWS + SB * 9 * SB


def series_kernel(core_ref, table_ref, one_ref, two_ref, kept_ref, got_ref, across_ref, *refs):
    cycle_ref, region_ref, wide_ref, rows_ref, held_ref, sems = refs
    step = pl.program_id(0)
    size = SB * SB

    def fetch(n):
        return pltpu.make_async_copy(table_ref.at[n], held_ref.at[n], sems.at[n])

    def place(k, source, first):
        for i in range(SB):
            for j in range(SB):
                for n, (c, d) in enumerate(pairs_of(0)):
                    if k < STEPS:
                        row = ((i * STEPS + k) * 9 + 3 * c + d) * SB + j
                    else:
                        row = CYCLE_ROWS + (i * 9 + 3 * c + d) * SB + j
                    wide_ref[row * TILE : (row + 1) * TILE, :] = source[
                        first + i * SB + j, n
                    ].astype(jnp.float32)

    @pl.when(step == 0)
    def _():
        for n in range(LAGS // COLUMNS):
            fetch(n).start()
        place(0, one_ref, 0)
        place(1, two_ref, 0)
        place(3, got_ref, 0)
        place(4, across_ref, 0)

        @pl.when(core_ref[0] == 0)
        def _():
            place(2, got_ref, size)

        @pl.when(core_ref[0] == 1)
        def _():
            place(2, kept_ref, size)

        for piece in range(TILE):
            rows_ref[:, piece * LANES : (piece + 1) * LANES] = wide_ref[
                pl.ds(piece, ALL_ROWS, stride=TILE), :
            ].astype(jnp.bfloat16)

    fetch(step).wait()
    series = jnp.dot(rows_ref[...], held_ref[step], preferred_element_type=jnp.float32)
    series = (series * (1.0 / math.sqrt(F * SEGS))).astype(jnp.bfloat16)
    for i in range(SB):
        for k in range(STEPS):
            for n in range(9):
                row = ((i * STEPS + k) * 9 + n) * SB
                cycle_ref[i, k, n] = series[row : row + SB]
        for n in range(9):
            row = CYCLE_ROWS + (i * 9 + n) * SB
            region_ref[i, n] = series[row : row + SB]


def lag_series(core, table, *sources):
    return pl.pallas_call(
        series_kernel,
        grid=(LAGS // COLUMNS,),
        in_specs=[SMEM, pl.BlockSpec(memory_space=pl.ANY)] + [VMEM] * len(sources),
        out_specs=[
            pl.BlockSpec((SB, STEPS, 9, SB, COLUMNS), lambda n: (0, 0, 0, 0, n)),
            pl.BlockSpec((SB, 9, SB, COLUMNS), lambda n: (0, 0, 0, n)),
        ],
        out_shape=[
            jax.ShapeDtypeStruct((SB, STEPS, 9, SB, LAGS), jnp.bfloat16),
            jax.ShapeDtypeStruct((SB, 9, SB, LAGS), jnp.bfloat16),
        ],
        scratch_shapes=[
            pltpu.VMEM((ALL_ROWS * TILE, LANES), jnp.float32),
            pltpu.VMEM((ALL_ROWS, 2 * F), jnp.bfloat16),
            pltpu.VMEM((LAGS // COLUMNS, 2 * F, COLUMNS), jnp.bfloat16),
            pltpu.SemaphoreType.DMA((LAGS // COLUMNS,)),
        ],
        compiler_params=pltpu.CompilerParams(vmem_limit_bytes=32 * 1024 * 1024),
        cost_estimate=pl.CostEstimate(
            flops=2 * ALL_ROWS * 2 * F * LAGS, bytes_accessed=12_000_000, transcendentals=0
        ),
        name="lag_series",
    )(core.reshape(1), pltpu.with_memory_space_constraint(table, pltpu.HBM), *sources)


def table_kernel(fine_ref, coarse_ref, out_ref):
    step = pl.program_id(0)
    for high in range(FH):
        cos_high = coarse_ref[0, high : high + 1, :]
        sin_high = coarse_ref[1, high : high + 1, :]
        cos_low, sin_low = fine_ref[0], fine_ref[1]

        @pl.when(step == 0)
        def _(high=high):
            out_ref[0, high * LANES : (high + 1) * LANES, :] = (
                cos_low * cos_high - sin_low * sin_high
            ).astype(jnp.bfloat16)

        @pl.when(step == 1)
        def _(high=high):
            out_ref[0, high * LANES : (high + 1) * LANES, :] = (
                -(sin_low * cos_high + cos_low * sin_high)
            ).astype(jnp.bfloat16)


def make_table():
    lag_index = jnp.arange(LAGS, dtype=jnp.int32) - LAGS // 2

    def angles(bins):
        phase = bins[:, None] * lag_index[None, :] % (2 * F)
        angle = phase.astype(jnp.float32) * (math.pi / F)
        return jnp.stack([jnp.cos(angle), jnp.sin(angle)])

    fine = angles(jnp.arange(LANES, dtype=jnp.int32))
    coarse = angles(LANES * jnp.arange(FH, dtype=jnp.int32))
    return pl.pallas_call(
        table_kernel,
        grid=(2, LAGS // COLUMNS),
        in_specs=[
            pl.BlockSpec((2, LANES, COLUMNS), lambda s, n: (0, 0, n)),
            pl.BlockSpec((2, FH, COLUMNS), lambda s, n: (0, 0, n)),
        ],
        out_specs=pl.BlockSpec((1, F, COLUMNS), lambda s, n: (n, s, 0)),
        out_shape=pltpu.HBM((LAGS // COLUMNS, 2 * F, COLUMNS), jnp.bfloat16),
        compiler_params=pltpu.CompilerParams(vmem_limit_bytes=16 * 1024 * 1024),
        cost_estimate=pl.CostEstimate(flops=16_000_000, bytes_accessed=12_000_000, transcendentals=0),
        name="lag_table",
    )(fine, coarse)


def shifted(block, axis, by):
    size = lax.axis_size(axis)
    return lax.ppermute(block, axis, [(i, (i + by) % size) for i in range(size)])


def swapped(block):
    return lax.ppermute(block, "blk", [(i, i ^ 1) for i in range(lax.axis_size("blk"))])


def spread(block, planes):
    starts = range(0, lax.axis_size("region"), planes)
    return [
        lax.ppermute(
            block[plane * PIECE : (plane + 1) * PIECE],
            "region",
            [(n + planes - 1, n + plane) for n in starts],
        )
        for plane in range(planes - 1)
    ]


def from_previous_region(block, piece, planes, *after):
    regions = lax.axis_size("region")
    near = lax.ppermute(
        block, "region", [(i, i + 1) for i in range(regions) if (i + 1) % planes]
    )
    piece = lax.ppermute(piece, "region", [(i, (i + planes) % regions) for i in range(regions)])
    far = [piece]
    piece = relay(piece, near, *after)
    for plane in range(1, planes):
        far.append(
            lax.ppermute(piece, "region", [(n + plane, n) for n in range(0, regions, planes)])
        )
    return near, far


def body(archive, unit_of, row_counts):
    blocks = lax.axis_size("blk")
    slot = jnp.arange(CAP, dtype=jnp.int32)
    ids = jnp.where(slot < row_counts[0], unit_of, -1)
    owners = jnp.arange(blocks, dtype=jnp.int32)
    sent = (ids >> 6)[None, :] == owners[:, None]
    key = slot * UNITS + (ids & (UNITS - 1))
    none = CAP * UNITS
    first = jnp.min(jnp.where(sent, key, none), axis=1)
    last = jnp.max(jnp.where(sent, key, -1), axis=1)
    source = jnp.clip(jnp.stack([first, last], axis=1) >> 6, 0, CAP - 1).reshape(2 * blocks)
    first_id = jnp.where(first < none, first & (UNITS - 1), -1).astype(jnp.bfloat16)
    last_id = jnp.where(last > first, last & (UNITS - 1), -1).astype(jnp.bfloat16)
    lane = jnp.arange(LANES, dtype=jnp.int32)
    marks = jnp.broadcast_to(
        jnp.where(lane[None, :] < LANES // 2, first_id[:, None], last_id[:, None])[:, None, :],
        (blocks, MARK, LANES),
    )
    send = whiten(source, archive.reshape(CAP, 3 * TILE, LANES), marks)
    got = [
        lax.all_to_all(part, "blk", split_axis=0, concat_axis=0, tiled=True) for part in send
    ]

    table = make_table()
    got[0], table = lax.optimization_barrier((got[0], table))
    found = got[0][:, 2 * len(CHUNKS[0]) * TILE, :].astype(jnp.int32)
    units = jnp.arange(UNITS, dtype=jnp.int32)[:, None]
    place = jnp.sum(
        jnp.where(found[:, 0][None, :] == units, 2 * owners[None, :], 0)
        + jnp.where(found[:, LANES - 1][None, :] == units, 2 * owners[None, :] + 1, 0),
        axis=1,
    )
    place = jnp.clip(place, 0, 2 * blocks - 1)

    planes = 4
    plane = lax.axis_index("region") % planes
    edge = (plane == 0).astype(jnp.int32)
    core = lax.axis_index("blk") & 1
    early = sort_units(place, got[0], 3 * TILE)
    piece, block = choose(plane, early, spread(early, planes))
    twin = swapped(block)
    near, far = from_previous_region(block, piece, planes, twin)
    two = shifted(block, "blk", 2)
    ahead = shifted(block, "blk", -2)
    beside = swapped(two)
    own, twin, two, ahead, beside, near, far = (
        [block] for block in ([block], [twin], [two], [ahead], [beside], [near], far)
    )
    by_two = cross(0, (((0, 1), (0, 1)),), core, (own, two), (), ())
    by_four = cross(0, (((0, 1), (0, 1)),), core, (ahead, two), (), (by_two,))
    by_region = cross(0, (((0, 1), (0, 2)),), edge, (own, near, far), (), (by_four,))
    sent = cross(0, (((1, 2), (0, 2)),), core, (own, ahead, beside), (by_four,), (by_region,))
    got_two = shifted(sent, "blk", 2)
    by_one = cross(0, (((0, 2), (0, 1)),), core, (own, twin, beside), (), (sent,))
    cycle_series, region_series = lag_series(
        core, table, by_one, by_two, sent, got_two, by_region
    )
    return jnp.swapaxes(cycle_series, 2, 3), jnp.swapaxes(region_series, 1, 2)


def solution(mesh):
    placed = (P(("region", "blk"), None, None), P(("region", "blk")), P(("region", "blk")))
    return jax.shard_map(
        body,
        mesh=mesh,
        in_specs=placed,
        out_specs=(
            P(("region", "blk"), None, None, None, None),
            P(("region", "blk"), None, None, None),
        ),
        check_vma=False,
    )
```

```python
import functools
import math

import jax
import jax.numpy as jnp
from jax import lax
from jax.experimental import pallas as pl
from jax.experimental.pallas import tpu as pltpu
from jax.sharding import PartitionSpec as P

SB = 2
SEGS = 32
F = 1024
LAGS = 2048
HALF = 24
STEPS = 4
UNITS = 64
CAP = 128
LANES = 128
FH = F // LANES
TILE = 2 * FH
epsilon = 1e-05

CHUNKS = ((0, 1, 2),)
GROUP = 32
MARK = 8
PIECE = 16
VMEM = pl.BlockSpec(memory_space=pltpu.VMEM)
SMEM = pl.BlockSpec(memory_space=pltpu.SMEM)


def pairs_of(chunk):
    before = [c for part in CHUNKS[:chunk] for c in part]
    now = before + list(CHUNKS[chunk])
    return [(c, d) for c in now for d in now if not (c in before and d in before)]


def place_of(component):
    for chunk, part in enumerate(CHUNKS):
        if component in part:
            return chunk, part.index(component)


def whiten_kernel(source_ref, band_ref, inverse_ref, archive_ref, mark_ref, *rest):
    outs, (level_ref,) = rest[:-1], rest[-1:]
    rows = GROUP * FH
    band = band_ref[...]
    inverse = inverse_ref[...]
    lane = lax.broadcasted_iota(jnp.int32, (rows, LANES), 1)
    row = lax.broadcasted_iota(jnp.int32, (rows, LANES), 0) % FH
    outs[0][:, 2 * len(CHUNKS[0]) * TILE :, :] = mark_ref[...]

    def group(step, carry):
        base = step * GROUP

        def slab_of(position):
            return archive_ref[source_ref[base + position]].astype(jnp.float32)

        def magnitude(position, carry):
            slab = slab_of(position)
            total = None
            for c in range(3):
                real = slab[c * TILE : c * TILE + FH]
                imag = slab[c * TILE + FH : (c + 1) * TILE]
                size = jnp.sqrt(real * real + imag * imag)
                total = size if total is None else total + size
            start = pl.multiple_of(FH + position * FH, FH)
            level_ref[pl.ds(start, FH), :] = total * (1.0 / 3.0)
            return carry

        lax.fori_loop(0, GROUP, magnitude, 0, unroll=8)
        here = level_ref[FH : FH + rows, :]
        before = level_ref[FH - 1 : FH - 1 + rows, :]
        after = level_ref[FH + 1 : FH + 1 + rows, :]
        edge = jnp.where(
            lane >= LANES // 2,
            jnp.where(row == 0, 0.0, before),
            jnp.where(row == FH - 1, 0.0, after),
        )
        spread = jnp.concatenate([here, edge], axis=1)
        high = spread.astype(jnp.bfloat16)
        low = (spread - high.astype(jnp.float32)).astype(jnp.bfloat16)
        window = jnp.dot(high, band, preferred_element_type=jnp.float32) + jnp.dot(
            low, band, preferred_element_type=jnp.float32
        )
        level = window.reshape(GROUP, FH, LANES) * inverse[None] + epsilon
        level_ref[FH : FH + rows, :] = (1.0 / level).reshape(rows, LANES)

        def divide(pair, carry):
            for slot in range(2):
                position = 2 * pair + slot
                slab = slab_of(position)
                gain = level_ref[pl.ds(pl.multiple_of(FH + position * FH, FH), FH), :]
                for out, part in zip(outs, CHUNKS):
                    pieces = []
                    for c in part:
                        for half in range(2):
                            start = c * TILE + half * FH
                            pieces.append(slab[start : start + FH] * gain)
                    size = len(part) * TILE
                    out[base // 2 + pair, slot * size : (slot + 1) * size, :] = (
                        jnp.concatenate(pieces, axis=0).astype(jnp.bfloat16)
                    )
            return carry

        lax.fori_loop(0, GROUP // 2, divide, 0, unroll=4)
        return carry

    lax.fori_loop(0, CAP // GROUP, group, 0)


def whiten(source, archive, marks):
    low = jnp.arange(LANES, dtype=jnp.int32)
    gap = jnp.abs(low[:, None] - low[None, :])
    band = jnp.concatenate([gap <= HALF, gap >= LANES - HALF], axis=0).astype(jnp.bfloat16)
    bin_index = jnp.arange(F, dtype=jnp.int32)
    bin_count = (
        jnp.minimum(bin_index + HALF, F - 1) - jnp.maximum(bin_index - HALF, 0) + 1
    ).astype(jnp.float32)
    inverse = (1.0 / bin_count).reshape(FH, LANES)
    sizes = [2 * len(part) * TILE for part in CHUNKS]
    sizes[0] += MARK
    return pl.pallas_call(
        whiten_kernel,
        in_specs=[SMEM, VMEM, VMEM, VMEM, VMEM],
        out_specs=[VMEM for _ in sizes],
        out_shape=[
            jax.ShapeDtypeStruct((marks.shape[0], size, LANES), jnp.bfloat16) for size in sizes
        ],
        scratch_shapes=[pltpu.VMEM((GROUP * FH + 2 * FH, LANES), jnp.float32)],
        compiler_params=pltpu.CompilerParams(vmem_limit_bytes=16 * 1024 * 1024),
        cost_estimate=pl.CostEstimate(flops=200_000_000, bytes_accessed=4_000_000, transcendentals=0),
        name="whiten",
    )(source, band, inverse, archive, marks)


def sort_kernel(source_ref, got_ref, out_ref):
    rows = out_ref.shape[1]

    def move(unit, carry):
        place = source_ref[unit]
        start = pl.multiple_of((place & 1) * rows, TILE)
        out_ref[unit] = got_ref[place >> 1, pl.ds(start, rows), :]
        return carry

    lax.fori_loop(0, UNITS, move, 0, unroll=8)


def sort_units(source, got, rows):
    return pl.pallas_call(
        sort_kernel,
        in_specs=[SMEM, VMEM],
        out_specs=VMEM,
        out_shape=jax.ShapeDtypeStruct((UNITS, rows, LANES), jnp.bfloat16),
        compiler_params=pltpu.CompilerParams(vmem_limit_bytes=16 * 1024 * 1024),
        cost_estimate=pl.CostEstimate(flops=0, bytes_accessed=3_000_000, transcendentals=0),
        name="sort_units",
    )(source, got)


def choose_kernel(plane_ref, block_ref, *refs):
    pieces, (piece_ref, out_ref) = refs[:-2], refs[-2:]
    last = len(pieces)
    out_ref[...] = block_ref[...]
    for plane, ref in enumerate(pieces):

        @pl.when(plane_ref[0] == plane)
        def _(ref=ref):
            piece_ref[...] = ref[...]

    @pl.when(plane_ref[0] == last)
    def _():
        piece_ref[...] = block_ref[last * PIECE :]


def choose(plane, block, pieces):
    return pl.pallas_call(
        choose_kernel,
        in_specs=[SMEM] + [VMEM] * (1 + len(pieces)),
        out_specs=[VMEM, VMEM],
        out_shape=[
            jax.ShapeDtypeStruct(pieces[0].shape, jnp.bfloat16),
            jax.ShapeDtypeStruct(block.shape, jnp.bfloat16),
        ],
        compiler_params=pltpu.CompilerParams(vmem_limit_bytes=16 * 1024 * 1024),
        cost_estimate=pl.CostEstimate(flops=20_000_000_000, bytes_accessed=2_000_000, transcendentals=0),
        name="choose_piece",
    )(plane.reshape(1), block, *pieces)


def relay_kernel(piece_ref, *refs):
    refs[-1][...] = piece_ref[...]


def relay(piece, *after):
    return pl.pallas_call(
        relay_kernel,
        in_specs=[VMEM] + [pl.BlockSpec(memory_space=pl.ANY)] * len(after),
        out_specs=VMEM,
        out_shape=jax.ShapeDtypeStruct(piece.shape, jnp.bfloat16),
        compiler_params=pltpu.CompilerParams(vmem_limit_bytes=8 * 1024 * 1024),
        cost_estimate=pl.CostEstimate(flops=20_000_000_000, bytes_accessed=400_000, transcendentals=0),
        name="relay_piece",
    )(piece, *after)


def products(left_block, right_block, chunk, store):
    pairs = pairs_of(chunk)

    def load(block, base, m, component):
        which, at = place_of(component)
        pieces = block[which]
        if len(pieces) > 1:
            ref, unit = pieces[base // PIECE], m
        else:
            ref, unit = pieces[0], base + m
        tile = ref[unit, at * TILE : (at + 1) * TILE, :].astype(jnp.float32)
        return tile[:FH], tile[FH:]

    firsts = sorted({c for c, _ in pairs})
    seconds = sorted({d for _, d in pairs})
    for i in range(SB):
        for j in range(SB):
            zero = jnp.zeros((FH, LANES), jnp.float32)
            sums = tuple((zero, zero) for _ in pairs)
            for start in range(0, SEGS, PIECE):

                def step(m, sums, start=start):
                    left = {c: load(left_block, i * SEGS + start, m, c) for c in firsts}
                    right = {d: load(right_block, j * SEGS + start, m, d) for d in seconds}
                    new = []
                    for n, (c, d) in enumerate(pairs):
                        real, imag = sums[n]
                        (ar, ai), (br, bi) = left[c], right[d]
                        new.append((real + ar * br + ai * bi, imag + ai * br - ar * bi))
                    return tuple(new)

                sums = lax.fori_loop(0, PIECE, step, sums, unroll=2)
            for n, (real, imag) in enumerate(sums):
                store(i, j, n, jnp.concatenate([real, imag], axis=0).astype(jnp.bfloat16))


def cross_kernel(chunk, plan, counts, carried, flag_ref, *refs):
    blocks, at = [], 0
    for count in counts:
        block = []
        for _ in range(chunk + 1):
            block.append(refs[at : at + count])
            at += count
        blocks.append(block)
    out = refs[-1]
    size = SB * SB
    for slot in range(carried):
        out[slot * size : (slot + 1) * size] = refs[at + slot][...]
    for slot, (when_zero, when_one) in enumerate(plan, carried):

        def store(i, j, n, tile, slot=slot):
            out[slot * size + i * SB + j, n] = tile

        if when_zero == when_one:
            products(blocks[when_zero[0]], blocks[when_zero[1]], chunk, store)
        else:
            for value, (left, right) in ((0, when_zero), (1, when_one)):

                @pl.when(flag_ref[0] == value)
                def _(right=right, left=left, store=store):
                    products(blocks[left], blocks[right], chunk, store)


def cross(chunk, plan, flag, blocks, carried=(), after=()):
    count = len(pairs_of(chunk))
    shape = ((len(carried) + len(plan)) * SB * SB, count, TILE, LANES)
    flat = [piece for block in blocks for part in block[: chunk + 1] for piece in part]
    flat += carried
    return pl.pallas_call(
        functools.partial(
            cross_kernel, chunk, plan, tuple(len(block[0]) for block in blocks), len(carried)
        ),
        in_specs=[SMEM]
        + [VMEM] * len(flat)
        + [pl.BlockSpec(memory_space=pl.ANY)] * len(after),
        out_specs=VMEM,
        out_shape=jax.ShapeDtypeStruct(shape, jnp.bfloat16),
        compiler_params=pltpu.CompilerParams(vmem_limit_bytes=24 * 1024 * 1024),
        cost_estimate=pl.CostEstimate(
            flops=len(plan) * 40_000_000, bytes_accessed=len(plan) * 1_500_000, transcendentals=0
        ),
        name="cross",
    )(flag.reshape(1), *flat, *after)


COLUMNS = 256
CYCLE_ROWS = SB * STEPS * 9 * SB
ALL_ROWS = CYCLE_ROWS + SB * 9 * SB


def series_kernel(core_ref, table_ref, one_ref, two_ref, kept_ref, got_ref, across_ref, *refs):
    cycle_ref, region_ref, wide_ref, rows_ref, held_ref, sems = refs
    step = pl.program_id(0)
    size = SB * SB

    def fetch(n):
        return pltpu.make_async_copy(table_ref.at[n], held_ref.at[n], sems.at[n])

    def place(k, source, first):
        for i in range(SB):
            for j in range(SB):
                for n, (c, d) in enumerate(pairs_of(0)):
                    if k < STEPS:
                        row = ((i * STEPS + k) * 9 + 3 * c + d) * SB + j
                    else:
                        row = CYCLE_ROWS + (i * 9 + 3 * c + d) * SB + j
                    wide_ref[row * TILE : (row + 1) * TILE, :] = source[
                        first + i * SB + j, n
                    ].astype(jnp.float32)

    @pl.when(step == 0)
    def _():
        for n in range(LAGS // COLUMNS):
            fetch(n).start()
        place(0, one_ref, 0)
        place(1, two_ref, 0)
        place(3, got_ref, 0)
        place(4, across_ref, 0)

        @pl.when(core_ref[0] == 0)
        def _():
            place(2, got_ref, size)

        @pl.when(core_ref[0] == 1)
        def _():
            place(2, kept_ref, size)

        for piece in range(TILE):
            rows_ref[:, piece * LANES : (piece + 1) * LANES] = wide_ref[
                pl.ds(piece, ALL_ROWS, stride=TILE), :
            ].astype(jnp.bfloat16)

    fetch(step).wait()
    series = jnp.dot(rows_ref[...], held_ref[step], preferred_element_type=jnp.float32)
    series = (series * (1.0 / math.sqrt(F * SEGS))).astype(jnp.bfloat16)
    for i in range(SB):
        for k in range(STEPS):
            for n in range(9):
                row = ((i * STEPS + k) * 9 + n) * SB
                cycle_ref[i, k, n] = series[row : row + SB]
        for n in range(9):
            row = CYCLE_ROWS + (i * 9 + n) * SB
            region_ref[i, n] = series[row : row + SB]


def lag_series(core, table, *sources):
    return pl.pallas_call(
        series_kernel,
        grid=(LAGS // COLUMNS,),
        in_specs=[SMEM, pl.BlockSpec(memory_space=pl.ANY)] + [VMEM] * len(sources),
        out_specs=[
            pl.BlockSpec((SB, STEPS, 9, SB, COLUMNS), lambda n: (0, 0, 0, 0, n)),
            pl.BlockSpec((SB, 9, SB, COLUMNS), lambda n: (0, 0, 0, n)),
        ],
        out_shape=[
            jax.ShapeDtypeStruct((SB, STEPS, 9, SB, LAGS), jnp.bfloat16),
            jax.ShapeDtypeStruct((SB, 9, SB, LAGS), jnp.bfloat16),
        ],
        scratch_shapes=[
            pltpu.VMEM((ALL_ROWS * TILE, LANES), jnp.float32),
            pltpu.VMEM((ALL_ROWS, 2 * F), jnp.bfloat16),
            pltpu.VMEM((LAGS // COLUMNS, 2 * F, COLUMNS), jnp.bfloat16),
            pltpu.SemaphoreType.DMA((LAGS // COLUMNS,)),
        ],
        compiler_params=pltpu.CompilerParams(vmem_limit_bytes=32 * 1024 * 1024),
        cost_estimate=pl.CostEstimate(
            flops=2 * ALL_ROWS * 2 * F * LAGS, bytes_accessed=12_000_000, transcendentals=0
        ),
        name="lag_series",
    )(core.reshape(1), pltpu.with_memory_space_constraint(table, pltpu.HBM), *sources)


def table_kernel(fine_ref, coarse_ref, out_ref):
    step = pl.program_id(0)
    for high in range(FH):
        cos_high = coarse_ref[0, high : high + 1, :]
        sin_high = coarse_ref[1, high : high + 1, :]
        cos_low, sin_low = fine_ref[0], fine_ref[1]

        @pl.when(step == 0)
        def _(high=high):
            out_ref[0, high * LANES : (high + 1) * LANES, :] = (
                cos_low * cos_high - sin_low * sin_high
            ).astype(jnp.bfloat16)

        @pl.when(step == 1)
        def _(high=high):
            out_ref[0, high * LANES : (high + 1) * LANES, :] = (
                -(sin_low * cos_high + cos_low * sin_high)
            ).astype(jnp.bfloat16)


def make_table():
    lag_index = jnp.arange(LAGS, dtype=jnp.int32) - LAGS // 2

    def angles(bins):
        phase = bins[:, None] * lag_index[None, :] % (2 * F)
        angle = phase.astype(jnp.float32) * (math.pi / F)
        return jnp.stack([jnp.cos(angle), jnp.sin(angle)])

    fine = angles(jnp.arange(LANES, dtype=jnp.int32))
    coarse = angles(LANES * jnp.arange(FH, dtype=jnp.int32))
    return pl.pallas_call(
        table_kernel,
        grid=(2, LAGS // COLUMNS),
        in_specs=[
            pl.BlockSpec((2, LANES, COLUMNS), lambda s, n: (0, 0, n)),
            pl.BlockSpec((2, FH, COLUMNS), lambda s, n: (0, 0, n)),
        ],
        out_specs=pl.BlockSpec((1, F, COLUMNS), lambda s, n: (n, s, 0)),
        out_shape=pltpu.HBM((LAGS // COLUMNS, 2 * F, COLUMNS), jnp.bfloat16),
        compiler_params=pltpu.CompilerParams(vmem_limit_bytes=16 * 1024 * 1024),
        cost_estimate=pl.CostEstimate(flops=16_000_000, bytes_accessed=12_000_000, transcendentals=0),
        name="lag_table",
    )(fine, coarse)


def shifted(block, axis, by):
    size = lax.axis_size(axis)
    return lax.ppermute(block, axis, [(i, (i + by) % size) for i in range(size)])


def swapped(block):
    return lax.ppermute(block, "blk", [(i, i ^ 1) for i in range(lax.axis_size("blk"))])


def spread(block, planes):
    starts = range(0, lax.axis_size("region"), planes)
    return [
        lax.ppermute(
            block[plane * PIECE : (plane + 1) * PIECE],
            "region",
            [(n + planes - 1, n + plane) for n in starts],
        )
        for plane in range(planes - 1)
    ]


def from_previous_region(block, piece, planes, *after):
    regions = lax.axis_size("region")
    near = lax.ppermute(
        block, "region", [(i, i + 1) for i in range(regions) if (i + 1) % planes]
    )
    piece = lax.ppermute(piece, "region", [(i, (i + planes) % regions) for i in range(regions)])
    far = [piece]
    piece = relay(piece, near, *after)
    for plane in range(1, planes):
        far.append(
            lax.ppermute(piece, "region", [(n + plane, n) for n in range(0, regions, planes)])
        )
    return near, far


def body(archive, unit_of, row_counts):
    blocks = lax.axis_size("blk")
    slot = jnp.arange(CAP, dtype=jnp.int32)
    ids = jnp.where(slot < row_counts[0], unit_of, -1)
    owners = jnp.arange(blocks, dtype=jnp.int32)
    sent = (ids >> 6)[None, :] == owners[:, None]
    key = slot * UNITS + (ids & (UNITS - 1))
    none = CAP * UNITS
    first = jnp.min(jnp.where(sent, key, none), axis=1)
    last = jnp.max(jnp.where(sent, key, -1), axis=1)
    source = jnp.clip(jnp.stack([first, last], axis=1) >> 6, 0, CAP - 1).reshape(2 * blocks)
    first_id = jnp.where(first < none, first & (UNITS - 1), -1).astype(jnp.bfloat16)
    last_id = jnp.where(last > first, last & (UNITS - 1), -1).astype(jnp.bfloat16)
    lane = jnp.arange(LANES, dtype=jnp.int32)
    marks = jnp.broadcast_to(
        jnp.where(lane[None, :] < LANES // 2, first_id[:, None], last_id[:, None])[:, None, :],
        (blocks, MARK, LANES),
    )
    send = whiten(source, archive.reshape(CAP, 3 * TILE, LANES), marks)
    got = [
        lax.all_to_all(part, "blk", split_axis=0, concat_axis=0, tiled=True) for part in send
    ]

    table = make_table()
    got[0], table = lax.optimization_barrier((got[0], table))
    found = got[0][:, 2 * len(CHUNKS[0]) * TILE, :].astype(jnp.int32)
    units = jnp.arange(UNITS, dtype=jnp.int32)[:, None]
    place = jnp.sum(
        jnp.where(found[:, 0][None, :] == units, 2 * owners[None, :], 0)
        + jnp.where(found[:, LANES - 1][None, :] == units, 2 * owners[None, :] + 1, 0),
        axis=1,
    )
    place = jnp.clip(place, 0, 2 * blocks - 1)

    planes = 4
    plane = lax.axis_index("region") % planes
    edge = (plane == 0).astype(jnp.int32)
    core = lax.axis_index("blk") & 1
    early = sort_units(place, got[0], 3 * TILE)
    piece, block = choose(plane, early, spread(early, planes))
    twin = swapped(early)
    near, far = from_previous_region(early, piece, planes, twin)
    two = shifted(early, "blk", 2)
    ahead = shifted(block, "blk", -2)
    beside = swapped(two)
    own, twin, two, ahead, beside, near, far = (
        [block] for block in ([block], [twin], [two], [ahead], [beside], [near], far)
    )
    by_two = cross(0, (((0, 1), (0, 1)),), core, (own, two), (), ())
    by_four = cross(0, (((0, 1), (0, 1)),), core, (ahead, two), (), (by_two,))
    by_region = cross(0, (((0, 1), (0, 2)),), edge, (own, near, far), (), (by_four,))
    sent = cross(0, (((1, 2), (0, 2)),), core, (own, ahead, beside), (by_four,), (by_region,))
    got_two = shifted(sent, "blk", 2)
    by_one = cross(0, (((0, 2), (0, 1)),), core, (own, twin, beside), (), (sent,))
    cycle_series, region_series = lag_series(
        core, table, by_one, by_two, sent, got_two, by_region
    )
    return jnp.swapaxes(cycle_series, 2, 3), jnp.swapaxes(region_series, 1, 2)


def solution(mesh):
    placed = (P(("region", "blk"), None, None), P(("region", "blk")), P(("region", "blk")))
    return jax.shard_map(
        body,
        mesh=mesh,
        in_specs=placed,
        out_specs=(
            P(("region", "blk"), None, None, None, None),
            P(("region", "blk"), None, None, None),
        ),
        check_vma=False,
    )
```

```python
import functools
import math

import jax
import jax.numpy as jnp
from jax import lax
from jax.experimental import pallas as pl
from jax.experimental.pallas import tpu as pltpu
from jax.sharding import PartitionSpec as P

SB = 2
SEGS = 32
F = 1024
LAGS = 2048
HALF = 24
STEPS = 4
UNITS = 64
CAP = 128
LANES = 128
FH = F // LANES
TILE = 2 * FH
epsilon = 1e-05

CHUNKS = ((0, 1, 2),)
GROUP = 32
MARK = 8
PIECE = 16
VMEM = pl.BlockSpec(memory_space=pltpu.VMEM)
SMEM = pl.BlockSpec(memory_space=pltpu.SMEM)


def pairs_of(chunk):
    before = [c for part in CHUNKS[:chunk] for c in part]
    now = before + list(CHUNKS[chunk])
    return [(c, d) for c in now for d in now if not (c in before and d in before)]


def place_of(component):
    for chunk, part in enumerate(CHUNKS):
        if component in part:
            return chunk, part.index(component)


def whiten_kernel(source_ref, band_ref, inverse_ref, archive_ref, mark_ref, *rest):
    outs, (level_ref,) = rest[:-1], rest[-1:]
    rows = GROUP * FH
    band = band_ref[...]
    inverse = inverse_ref[...]
    lane = lax.broadcasted_iota(jnp.int32, (rows, LANES), 1)
    row = lax.broadcasted_iota(jnp.int32, (rows, LANES), 0) % FH
    outs[0][:, 2 * len(CHUNKS[0]) * TILE :, :] = mark_ref[...]

    def group(step, carry):
        base = step * GROUP

        def slab_of(position):
            return archive_ref[source_ref[base + position]].astype(jnp.float32)

        def magnitude(position, carry):
            slab = slab_of(position)
            total = None
            for c in range(3):
                real = slab[c * TILE : c * TILE + FH]
                imag = slab[c * TILE + FH : (c + 1) * TILE]
                size = jnp.sqrt(real * real + imag * imag)
                total = size if total is None else total + size
            start = pl.multiple_of(FH + position * FH, FH)
            level_ref[pl.ds(start, FH), :] = total * (1.0 / 3.0)
            return carry

        lax.fori_loop(0, GROUP, magnitude, 0, unroll=8)
        here = level_ref[FH : FH + rows, :]
        before = level_ref[FH - 1 : FH - 1 + rows, :]
        after = level_ref[FH + 1 : FH + 1 + rows, :]
        edge = jnp.where(
            lane >= LANES // 2,
            jnp.where(row == 0, 0.0, before),
            jnp.where(row == FH - 1, 0.0, after),
        )
        spread = jnp.concatenate([here, edge], axis=1)
        high = spread.astype(jnp.bfloat16)
        low = (spread - high.astype(jnp.float32)).astype(jnp.bfloat16)
        window = jnp.dot(high, band, preferred_element_type=jnp.float32) + jnp.dot(
            low, band, preferred_element_type=jnp.float32
        )
        level = window.reshape(GROUP, FH, LANES) * inverse[None] + epsilon
        level_ref[FH : FH + rows, :] = (1.0 / level).reshape(rows, LANES)

        def divide(pair, carry):
            for slot in range(2):
                position = 2 * pair + slot
                slab = slab_of(position)
                gain = level_ref[pl.ds(pl.multiple_of(FH + position * FH, FH), FH), :]
                for out, part in zip(outs, CHUNKS):
                    pieces = []
                    for c in part:
                        for half in range(2):
                            start = c * TILE + half * FH
                            pieces.append(slab[start : start + FH] * gain)
                    size = len(part) * TILE
                    out[base // 2 + pair, slot * size : (slot + 1) * size, :] = (
                        jnp.concatenate(pieces, axis=0).astype(jnp.bfloat16)
                    )
            return carry

        lax.fori_loop(0, GROUP // 2, divide, 0, unroll=4)
        return carry

    lax.fori_loop(0, CAP // GROUP, group, 0)


def whiten(source, archive, marks):
    low = jnp.arange(LANES, dtype=jnp.int32)
    gap = jnp.abs(low[:, None] - low[None, :])
    band = jnp.concatenate([gap <= HALF, gap >= LANES - HALF], axis=0).astype(jnp.bfloat16)
    bin_index = jnp.arange(F, dtype=jnp.int32)
    bin_count = (
        jnp.minimum(bin_index + HALF, F - 1) - jnp.maximum(bin_index - HALF, 0) + 1
    ).astype(jnp.float32)
    inverse = (1.0 / bin_count).reshape(FH, LANES)
    sizes = [2 * len(part) * TILE for part in CHUNKS]
    sizes[0] += MARK
    return pl.pallas_call(
        whiten_kernel,
        in_specs=[SMEM, VMEM, VMEM, VMEM, VMEM],
        out_specs=[VMEM for _ in sizes],
        out_shape=[
            jax.ShapeDtypeStruct((marks.shape[0], size, LANES), jnp.bfloat16) for size in sizes
        ],
        scratch_shapes=[pltpu.VMEM((GROUP * FH + 2 * FH, LANES), jnp.float32)],
        compiler_params=pltpu.CompilerParams(vmem_limit_bytes=16 * 1024 * 1024),
        cost_estimate=pl.CostEstimate(flops=200_000_000, bytes_accessed=4_000_000, transcendentals=0),
        name="whiten",
    )(source, band, inverse, archive, marks)


def sort_kernel(source_ref, got_ref, out_ref, *piece_refs):
    rows = out_ref.shape[1]

    def move(unit, carry):
        place = source_ref[unit]
        start = pl.multiple_of((place & 1) * rows, TILE)
        out_ref[unit] = got_ref[place >> 1, pl.ds(start, rows), :]
        return carry

    lax.fori_loop(0, UNITS, move, 0, unroll=8)
    for n, ref in enumerate(piece_refs):
        ref[...] = out_ref[n * PIECE : (n + 1) * PIECE]


def sort_units(source, got, rows, pieces):
    shapes = [(UNITS, rows, LANES)] + [(PIECE, rows, LANES)] * pieces
    return pl.pallas_call(
        sort_kernel,
        in_specs=[SMEM, VMEM],
        out_specs=[VMEM for _ in shapes],
        out_shape=[jax.ShapeDtypeStruct(shape, jnp.bfloat16) for shape in shapes],
        compiler_params=pltpu.CompilerParams(vmem_limit_bytes=16 * 1024 * 1024),
        cost_estimate=pl.CostEstimate(flops=0, bytes_accessed=3_000_000, transcendentals=0),
        name="sort_units",
    )(source, got)


def choose_kernel(plane_ref, block_ref, *refs):
    pieces, (piece_ref, out_ref) = refs[:-2], refs[-2:]
    last = len(pieces)
    out_ref[...] = block_ref[...]
    for plane, ref in enumerate(pieces):

        @pl.when(plane_ref[0] == plane)
        def _(ref=ref):
            piece_ref[...] = ref[...]

    @pl.when(plane_ref[0] == last)
    def _():
        piece_ref[...] = block_ref[last * PIECE :]


def choose(plane, block, pieces):
    return pl.pallas_call(
        choose_kernel,
        in_specs=[SMEM] + [VMEM] * (1 + len(pieces)),
        out_specs=[VMEM, VMEM],
        out_shape=[
            jax.ShapeDtypeStruct(pieces[0].shape, jnp.bfloat16),
            jax.ShapeDtypeStruct(block.shape, jnp.bfloat16),
        ],
        compiler_params=pltpu.CompilerParams(vmem_limit_bytes=16 * 1024 * 1024),
        cost_estimate=pl.CostEstimate(flops=20_000_000_000, bytes_accessed=2_000_000, transcendentals=0),
        name="choose_piece",
    )(plane.reshape(1), block, *pieces)


def relay_kernel(piece_ref, *refs):
    refs[-1][...] = piece_ref[...]


def relay(piece, *after):
    return pl.pallas_call(
        relay_kernel,
        in_specs=[VMEM] + [pl.BlockSpec(memory_space=pl.ANY)] * len(after),
        out_specs=VMEM,
        out_shape=jax.ShapeDtypeStruct(piece.shape, jnp.bfloat16),
        compiler_params=pltpu.CompilerParams(vmem_limit_bytes=8 * 1024 * 1024),
        cost_estimate=pl.CostEstimate(flops=20_000_000_000, bytes_accessed=400_000, transcendentals=0),
        name="relay_piece",
    )(piece, *after)


def products(left_block, right_block, chunk, store):
    pairs = pairs_of(chunk)

    def load(block, base, m, component):
        which, at = place_of(component)
        pieces = block[which]
        if len(pieces) > 1:
            ref, unit = pieces[base // PIECE], m
        else:
            ref, unit = pieces[0], base + m
        tile = ref[unit, at * TILE : (at + 1) * TILE, :].astype(jnp.float32)
        return tile[:FH], tile[FH:]

    firsts = sorted({c for c, _ in pairs})
    seconds = sorted({d for _, d in pairs})
    for i in range(SB):
        for j in range(SB):
            zero = jnp.zeros((FH, LANES), jnp.float32)
            sums = tuple((zero, zero) for _ in pairs)
            for start in range(0, SEGS, PIECE):

                def step(m, sums, start=start):
                    left = {c: load(left_block, i * SEGS + start, m, c) for c in firsts}
                    right = {d: load(right_block, j * SEGS + start, m, d) for d in seconds}
                    new = []
                    for n, (c, d) in enumerate(pairs):
                        real, imag = sums[n]
                        (ar, ai), (br, bi) = left[c], right[d]
                        new.append((real + ar * br + ai * bi, imag + ai * br - ar * bi))
                    return tuple(new)

                sums = lax.fori_loop(0, PIECE, step, sums, unroll=2)
            for n, (real, imag) in enumerate(sums):
                store(i, j, n, jnp.concatenate([real, imag], axis=0).astype(jnp.bfloat16))


def cross_kernel(chunk, plan, counts, carried, flag_ref, *refs):
    blocks, at = [], 0
    for count in counts:
        block = []
        for _ in range(chunk + 1):
            block.append(refs[at : at + count])
            at += count
        blocks.append(block)
    out = refs[-1]
    size = SB * SB
    for slot in range(carried):
        out[slot * size : (slot + 1) * size] = refs[at + slot][...]
    for slot, (when_zero, when_one) in enumerate(plan, carried):

        def store(i, j, n, tile, slot=slot):
            out[slot * size + i * SB + j, n] = tile

        if when_zero == when_one:
            products(blocks[when_zero[0]], blocks[when_zero[1]], chunk, store)
        else:
            for value, (left, right) in ((0, when_zero), (1, when_one)):

                @pl.when(flag_ref[0] == value)
                def _(right=right, left=left, store=store):
                    products(blocks[left], blocks[right], chunk, store)


def cross(chunk, plan, flag, blocks, carried=(), after=()):
    count = len(pairs_of(chunk))
    shape = ((len(carried) + len(plan)) * SB * SB, count, TILE, LANES)
    flat = [piece for block in blocks for part in block[: chunk + 1] for piece in part]
    flat += carried
    return pl.pallas_call(
        functools.partial(
            cross_kernel, chunk, plan, tuple(len(block[0]) for block in blocks), len(carried)
        ),
        in_specs=[SMEM]
        + [VMEM] * len(flat)
        + [pl.BlockSpec(memory_space=pl.ANY)] * len(after),
        out_specs=VMEM,
        out_shape=jax.ShapeDtypeStruct(shape, jnp.bfloat16),
        compiler_params=pltpu.CompilerParams(vmem_limit_bytes=24 * 1024 * 1024),
        cost_estimate=pl.CostEstimate(
            flops=len(plan) * 40_000_000, bytes_accessed=len(plan) * 1_500_000, transcendentals=0
        ),
        name="cross",
    )(flag.reshape(1), *flat, *after)


COLUMNS = 256
CYCLE_ROWS = SB * STEPS * 9 * SB
ALL_ROWS = CYCLE_ROWS + SB * 9 * SB


def series_kernel(core_ref, table_ref, one_ref, two_ref, kept_ref, got_ref, across_ref, *refs):
    cycle_ref, region_ref, wide_ref, rows_ref, held_ref, sems = refs
    step = pl.program_id(0)
    size = SB * SB

    def fetch(n):
        return pltpu.make_async_copy(table_ref.at[n], held_ref.at[n], sems.at[n])

    def place(k, source, first):
        for i in range(SB):
            for j in range(SB):
                for n, (c, d) in enumerate(pairs_of(0)):
                    if k < STEPS:
                        row = ((i * STEPS + k) * 9 + 3 * c + d) * SB + j
                    else:
                        row = CYCLE_ROWS + (i * 9 + 3 * c + d) * SB + j
                    wide_ref[row * TILE : (row + 1) * TILE, :] = source[
                        first + i * SB + j, n
                    ].astype(jnp.float32)

    @pl.when(step == 0)
    def _():
        for n in range(LAGS // COLUMNS):
            fetch(n).start()
        place(0, one_ref, 0)
        place(1, two_ref, 0)
        place(3, got_ref, 0)
        place(4, across_ref, 0)

        @pl.when(core_ref[0] == 0)
        def _():
            place(2, got_ref, size)

        @pl.when(core_ref[0] == 1)
        def _():
            place(2, kept_ref, size)

        for piece in range(TILE):
            rows_ref[:, piece * LANES : (piece + 1) * LANES] = wide_ref[
                pl.ds(piece, ALL_ROWS, stride=TILE), :
            ].astype(jnp.bfloat16)

    fetch(step).wait()
    series = jnp.dot(rows_ref[...], held_ref[step], preferred_element_type=jnp.float32)
    series = (series * (1.0 / math.sqrt(F * SEGS))).astype(jnp.bfloat16)
    for i in range(SB):
        for k in range(STEPS):
            for n in range(9):
                row = ((i * STEPS + k) * 9 + n) * SB
                cycle_ref[i, k, n] = series[row : row + SB]
        for n in range(9):
            row = CYCLE_ROWS + (i * 9 + n) * SB
            region_ref[i, n] = series[row : row + SB]


def lag_series(core, table, *sources):
    return pl.pallas_call(
        series_kernel,
        grid=(LAGS // COLUMNS,),
        in_specs=[SMEM, pl.BlockSpec(memory_space=pl.ANY)] + [VMEM] * len(sources),
        out_specs=[
            pl.BlockSpec((SB, STEPS, 9, SB, COLUMNS), lambda n: (0, 0, 0, 0, n)),
            pl.BlockSpec((SB, 9, SB, COLUMNS), lambda n: (0, 0, 0, n)),
        ],
        out_shape=[
            jax.ShapeDtypeStruct((SB, STEPS, 9, SB, LAGS), jnp.bfloat16),
            jax.ShapeDtypeStruct((SB, 9, SB, LAGS), jnp.bfloat16),
        ],
        scratch_shapes=[
            pltpu.VMEM((ALL_ROWS * TILE, LANES), jnp.float32),
            pltpu.VMEM((ALL_ROWS, 2 * F), jnp.bfloat16),
            pltpu.VMEM((LAGS // COLUMNS, 2 * F, COLUMNS), jnp.bfloat16),
            pltpu.SemaphoreType.DMA((LAGS // COLUMNS,)),
        ],
        compiler_params=pltpu.CompilerParams(vmem_limit_bytes=32 * 1024 * 1024),
        cost_estimate=pl.CostEstimate(
            flops=2 * ALL_ROWS * 2 * F * LAGS, bytes_accessed=12_000_000, transcendentals=0
        ),
        name="lag_series",
    )(core.reshape(1), pltpu.with_memory_space_constraint(table, pltpu.HBM), *sources)


def table_kernel(fine_ref, coarse_ref, out_ref):
    step = pl.program_id(0)
    for high in range(FH):
        cos_high = coarse_ref[0, high : high + 1, :]
        sin_high = coarse_ref[1, high : high + 1, :]
        cos_low, sin_low = fine_ref[0], fine_ref[1]

        @pl.when(step == 0)
        def _(high=high):
            out_ref[0, high * LANES : (high + 1) * LANES, :] = (
                cos_low * cos_high - sin_low * sin_high
            ).astype(jnp.bfloat16)

        @pl.when(step == 1)
        def _(high=high):
            out_ref[0, high * LANES : (high + 1) * LANES, :] = (
                -(sin_low * cos_high + cos_low * sin_high)
            ).astype(jnp.bfloat16)


def make_table():
    lag_index = jnp.arange(LAGS, dtype=jnp.int32) - LAGS // 2

    def angles(bins):
        phase = bins[:, None] * lag_index[None, :] % (2 * F)
        angle = phase.astype(jnp.float32) * (math.pi / F)
        return jnp.stack([jnp.cos(angle), jnp.sin(angle)])

    fine = angles(jnp.arange(LANES, dtype=jnp.int32))
    coarse = angles(LANES * jnp.arange(FH, dtype=jnp.int32))
    return pl.pallas_call(
        table_kernel,
        grid=(2, LAGS // COLUMNS),
        in_specs=[
            pl.BlockSpec((2, LANES, COLUMNS), lambda s, n: (0, 0, n)),
            pl.BlockSpec((2, FH, COLUMNS), lambda s, n: (0, 0, n)),
        ],
        out_specs=pl.BlockSpec((1, F, COLUMNS), lambda s, n: (n, s, 0)),
        out_shape=pltpu.HBM((LAGS // COLUMNS, 2 * F, COLUMNS), jnp.bfloat16),
        compiler_params=pltpu.CompilerParams(vmem_limit_bytes=16 * 1024 * 1024),
        cost_estimate=pl.CostEstimate(flops=16_000_000, bytes_accessed=12_000_000, transcendentals=0),
        name="lag_table",
    )(fine, coarse)


def shifted(block, axis, by):
    size = lax.axis_size(axis)
    return lax.ppermute(block, axis, [(i, (i + by) % size) for i in range(size)])


def swapped(block):
    return lax.ppermute(block, "blk", [(i, i ^ 1) for i in range(lax.axis_size("blk"))])


def spread(pieces):
    planes = len(pieces) + 1
    starts = range(0, lax.axis_size("region"), planes)
    return [
        lax.ppermute(piece, "region", [(n + planes - 1, n + plane) for n in starts])
        for plane, piece in enumerate(pieces)
    ]


def from_previous_region(block, piece, planes, *after):
    regions = lax.axis_size("region")
    near = lax.ppermute(
        block, "region", [(i, i + 1) for i in range(regions) if (i + 1) % planes]
    )
    piece = lax.ppermute(piece, "region", [(i, (i + planes) % regions) for i in range(regions)])
    far = [piece]
    piece = relay(piece, near, *after)
    for plane in range(1, planes):
        far.append(
            lax.ppermute(piece, "region", [(n + plane, n) for n in range(0, regions, planes)])
        )
    return near, far, piece


def body(archive, unit_of, row_counts):
    blocks = lax.axis_size("blk")
    slot = jnp.arange(CAP, dtype=jnp.int32)
    ids = jnp.where(slot < row_counts[0], unit_of, -1)
    owners = jnp.arange(blocks, dtype=jnp.int32)
    sent = (ids >> 6)[None, :] == owners[:, None]
    key = slot * UNITS + (ids & (UNITS - 1))
    none = CAP * UNITS
    first = jnp.min(jnp.where(sent, key, none), axis=1)
    last = jnp.max(jnp.where(sent, key, -1), axis=1)
    source = jnp.clip(jnp.stack([first, last], axis=1) >> 6, 0, CAP - 1).reshape(2 * blocks)
    first_id = jnp.where(first < none, first & (UNITS - 1), -1).astype(jnp.bfloat16)
    last_id = jnp.where(last > first, last & (UNITS - 1), -1).astype(jnp.bfloat16)
    lane = jnp.arange(LANES, dtype=jnp.int32)
    marks = jnp.broadcast_to(
        jnp.where(lane[None, :] < LANES // 2, first_id[:, None], last_id[:, None])[:, None, :],
        (blocks, MARK, LANES),
    )
    send = whiten(source, archive.reshape(CAP, 3 * TILE, LANES), marks)
    got = [
        lax.all_to_all(part, "blk", split_axis=0, concat_axis=0, tiled=True) for part in send
    ]

    table = make_table()
    got[0], table = lax.optimization_barrier((got[0], table))
    found = got[0][:, 2 * len(CHUNKS[0]) * TILE, :].astype(jnp.int32)
    units = jnp.arange(UNITS, dtype=jnp.int32)[:, None]
    place = jnp.sum(
        jnp.where(found[:, 0][None, :] == units, 2 * owners[None, :], 0)
        + jnp.where(found[:, LANES - 1][None, :] == units, 2 * owners[None, :] + 1, 0),
        axis=1,
    )
    place = jnp.clip(place, 0, 2 * blocks - 1)

    planes = 4
    plane = lax.axis_index("region") % planes
    edge = (plane == 0).astype(jnp.int32)
    core = lax.axis_index("blk") & 1
    early, *pieces = sort_units(place, got[0], 3 * TILE, planes - 1)
    piece, block = choose(plane, early, spread(pieces))
    twin = swapped(early)
    near, far, passed = from_previous_region(early, piece, planes, twin)
    two = shifted(early, "blk", 2)
    ahead = shifted(block, "blk", -2)
    beside = swapped(two)
    own, twin, two, ahead, beside, near, far = (
        [block] for block in ([block], [twin], [two], [ahead], [beside], [near], far)
    )
    by_four = cross(0, (((0, 1), (0, 1)),), core, (ahead, two), (), (passed,))
    sent = cross(0, (((1, 2), (0, 2)),), core, (own, ahead, beside), (by_four,))
    got_two = shifted(sent, "blk", 2)
    by_two = cross(0, (((0, 1), (0, 1)),), core, (own, two), (), (sent,))
    by_one = cross(0, (((0, 2), (0, 1)),), core, (own, twin, beside), (), (by_two,))
    by_region = cross(0, (((0, 1), (0, 2)),), edge, (own, near, far), (), (by_one,))
    cycle_series, region_series = lag_series(
        core, table, by_one, by_two, sent, got_two, by_region
    )
    return jnp.swapaxes(cycle_series, 2, 3), jnp.swapaxes(region_series, 1, 2)


def solution(mesh):
    placed = (P(("region", "blk"), None, None), P(("region", "blk")), P(("region", "blk")))
    return jax.shard_map(
        body,
        mesh=mesh,
        in_specs=placed,
        out_specs=(
            P(("region", "blk"), None, None, None, None),
            P(("region", "blk"), None, None, None),
        ),
        check_vma=False,
    )
```

```python
import functools
import math

import jax
import jax.numpy as jnp
from jax import lax
from jax.experimental import pallas as pl
from jax.experimental.pallas import tpu as pltpu
from jax.sharding import PartitionSpec as P

SB = 2
SEGS = 32
F = 1024
LAGS = 2048
HALF = 24
STEPS = 4
UNITS = 64
CAP = 128
LANES = 128
FH = F // LANES
TILE = 2 * FH
epsilon = 1e-05

CHUNKS = ((0, 1, 2),)
GROUP = 32
MARK = 8
PIECE = 16
VMEM = pl.BlockSpec(memory_space=pltpu.VMEM)
SMEM = pl.BlockSpec(memory_space=pltpu.SMEM)


def pairs_of(chunk):
    before = [c for part in CHUNKS[:chunk] for c in part]
    now = before + list(CHUNKS[chunk])
    return [(c, d) for c in now for d in now if not (c in before and d in before)]


def place_of(component):
    for chunk, part in enumerate(CHUNKS):
        if component in part:
            return chunk, part.index(component)


def whiten_kernel(source_ref, band_ref, inverse_ref, archive_ref, mark_ref, *rest):
    outs, (level_ref,) = rest[:-1], rest[-1:]
    rows = GROUP * FH
    band = band_ref[...]
    inverse = inverse_ref[...]
    lane = lax.broadcasted_iota(jnp.int32, (rows, LANES), 1)
    row = lax.broadcasted_iota(jnp.int32, (rows, LANES), 0) % FH
    outs[0][:, 2 * len(CHUNKS[0]) * TILE :, :] = mark_ref[...]

    def group(step, carry):
        base = step * GROUP

        def slab_of(position):
            return archive_ref[source_ref[base + position]].astype(jnp.float32)

        def magnitude(position, carry):
            slab = slab_of(position)
            total = None
            for c in range(3):
                real = slab[c * TILE : c * TILE + FH]
                imag = slab[c * TILE + FH : (c + 1) * TILE]
                size = jnp.sqrt(real * real + imag * imag)
                total = size if total is None else total + size
            start = pl.multiple_of(FH + position * FH, FH)
            level_ref[pl.ds(start, FH), :] = total * (1.0 / 3.0)
            return carry

        lax.fori_loop(0, GROUP, magnitude, 0, unroll=8)
        here = level_ref[FH : FH + rows, :]
        before = level_ref[FH - 1 : FH - 1 + rows, :]
        after = level_ref[FH + 1 : FH + 1 + rows, :]
        edge = jnp.where(
            lane >= LANES // 2,
            jnp.where(row == 0, 0.0, before),
            jnp.where(row == FH - 1, 0.0, after),
        )
        spread = jnp.concatenate([here, edge], axis=1)
        high = spread.astype(jnp.bfloat16)
        low = (spread - high.astype(jnp.float32)).astype(jnp.bfloat16)
        window = jnp.dot(high, band, preferred_element_type=jnp.float32) + jnp.dot(
            low, band, preferred_element_type=jnp.float32
        )
        level = window.reshape(GROUP, FH, LANES) * inverse[None] + epsilon
        level_ref[FH : FH + rows, :] = (1.0 / level).reshape(rows, LANES)

        def divide(pair, carry):
            for slot in range(2):
                position = 2 * pair + slot
                slab = slab_of(position)
                gain = level_ref[pl.ds(pl.multiple_of(FH + position * FH, FH), FH), :]
                for out, part in zip(outs, CHUNKS):
                    pieces = []
                    for c in part:
                        for half in range(2):
                            start = c * TILE + half * FH
                            pieces.append(slab[start : start + FH] * gain)
                    size = len(part) * TILE
                    out[base // 2 + pair, slot * size : (slot + 1) * size, :] = (
                        jnp.concatenate(pieces, axis=0).astype(jnp.bfloat16)
                    )
            return carry

        lax.fori_loop(0, GROUP // 2, divide, 0, unroll=4)
        return carry

    lax.fori_loop(0, CAP // GROUP, group, 0)


def whiten(source, archive, marks):
    low = jnp.arange(LANES, dtype=jnp.int32)
    gap = jnp.abs(low[:, None] - low[None, :])
    band = jnp.concatenate([gap <= HALF, gap >= LANES - HALF], axis=0).astype(jnp.bfloat16)
    bin_index = jnp.arange(F, dtype=jnp.int32)
    bin_count = (
        jnp.minimum(bin_index + HALF, F - 1) - jnp.maximum(bin_index - HALF, 0) + 1
    ).astype(jnp.float32)
    inverse = (1.0 / bin_count).reshape(FH, LANES)
    sizes = [2 * len(part) * TILE for part in CHUNKS]
    sizes[0] += MARK
    return pl.pallas_call(
        whiten_kernel,
        in_specs=[SMEM, VMEM, VMEM, VMEM, VMEM],
        out_specs=[VMEM for _ in sizes],
        out_shape=[
            jax.ShapeDtypeStruct((marks.shape[0], size, LANES), jnp.bfloat16) for size in sizes
        ],
        scratch_shapes=[pltpu.VMEM((GROUP * FH + 2 * FH, LANES), jnp.float32)],
        compiler_params=pltpu.CompilerParams(vmem_limit_bytes=8 * 1024 * 1024),
        cost_estimate=pl.CostEstimate(flops=200_000_000, bytes_accessed=4_000_000, transcendentals=0),
        name="whiten",
    )(source, band, inverse, archive, marks)


def sort_kernel(source_ref, got_ref, out_ref, *piece_refs):
    rows = out_ref.shape[1]

    def move(unit, carry):
        place = source_ref[unit]
        start = pl.multiple_of((place & 1) * rows, TILE)
        out_ref[unit] = got_ref[place >> 1, pl.ds(start, rows), :]
        return carry

    lax.fori_loop(0, UNITS, move, 0, unroll=8)
    for n, ref in enumerate(piece_refs):
        ref[...] = out_ref[n * PIECE : (n + 1) * PIECE]


def sort_units(source, got, rows, pieces):
    shapes = [(UNITS, rows, LANES)] + [(PIECE, rows, LANES)] * pieces
    return pl.pallas_call(
        sort_kernel,
        in_specs=[SMEM, VMEM],
        out_specs=[VMEM for _ in shapes],
        out_shape=[jax.ShapeDtypeStruct(shape, jnp.bfloat16) for shape in shapes],
        compiler_params=pltpu.CompilerParams(vmem_limit_bytes=6 * 1024 * 1024),
        cost_estimate=pl.CostEstimate(flops=0, bytes_accessed=3_000_000, transcendentals=0),
        name="sort_units",
    )(source, got)


def choose_kernel(plane_ref, block_ref, *refs):
    pieces, (piece_ref, out_ref) = refs[:-2], refs[-2:]
    last = len(pieces)
    out_ref[...] = block_ref[...]
    for plane, ref in enumerate(pieces):

        @pl.when(plane_ref[0] == plane)
        def _(ref=ref):
            piece_ref[...] = ref[...]

    @pl.when(plane_ref[0] == last)
    def _():
        piece_ref[...] = block_ref[last * PIECE :]


def choose(plane, block, pieces):
    return pl.pallas_call(
        choose_kernel,
        in_specs=[SMEM] + [VMEM] * (1 + len(pieces)),
        out_specs=[VMEM, VMEM],
        out_shape=[
            jax.ShapeDtypeStruct(pieces[0].shape, jnp.bfloat16),
            jax.ShapeDtypeStruct(block.shape, jnp.bfloat16),
        ],
        compiler_params=pltpu.CompilerParams(vmem_limit_bytes=6 * 1024 * 1024),
        cost_estimate=pl.CostEstimate(flops=20_000_000_000, bytes_accessed=2_000_000, transcendentals=0),
        name="choose_piece",
    )(plane.reshape(1), block, *pieces)


def relay_kernel(piece_ref, *refs):
    refs[-1][...] = piece_ref[...]


def relay(piece, *after):
    return pl.pallas_call(
        relay_kernel,
        in_specs=[VMEM] + [pl.BlockSpec(memory_space=pl.ANY)] * len(after),
        out_specs=VMEM,
        out_shape=jax.ShapeDtypeStruct(piece.shape, jnp.bfloat16),
        compiler_params=pltpu.CompilerParams(vmem_limit_bytes=4 * 1024 * 1024),
        cost_estimate=pl.CostEstimate(flops=20_000_000_000, bytes_accessed=400_000, transcendentals=0),
        name="relay_piece",
    )(piece, *after)


def products(left_block, right_block, chunk, store):
    pairs = pairs_of(chunk)

    def load(block, base, m, component):
        which, at = place_of(component)
        pieces = block[which]
        if len(pieces) > 1:
            ref, unit = pieces[base // PIECE], m
        else:
            ref, unit = pieces[0], base + m
        tile = ref[unit, at * TILE : (at + 1) * TILE, :].astype(jnp.float32)
        return tile[:FH], tile[FH:]

    firsts = sorted({c for c, _ in pairs})
    seconds = sorted({d for _, d in pairs})
    for i in range(SB):
        for j in range(SB):
            zero = jnp.zeros((FH, LANES), jnp.float32)
            sums = tuple((zero, zero) for _ in pairs)
            for start in range(0, SEGS, PIECE):

                def step(m, sums, start=start):
                    left = {c: load(left_block, i * SEGS + start, m, c) for c in firsts}
                    right = {d: load(right_block, j * SEGS + start, m, d) for d in seconds}
                    new = []
                    for n, (c, d) in enumerate(pairs):
                        real, imag = sums[n]
                        (ar, ai), (br, bi) = left[c], right[d]
                        new.append((real + ar * br + ai * bi, imag + ai * br - ar * bi))
                    return tuple(new)

                sums = lax.fori_loop(0, PIECE, step, sums, unroll=2)
            for n, (real, imag) in enumerate(sums):
                store(i, j, n, jnp.concatenate([real, imag], axis=0).astype(jnp.bfloat16))


def cross_kernel(chunk, plan, counts, carried, flag_ref, *refs):
    blocks, at = [], 0
    for count in counts:
        block = []
        for _ in range(chunk + 1):
            block.append(refs[at : at + count])
            at += count
        blocks.append(block)
    out = refs[-1]
    size = SB * SB
    for slot in range(carried):
        out[slot * size : (slot + 1) * size] = refs[at + slot][...]
    for slot, (when_zero, when_one) in enumerate(plan, carried):

        def store(i, j, n, tile, slot=slot):
            out[slot * size + i * SB + j, n] = tile

        if when_zero == when_one:
            products(blocks[when_zero[0]], blocks[when_zero[1]], chunk, store)
        else:
            for value, (left, right) in ((0, when_zero), (1, when_one)):

                @pl.when(flag_ref[0] == value)
                def _(right=right, left=left, store=store):
                    products(blocks[left], blocks[right], chunk, store)


def cross(chunk, plan, flag, blocks, carried=(), after=()):
    count = len(pairs_of(chunk))
    shape = ((len(carried) + len(plan)) * SB * SB, count, TILE, LANES)
    flat = [piece for block in blocks for part in block[: chunk + 1] for piece in part]
    flat += carried
    return pl.pallas_call(
        functools.partial(
            cross_kernel, chunk, plan, tuple(len(block[0]) for block in blocks), len(carried)
        ),
        in_specs=[SMEM]
        + [VMEM] * len(flat)
        + [pl.BlockSpec(memory_space=pl.ANY)] * len(after),
        out_specs=VMEM,
        out_shape=jax.ShapeDtypeStruct(shape, jnp.bfloat16),
        compiler_params=pltpu.CompilerParams(vmem_limit_bytes=8 * 1024 * 1024),
        cost_estimate=pl.CostEstimate(
            flops=len(plan) * 40_000_000, bytes_accessed=len(plan) * 1_500_000, transcendentals=0
        ),
        name="cross",
    )(flag.reshape(1), *flat, *after)


COLUMNS = 256
CYCLE_ROWS = SB * STEPS * 9 * SB
ALL_ROWS = CYCLE_ROWS + SB * 9 * SB


def series_kernel(core_ref, table_ref, one_ref, two_ref, kept_ref, got_ref, across_ref, *refs):
    cycle_ref, region_ref, wide_ref, rows_ref, held_ref, sems = refs
    step = pl.program_id(0)
    size = SB * SB

    def fetch(n):
        return pltpu.make_async_copy(table_ref.at[n], held_ref.at[n], sems.at[n])

    def place(k, source, first):
        for i in range(SB):
            for j in range(SB):
                for n, (c, d) in enumerate(pairs_of(0)):
                    if k < STEPS:
                        row = ((i * STEPS + k) * 9 + 3 * c + d) * SB + j
                    else:
                        row = CYCLE_ROWS + (i * 9 + 3 * c + d) * SB + j
                    wide_ref[row * TILE : (row + 1) * TILE, :] = source[
                        first + i * SB + j, n
                    ].astype(jnp.float32)

    @pl.when(step == 0)
    def _():
        for n in range(LAGS // COLUMNS):
            fetch(n).start()
        place(0, one_ref, 0)
        place(1, two_ref, 0)
        place(3, got_ref, 0)
        place(4, across_ref, 0)

        @pl.when(core_ref[0] == 0)
        def _():
            place(2, got_ref, size)

        @pl.when(core_ref[0] == 1)
        def _():
            place(2, kept_ref, size)

        for piece in range(TILE):
            rows_ref[:, piece * LANES : (piece + 1) * LANES] = wide_ref[
                pl.ds(piece, ALL_ROWS, stride=TILE), :
            ].astype(jnp.bfloat16)

    fetch(step).wait()
    series = jnp.dot(rows_ref[...], held_ref[step], preferred_element_type=jnp.float32)
    series = (series * (1.0 / math.sqrt(F * SEGS))).astype(jnp.bfloat16)
    for i in range(SB):
        for k in range(STEPS):
            for n in range(9):
                row = ((i * STEPS + k) * 9 + n) * SB
                cycle_ref[i, k, n] = series[row : row + SB]
        for n in range(9):
            row = CYCLE_ROWS + (i * 9 + n) * SB
            region_ref[i, n] = series[row : row + SB]


def lag_series(core, table, *sources):
    return pl.pallas_call(
        series_kernel,
        grid=(LAGS // COLUMNS,),
        in_specs=[SMEM, pl.BlockSpec(memory_space=pl.ANY)] + [VMEM] * len(sources),
        out_specs=[
            pl.BlockSpec((SB, STEPS, 9, SB, COLUMNS), lambda n: (0, 0, 0, 0, n)),
            pl.BlockSpec((SB, 9, SB, COLUMNS), lambda n: (0, 0, 0, n)),
        ],
        out_shape=[
            jax.ShapeDtypeStruct((SB, STEPS, 9, SB, LAGS), jnp.bfloat16),
            jax.ShapeDtypeStruct((SB, 9, SB, LAGS), jnp.bfloat16),
        ],
        scratch_shapes=[
            pltpu.VMEM((ALL_ROWS * TILE, LANES), jnp.float32),
            pltpu.VMEM((ALL_ROWS, 2 * F), jnp.bfloat16),
            pltpu.VMEM((LAGS // COLUMNS, 2 * F, COLUMNS), jnp.bfloat16),
            pltpu.SemaphoreType.DMA((LAGS // COLUMNS,)),
        ],
        compiler_params=pltpu.CompilerParams(vmem_limit_bytes=18 * 1024 * 1024),
        cost_estimate=pl.CostEstimate(
            flops=2 * ALL_ROWS * 2 * F * LAGS, bytes_accessed=12_000_000, transcendentals=0
        ),
        name="lag_series",
    )(core.reshape(1), pltpu.with_memory_space_constraint(table, pltpu.HBM), *sources)


def table_kernel(fine_ref, coarse_ref, out_ref):
    step = pl.program_id(0)
    for high in range(FH):
        cos_high = coarse_ref[0, high : high + 1, :]
        sin_high = coarse_ref[1, high : high + 1, :]
        cos_low, sin_low = fine_ref[0], fine_ref[1]

        @pl.when(step == 0)
        def _(high=high):
            out_ref[0, high * LANES : (high + 1) * LANES, :] = (
                cos_low * cos_high - sin_low * sin_high
            ).astype(jnp.bfloat16)

        @pl.when(step == 1)
        def _(high=high):
            out_ref[0, high * LANES : (high + 1) * LANES, :] = (
                -(sin_low * cos_high + cos_low * sin_high)
            ).astype(jnp.bfloat16)


def make_table():
    lag_index = jnp.arange(LAGS, dtype=jnp.int32) - LAGS // 2

    def angles(bins):
        phase = bins[:, None] * lag_index[None, :] % (2 * F)
        angle = phase.astype(jnp.float32) * (math.pi / F)
        return jnp.stack([jnp.cos(angle), jnp.sin(angle)])

    fine = angles(jnp.arange(LANES, dtype=jnp.int32))
    coarse = angles(LANES * jnp.arange(FH, dtype=jnp.int32))
    return pl.pallas_call(
        table_kernel,
        grid=(2, LAGS // COLUMNS),
        in_specs=[
            pl.BlockSpec((2, LANES, COLUMNS), lambda s, n: (0, 0, n)),
            pl.BlockSpec((2, FH, COLUMNS), lambda s, n: (0, 0, n)),
        ],
        out_specs=pl.BlockSpec((1, F, COLUMNS), lambda s, n: (n, s, 0)),
        out_shape=pltpu.HBM((LAGS // COLUMNS, 2 * F, COLUMNS), jnp.bfloat16),
        compiler_params=pltpu.CompilerParams(vmem_limit_bytes=8 * 1024 * 1024),
        cost_estimate=pl.CostEstimate(flops=16_000_000, bytes_accessed=12_000_000, transcendentals=0),
        name="lag_table",
    )(fine, coarse)


def shifted(block, axis, by):
    size = lax.axis_size(axis)
    return lax.ppermute(block, axis, [(i, (i + by) % size) for i in range(size)])


def swapped(block):
    return lax.ppermute(block, "blk", [(i, i ^ 1) for i in range(lax.axis_size("blk"))])


def spread(pieces):
    planes = len(pieces) + 1
    starts = range(0, lax.axis_size("region"), planes)
    return [
        lax.ppermute(piece, "region", [(n + planes - 1, n + plane) for n in starts])
        for plane, piece in enumerate(pieces)
    ]


def from_previous_region(block, piece, planes, *after):
    regions = lax.axis_size("region")
    near = lax.ppermute(
        block, "region", [(i, i + 1) for i in range(regions) if (i + 1) % planes]
    )
    piece = lax.ppermute(piece, "region", [(i, (i + planes) % regions) for i in range(regions)])
    far = [piece]
    piece = relay(piece, near, *after)
    for plane in range(1, planes):
        far.append(
            lax.ppermute(piece, "region", [(n + plane, n) for n in range(0, regions, planes)])
        )
    return near, far, piece


def body(archive, unit_of, row_counts):
    blocks = lax.axis_size("blk")
    slot = jnp.arange(CAP, dtype=jnp.int32)
    ids = jnp.where(slot < row_counts[0], unit_of, -1)
    owners = jnp.arange(blocks, dtype=jnp.int32)
    sent = (ids >> 6)[None, :] == owners[:, None]
    key = slot * UNITS + (ids & (UNITS - 1))
    none = CAP * UNITS
    first = jnp.min(jnp.where(sent, key, none), axis=1)
    last = jnp.max(jnp.where(sent, key, -1), axis=1)
    source = jnp.clip(jnp.stack([first, last], axis=1) >> 6, 0, CAP - 1).reshape(2 * blocks)
    first_id = jnp.where(first < none, first & (UNITS - 1), -1).astype(jnp.bfloat16)
    last_id = jnp.where(last > first, last & (UNITS - 1), -1).astype(jnp.bfloat16)
    lane = jnp.arange(LANES, dtype=jnp.int32)
    marks = jnp.broadcast_to(
        jnp.where(lane[None, :] < LANES // 2, first_id[:, None], last_id[:, None])[:, None, :],
        (blocks, MARK, LANES),
    )
    send = whiten(source, archive.reshape(CAP, 3 * TILE, LANES), marks)
    got = [
        lax.all_to_all(part, "blk", split_axis=0, concat_axis=0, tiled=True) for part in send
    ]

    table = make_table()
    got[0], table = lax.optimization_barrier((got[0], table))
    found = got[0][:, 2 * len(CHUNKS[0]) * TILE, :].astype(jnp.int32)
    units = jnp.arange(UNITS, dtype=jnp.int32)[:, None]
    place = jnp.sum(
        jnp.where(found[:, 0][None, :] == units, 2 * owners[None, :], 0)
        + jnp.where(found[:, LANES - 1][None, :] == units, 2 * owners[None, :] + 1, 0),
        axis=1,
    )
    place = jnp.clip(place, 0, 2 * blocks - 1)

    planes = 4
    plane = lax.axis_index("region") % planes
    edge = (plane == 0).astype(jnp.int32)
    core = lax.axis_index("blk") & 1
    early, *pieces = sort_units(place, got[0], 3 * TILE, planes - 1)
    piece, block = choose(plane, early, spread(pieces))
    twin = swapped(early)
    near, far, passed = from_previous_region(early, piece, planes, twin)
    two = shifted(early, "blk", 2)
    ahead = shifted(block, "blk", -2)
    beside = swapped(two)
    own, twin, two, ahead, beside, near, far = (
        [block] for block in ([block], [twin], [two], [ahead], [beside], [near], far)
    )
    by_four = cross(0, (((0, 1), (0, 1)),), core, (ahead, two), (), (passed,))
    sent = cross(0, (((1, 2), (0, 2)),), core, (own, ahead, beside), (by_four,))
    got_two = shifted(sent, "blk", 2)
    by_two = cross(0, (((0, 1), (0, 1)),), core, (own, two), (), (sent,))
    by_one = cross(0, (((0, 2), (0, 1)),), core, (own, twin, beside), (), (by_two,))
    by_region = cross(0, (((0, 1), (0, 2)),), edge, (own, near, far), (), (by_one,))
    cycle_series, region_series = lag_series(
        core, table, by_one, by_two, sent, got_two, by_region
    )
    return jnp.swapaxes(cycle_series, 2, 3), jnp.swapaxes(region_series, 1, 2)


def solution(mesh):
    placed = (P(("region", "blk"), None, None), P(("region", "blk")), P(("region", "blk")))
    return jax.shard_map(
        body,
        mesh=mesh,
        in_specs=placed,
        out_specs=(
            P(("region", "blk"), None, None, None, None),
            P(("region", "blk"), None, None, None),
        ),
        check_vma=False,
    )
```

```python
import functools
import math

import jax
import jax.numpy as jnp
from jax import lax
from jax.experimental import pallas as pl
from jax.experimental.pallas import tpu as pltpu
from jax.sharding import PartitionSpec as P

SB = 2
SEGS = 32
F = 1024
LAGS = 2048
HALF = 24
STEPS = 4
UNITS = 64
CAP = 128
LANES = 128
FH = F // LANES
TILE = 2 * FH
epsilon = 1e-05

CHUNKS = ((0, 1, 2),)
GROUP = 32
MARK = 8
PIECE = 16
VMEM = pl.BlockSpec(memory_space=pltpu.VMEM)
SMEM = pl.BlockSpec(memory_space=pltpu.SMEM)


def pairs_of(chunk):
    before = [c for part in CHUNKS[:chunk] for c in part]
    now = before + list(CHUNKS[chunk])
    return [(c, d) for c in now for d in now if not (c in before and d in before)]


def place_of(component):
    for chunk, part in enumerate(CHUNKS):
        if component in part:
            return chunk, part.index(component)


def whiten_kernel(source_ref, band_ref, inverse_ref, archive_ref, mark_ref, *rest):
    outs, (level_ref,) = rest[:-1], rest[-1:]
    rows = GROUP * FH
    band = band_ref[...]
    inverse = inverse_ref[...]
    lane = lax.broadcasted_iota(jnp.int32, (rows, LANES), 1)
    row = lax.broadcasted_iota(jnp.int32, (rows, LANES), 0) % FH
    outs[0][:, 2 * len(CHUNKS[0]) * TILE :, :] = mark_ref[...]

    def group(step, carry):
        base = step * GROUP

        def slab_of(position):
            return archive_ref[source_ref[base + position]].astype(jnp.float32)

        def magnitude(position, carry):
            slab = slab_of(position)
            total = None
            for c in range(3):
                real = slab[c * TILE : c * TILE + FH]
                imag = slab[c * TILE + FH : (c + 1) * TILE]
                size = jnp.sqrt(real * real + imag * imag)
                total = size if total is None else total + size
            start = pl.multiple_of(FH + position * FH, FH)
            level_ref[pl.ds(start, FH), :] = total * (1.0 / 3.0)
            return carry

        lax.fori_loop(0, GROUP, magnitude, 0, unroll=8)
        here = level_ref[FH : FH + rows, :]
        before = level_ref[FH - 1 : FH - 1 + rows, :]
        after = level_ref[FH + 1 : FH + 1 + rows, :]
        edge = jnp.where(
            lane >= LANES // 2,
            jnp.where(row == 0, 0.0, before),
            jnp.where(row == FH - 1, 0.0, after),
        )
        spread = jnp.concatenate([here, edge], axis=1)
        high = spread.astype(jnp.bfloat16)
        low = (spread - high.astype(jnp.float32)).astype(jnp.bfloat16)
        window = jnp.dot(high, band, preferred_element_type=jnp.float32) + jnp.dot(
            low, band, preferred_element_type=jnp.float32
        )
        level = window.reshape(GROUP, FH, LANES) * inverse[None] + epsilon
        level_ref[FH : FH + rows, :] = (1.0 / level).reshape(rows, LANES)

        def divide(pair, carry):
            for slot in range(2):
                position = 2 * pair + slot
                slab = slab_of(position)
                gain = level_ref[pl.ds(pl.multiple_of(FH + position * FH, FH), FH), :]
                for out, part in zip(outs, CHUNKS):
                    pieces = []
                    for c in part:
                        for half in range(2):
                            start = c * TILE + half * FH
                            pieces.append(slab[start : start + FH] * gain)
                    size = len(part) * TILE
                    out[base // 2 + pair, slot * size : (slot + 1) * size, :] = (
                        jnp.concatenate(pieces, axis=0).astype(jnp.bfloat16)
                    )
            return carry

        lax.fori_loop(0, GROUP // 2, divide, 0, unroll=4)
        return carry

    lax.fori_loop(0, CAP // GROUP, group, 0)


def whiten(source, archive, marks):
    low = jnp.arange(LANES, dtype=jnp.int32)
    gap = jnp.abs(low[:, None] - low[None, :])
    band = jnp.concatenate([gap <= HALF, gap >= LANES - HALF], axis=0).astype(jnp.bfloat16)
    bin_index = jnp.arange(F, dtype=jnp.int32)
    bin_count = (
        jnp.minimum(bin_index + HALF, F - 1) - jnp.maximum(bin_index - HALF, 0) + 1
    ).astype(jnp.float32)
    inverse = (1.0 / bin_count).reshape(FH, LANES)
    sizes = [2 * len(part) * TILE for part in CHUNKS]
    sizes[0] += MARK
    return pl.pallas_call(
        whiten_kernel,
        in_specs=[SMEM, VMEM, VMEM, VMEM, VMEM],
        out_specs=[VMEM for _ in sizes],
        out_shape=[
            jax.ShapeDtypeStruct((marks.shape[0], size, LANES), jnp.bfloat16) for size in sizes
        ],
        scratch_shapes=[pltpu.VMEM((GROUP * FH + 2 * FH, LANES), jnp.float32)],
        compiler_params=pltpu.CompilerParams(vmem_limit_bytes=8 * 1024 * 1024),
        cost_estimate=pl.CostEstimate(flops=200_000_000, bytes_accessed=4_000_000, transcendentals=0),
        name="whiten",
    )(source, band, inverse, archive, marks)


def sort_kernel(source_ref, got_ref, out_ref, *piece_refs):
    rows = out_ref.shape[1]

    def move(unit, carry):
        place = source_ref[unit]
        start = pl.multiple_of((place & 1) * rows, TILE)
        out_ref[unit] = got_ref[place >> 1, pl.ds(start, rows), :]
        return carry

    lax.fori_loop(0, UNITS, move, 0, unroll=8)
    for n, ref in enumerate(piece_refs):
        ref[...] = out_ref[n * PIECE : (n + 1) * PIECE]


def sort_units(source, got, rows, pieces):
    shapes = [(UNITS, rows, LANES)] + [(PIECE, rows, LANES)] * pieces
    return pl.pallas_call(
        sort_kernel,
        in_specs=[SMEM, VMEM],
        out_specs=[VMEM for _ in shapes],
        out_shape=[jax.ShapeDtypeStruct(shape, jnp.bfloat16) for shape in shapes],
        compiler_params=pltpu.CompilerParams(vmem_limit_bytes=6 * 1024 * 1024),
        cost_estimate=pl.CostEstimate(flops=0, bytes_accessed=3_000_000, transcendentals=0),
        name="sort_units",
    )(source, got)


def choose_kernel(plane_ref, block_ref, *refs):
    pieces, piece_ref = refs[:-1], refs[-1]
    last = len(pieces)
    for plane, ref in enumerate(pieces):

        @pl.when(plane_ref[0] == plane)
        def _(ref=ref):
            piece_ref[...] = ref[...]

    @pl.when(plane_ref[0] == last)
    def _():
        piece_ref[...] = block_ref[last * PIECE :]


def choose(plane, block, pieces):
    return pl.pallas_call(
        choose_kernel,
        in_specs=[SMEM] + [VMEM] * (1 + len(pieces)),
        out_specs=VMEM,
        out_shape=jax.ShapeDtypeStruct(pieces[0].shape, jnp.bfloat16),
        compiler_params=pltpu.CompilerParams(vmem_limit_bytes=6 * 1024 * 1024),
        cost_estimate=pl.CostEstimate(flops=20_000_000_000, bytes_accessed=2_000_000, transcendentals=0),
        name="choose_piece",
    )(plane.reshape(1), block, *pieces)


def relay_kernel(piece_ref, *refs):
    refs[-1][...] = piece_ref[...]


def relay(piece, *after):
    return pl.pallas_call(
        relay_kernel,
        in_specs=[VMEM] + [pl.BlockSpec(memory_space=pl.ANY)] * len(after),
        out_specs=VMEM,
        out_shape=jax.ShapeDtypeStruct(piece.shape, jnp.bfloat16),
        compiler_params=pltpu.CompilerParams(vmem_limit_bytes=4 * 1024 * 1024),
        cost_estimate=pl.CostEstimate(flops=20_000_000_000, bytes_accessed=400_000, transcendentals=0),
        name="relay_piece",
    )(piece, *after)


def products(left_block, right_block, chunk, store):
    pairs = pairs_of(chunk)

    def load(block, base, m, component):
        which, at = place_of(component)
        pieces = block[which]
        if len(pieces) > 1:
            ref, unit = pieces[base // PIECE], m
        else:
            ref, unit = pieces[0], base + m
        tile = ref[unit, at * TILE : (at + 1) * TILE, :].astype(jnp.float32)
        return tile[:FH], tile[FH:]

    firsts = sorted({c for c, _ in pairs})
    seconds = sorted({d for _, d in pairs})
    for i in range(SB):
        for j in range(SB):
            zero = jnp.zeros((FH, LANES), jnp.float32)
            sums = tuple((zero, zero) for _ in pairs)
            for start in range(0, SEGS, PIECE):

                def step(m, sums, start=start):
                    left = {c: load(left_block, i * SEGS + start, m, c) for c in firsts}
                    right = {d: load(right_block, j * SEGS + start, m, d) for d in seconds}
                    new = []
                    for n, (c, d) in enumerate(pairs):
                        real, imag = sums[n]
                        (ar, ai), (br, bi) = left[c], right[d]
                        new.append((real + ar * br + ai * bi, imag + ai * br - ar * bi))
                    return tuple(new)

                sums = lax.fori_loop(0, PIECE, step, sums, unroll=2)
            for n, (real, imag) in enumerate(sums):
                store(i, j, n, jnp.concatenate([real, imag], axis=0).astype(jnp.bfloat16))


def cross_kernel(chunk, plan, counts, carried, flag_ref, *refs):
    blocks, at = [], 0
    for count in counts:
        block = []
        for _ in range(chunk + 1):
            block.append(refs[at : at + count])
            at += count
        blocks.append(block)
    out = refs[-1]
    size = SB * SB
    for slot in range(carried):
        out[slot * size : (slot + 1) * size] = refs[at + slot][...]
    for slot, (when_zero, when_one) in enumerate(plan, carried):

        def store(i, j, n, tile, slot=slot):
            out[slot * size + i * SB + j, n] = tile

        if when_zero == when_one:
            products(blocks[when_zero[0]], blocks[when_zero[1]], chunk, store)
        else:
            for value, (left, right) in ((0, when_zero), (1, when_one)):

                @pl.when(flag_ref[0] == value)
                def _(right=right, left=left, store=store):
                    products(blocks[left], blocks[right], chunk, store)


def cross(chunk, plan, flag, blocks, carried=(), after=()):
    count = len(pairs_of(chunk))
    shape = ((len(carried) + len(plan)) * SB * SB, count, TILE, LANES)
    flat = [piece for block in blocks for part in block[: chunk + 1] for piece in part]
    flat += carried
    return pl.pallas_call(
        functools.partial(
            cross_kernel, chunk, plan, tuple(len(block[0]) for block in blocks), len(carried)
        ),
        in_specs=[SMEM]
        + [VMEM] * len(flat)
        + [pl.BlockSpec(memory_space=pl.ANY)] * len(after),
        out_specs=VMEM,
        out_shape=jax.ShapeDtypeStruct(shape, jnp.bfloat16),
        compiler_params=pltpu.CompilerParams(vmem_limit_bytes=8 * 1024 * 1024),
        cost_estimate=pl.CostEstimate(
            flops=len(plan) * 40_000_000, bytes_accessed=len(plan) * 1_500_000, transcendentals=0
        ),
        name="cross",
    )(flag.reshape(1), *flat, *after)


COLUMNS = 256
CYCLE_ROWS = SB * STEPS * 9 * SB
ALL_ROWS = CYCLE_ROWS + SB * 9 * SB


def series_kernel(core_ref, table_ref, one_ref, two_ref, kept_ref, got_ref, across_ref, *refs):
    cycle_ref, region_ref, wide_ref, rows_ref, held_ref, sems = refs
    step = pl.program_id(0)
    size = SB * SB

    def fetch(n):
        return pltpu.make_async_copy(table_ref.at[n], held_ref.at[n], sems.at[n])

    def place(k, source, first):
        for i in range(SB):
            for j in range(SB):
                for n, (c, d) in enumerate(pairs_of(0)):
                    if k < STEPS:
                        row = ((i * STEPS + k) * 9 + 3 * c + d) * SB + j
                    else:
                        row = CYCLE_ROWS + (i * 9 + 3 * c + d) * SB + j
                    wide_ref[row * TILE : (row + 1) * TILE, :] = source[
                        first + i * SB + j, n
                    ].astype(jnp.float32)

    @pl.when(step == 0)
    def _():
        for n in range(LAGS // COLUMNS):
            fetch(n).start()
        place(0, one_ref, 0)
        place(1, two_ref, 0)
        place(3, got_ref, 0)
        place(4, across_ref, 0)

        @pl.when(core_ref[0] == 0)
        def _():
            place(2, got_ref, size)

        @pl.when(core_ref[0] == 1)
        def _():
            place(2, kept_ref, size)

        for piece in range(TILE):
            rows_ref[:, piece * LANES : (piece + 1) * LANES] = wide_ref[
                pl.ds(piece, ALL_ROWS, stride=TILE), :
            ].astype(jnp.bfloat16)

    fetch(step).wait()
    series = jnp.dot(rows_ref[...], held_ref[step], preferred_element_type=jnp.float32)
    series = (series * (1.0 / math.sqrt(F * SEGS))).astype(jnp.bfloat16)
    for i in range(SB):
        for k in range(STEPS):
            for n in range(9):
                row = ((i * STEPS + k) * 9 + n) * SB
                cycle_ref[i, k, n] = series[row : row + SB]
        for n in range(9):
            row = CYCLE_ROWS + (i * 9 + n) * SB
            region_ref[i, n] = series[row : row + SB]


def lag_series(core, table, *sources):
    return pl.pallas_call(
        series_kernel,
        grid=(LAGS // COLUMNS,),
        in_specs=[SMEM, pl.BlockSpec(memory_space=pl.ANY)] + [VMEM] * len(sources),
        out_specs=[
            pl.BlockSpec((SB, STEPS, 9, SB, COLUMNS), lambda n: (0, 0, 0, 0, n)),
            pl.BlockSpec((SB, 9, SB, COLUMNS), lambda n: (0, 0, 0, n)),
        ],
        out_shape=[
            jax.ShapeDtypeStruct((SB, STEPS, 9, SB, LAGS), jnp.bfloat16),
            jax.ShapeDtypeStruct((SB, 9, SB, LAGS), jnp.bfloat16),
        ],
        scratch_shapes=[
            pltpu.VMEM((ALL_ROWS * TILE, LANES), jnp.float32),
            pltpu.VMEM((ALL_ROWS, 2 * F), jnp.bfloat16),
            pltpu.VMEM((LAGS // COLUMNS, 2 * F, COLUMNS), jnp.bfloat16),
            pltpu.SemaphoreType.DMA((LAGS // COLUMNS,)),
        ],
        compiler_params=pltpu.CompilerParams(vmem_limit_bytes=18 * 1024 * 1024),
        cost_estimate=pl.CostEstimate(
            flops=2 * ALL_ROWS * 2 * F * LAGS, bytes_accessed=12_000_000, transcendentals=0
        ),
        name="lag_series",
    )(core.reshape(1), pltpu.with_memory_space_constraint(table, pltpu.HBM), *sources)


def table_kernel(fine_ref, coarse_ref, out_ref):
    step = pl.program_id(0)
    for high in range(FH):
        cos_high = coarse_ref[0, high : high + 1, :]
        sin_high = coarse_ref[1, high : high + 1, :]
        cos_low, sin_low = fine_ref[0], fine_ref[1]

        @pl.when(step == 0)
        def _(high=high):
            out_ref[0, high * LANES : (high + 1) * LANES, :] = (
                cos_low * cos_high - sin_low * sin_high
            ).astype(jnp.bfloat16)

        @pl.when(step == 1)
        def _(high=high):
            out_ref[0, high * LANES : (high + 1) * LANES, :] = (
                -(sin_low * cos_high + cos_low * sin_high)
            ).astype(jnp.bfloat16)


def make_table():
    lag_index = jnp.arange(LAGS, dtype=jnp.int32) - LAGS // 2

    def angles(bins):
        phase = bins[:, None] * lag_index[None, :] % (2 * F)
        angle = phase.astype(jnp.float32) * (math.pi / F)
        return jnp.stack([jnp.cos(angle), jnp.sin(angle)])

    fine = angles(jnp.arange(LANES, dtype=jnp.int32))
    coarse = angles(LANES * jnp.arange(FH, dtype=jnp.int32))
    return pl.pallas_call(
        table_kernel,
        grid=(2, LAGS // COLUMNS),
        in_specs=[
            pl.BlockSpec((2, LANES, COLUMNS), lambda s, n: (0, 0, n)),
            pl.BlockSpec((2, FH, COLUMNS), lambda s, n: (0, 0, n)),
        ],
        out_specs=pl.BlockSpec((1, F, COLUMNS), lambda s, n: (n, s, 0)),
        out_shape=pltpu.HBM((LAGS // COLUMNS, 2 * F, COLUMNS), jnp.bfloat16),
        compiler_params=pltpu.CompilerParams(vmem_limit_bytes=8 * 1024 * 1024),
        cost_estimate=pl.CostEstimate(flops=16_000_000, bytes_accessed=12_000_000, transcendentals=0),
        name="lag_table",
    )(fine, coarse)


def shifted(block, axis, by):
    size = lax.axis_size(axis)
    return lax.ppermute(block, axis, [(i, (i + by) % size) for i in range(size)])


def swapped(block):
    return lax.ppermute(block, "blk", [(i, i ^ 1) for i in range(lax.axis_size("blk"))])


def spread(pieces):
    planes = len(pieces) + 1
    starts = range(0, lax.axis_size("region"), planes)
    return [
        lax.ppermute(piece, "region", [(n + planes - 1, n + plane) for n in starts])
        for plane, piece in enumerate(pieces)
    ]


def from_previous_region(block, piece, planes, *after):
    regions = lax.axis_size("region")
    near = lax.ppermute(
        block, "region", [(i, i + 1) for i in range(regions) if (i + 1) % planes]
    )
    piece = lax.ppermute(piece, "region", [(i, (i + planes) % regions) for i in range(regions)])
    far = [piece]
    piece = relay(piece, near, *after)
    for plane in range(1, planes):
        far.append(
            lax.ppermute(piece, "region", [(n + plane, n) for n in range(0, regions, planes)])
        )
    return near, far, piece


def body(archive, unit_of, row_counts):
    blocks = lax.axis_size("blk")
    slot = jnp.arange(CAP, dtype=jnp.int32)
    ids = jnp.where(slot < row_counts[0], unit_of, -1)
    owners = jnp.arange(blocks, dtype=jnp.int32)
    sent = (ids >> 6)[None, :] == owners[:, None]
    key = slot * UNITS + (ids & (UNITS - 1))
    none = CAP * UNITS
    first = jnp.min(jnp.where(sent, key, none), axis=1)
    last = jnp.max(jnp.where(sent, key, -1), axis=1)
    source = jnp.clip(jnp.stack([first, last], axis=1) >> 6, 0, CAP - 1).reshape(2 * blocks)
    first_id = jnp.where(first < none, first & (UNITS - 1), -1).astype(jnp.bfloat16)
    last_id = jnp.where(last > first, last & (UNITS - 1), -1).astype(jnp.bfloat16)
    lane = jnp.arange(LANES, dtype=jnp.int32)
    marks = jnp.broadcast_to(
        jnp.where(lane[None, :] < LANES // 2, first_id[:, None], last_id[:, None])[:, None, :],
        (blocks, MARK, LANES),
    )
    send = whiten(source, archive.reshape(CAP, 3 * TILE, LANES), marks)
    got = [
        lax.all_to_all(part, "blk", split_axis=0, concat_axis=0, tiled=True) for part in send
    ]

    table = make_table()
    got[0], table = lax.optimization_barrier((got[0], table))
    found = got[0][:, 2 * len(CHUNKS[0]) * TILE, :].astype(jnp.int32)
    units = jnp.arange(UNITS, dtype=jnp.int32)[:, None]
    place = jnp.sum(
        jnp.where(found[:, 0][None, :] == units, 2 * owners[None, :], 0)
        + jnp.where(found[:, LANES - 1][None, :] == units, 2 * owners[None, :] + 1, 0),
        axis=1,
    )
    place = jnp.clip(place, 0, 2 * blocks - 1)

    planes = 4
    plane = lax.axis_index("region") % planes
    edge = (plane == 0).astype(jnp.int32)
    core = lax.axis_index("blk") & 1
    block, *pieces = sort_units(place, got[0], 3 * TILE, planes - 1)
    piece = choose(plane, block, spread(pieces))
    twin = swapped(block)
    near, far, passed = from_previous_region(block, piece, planes, twin)
    two = shifted(block, "blk", 2)
    ahead = shifted(block, "blk", -2)
    beside = swapped(two)
    own, twin, two, ahead, beside, near, far = (
        [block] for block in ([block], [twin], [two], [ahead], [beside], [near], far)
    )
    by_four = cross(0, (((0, 1), (0, 1)),), core, (ahead, two), (), (passed,))
    sent = cross(0, (((1, 2), (0, 2)),), core, (own, ahead, beside), (by_four,))
    got_two = shifted(sent, "blk", 2)
    by_two = cross(0, (((0, 1), (0, 1)),), core, (own, two), (), (sent,))
    by_one = cross(0, (((0, 2), (0, 1)),), core, (own, twin, beside), (), (by_two,))
    by_region = cross(0, (((0, 1), (0, 2)),), edge, (own, near, far), (), (by_one,))
    cycle_series, region_series = lag_series(
        core, table, by_one, by_two, sent, got_two, by_region
    )
    return jnp.swapaxes(cycle_series, 2, 3), jnp.swapaxes(region_series, 1, 2)


def solution(mesh):
    placed = (P(("region", "blk"), None, None), P(("region", "blk")), P(("region", "blk")))
    return jax.shard_map(
        body,
        mesh=mesh,
        in_specs=placed,
        out_specs=(
            P(("region", "blk"), None, None, None, None),
            P(("region", "blk"), None, None, None),
        ),
        check_vma=False,
    )
```

```python
import functools
import math

import jax
import jax.numpy as jnp
from jax import lax
from jax.experimental import pallas as pl
from jax.experimental.pallas import tpu as pltpu
from jax.sharding import PartitionSpec as P

SB = 2
SEGS = 32
F = 1024
LAGS = 2048
HALF = 24
STEPS = 4
UNITS = 64
CAP = 128
LANES = 128
FH = F // LANES
TILE = 2 * FH
epsilon = 1e-05

CHUNKS = ((0, 1, 2),)
GROUP = 32
MARK = 8
PIECE = 16
VMEM = pl.BlockSpec(memory_space=pltpu.VMEM)
SMEM = pl.BlockSpec(memory_space=pltpu.SMEM)


def pairs_of(chunk):
    before = [c for part in CHUNKS[:chunk] for c in part]
    now = before + list(CHUNKS[chunk])
    return [(c, d) for c in now for d in now if not (c in before and d in before)]


def place_of(component):
    for chunk, part in enumerate(CHUNKS):
        if component in part:
            return chunk, part.index(component)


def whiten_kernel(source_ref, band_ref, inverse_ref, archive_ref, mark_ref, *rest):
    outs, (level_ref,) = rest[:-1], rest[-1:]
    rows = GROUP * FH
    band = band_ref[...]
    inverse = inverse_ref[...]
    lane = lax.broadcasted_iota(jnp.int32, (rows, LANES), 1)
    row = lax.broadcasted_iota(jnp.int32, (rows, LANES), 0) % FH
    outs[0][:, 2 * len(CHUNKS[0]) * TILE :, :] = mark_ref[...]

    def group(step, carry):
        base = step * GROUP

        def slab_of(position):
            return archive_ref[source_ref[base + position]].astype(jnp.float32)

        def magnitude(position, carry):
            slab = slab_of(position)
            total = None
            for c in range(3):
                real = slab[c * TILE : c * TILE + FH]
                imag = slab[c * TILE + FH : (c + 1) * TILE]
                size = jnp.sqrt(real * real + imag * imag)
                total = size if total is None else total + size
            start = pl.multiple_of(FH + position * FH, FH)
            level_ref[pl.ds(start, FH), :] = total * (1.0 / 3.0)
            return carry

        lax.fori_loop(0, GROUP, magnitude, 0, unroll=8)
        here = level_ref[FH : FH + rows, :]
        before = level_ref[FH - 1 : FH - 1 + rows, :]
        after = level_ref[FH + 1 : FH + 1 + rows, :]
        edge = jnp.where(
            lane >= LANES // 2,
            jnp.where(row == 0, 0.0, before),
            jnp.where(row == FH - 1, 0.0, after),
        )
        spread = jnp.concatenate([here, edge], axis=1)
        high = spread.astype(jnp.bfloat16)
        low = (spread - high.astype(jnp.float32)).astype(jnp.bfloat16)
        window = jnp.dot(high, band, preferred_element_type=jnp.float32) + jnp.dot(
            low, band, preferred_element_type=jnp.float32
        )
        level = window.reshape(GROUP, FH, LANES) * inverse[None] + epsilon
        level_ref[FH : FH + rows, :] = (1.0 / level).reshape(rows, LANES)

        def divide(pair, carry):
            for slot in range(2):
                position = 2 * pair + slot
                slab = slab_of(position)
                gain = level_ref[pl.ds(pl.multiple_of(FH + position * FH, FH), FH), :]
                for out, part in zip(outs, CHUNKS):
                    pieces = []
                    for c in part:
                        for half in range(2):
                            start = c * TILE + half * FH
                            pieces.append(slab[start : start + FH] * gain)
                    size = len(part) * TILE
                    out[base // 2 + pair, slot * size : (slot + 1) * size, :] = (
                        jnp.concatenate(pieces, axis=0).astype(jnp.bfloat16)
                    )
            return carry

        lax.fori_loop(0, GROUP // 2, divide, 0, unroll=4)
        return carry

    lax.fori_loop(0, CAP // GROUP, group, 0)


def whiten(source, archive, marks):
    low = jnp.arange(LANES, dtype=jnp.int32)
    gap = jnp.abs(low[:, None] - low[None, :])
    band = jnp.concatenate([gap <= HALF, gap >= LANES - HALF], axis=0).astype(jnp.bfloat16)
    bin_index = jnp.arange(F, dtype=jnp.int32)
    bin_count = (
        jnp.minimum(bin_index + HALF, F - 1) - jnp.maximum(bin_index - HALF, 0) + 1
    ).astype(jnp.float32)
    inverse = (1.0 / bin_count).reshape(FH, LANES)
    sizes = [2 * len(part) * TILE for part in CHUNKS]
    sizes[0] += MARK
    return pl.pallas_call(
        whiten_kernel,
        in_specs=[SMEM, VMEM, VMEM, VMEM, VMEM],
        out_specs=[VMEM for _ in sizes],
        out_shape=[
            jax.ShapeDtypeStruct((marks.shape[0], size, LANES), jnp.bfloat16) for size in sizes
        ],
        scratch_shapes=[pltpu.VMEM((GROUP * FH + 2 * FH, LANES), jnp.float32)],
        compiler_params=pltpu.CompilerParams(vmem_limit_bytes=8 * 1024 * 1024),
        cost_estimate=pl.CostEstimate(flops=200_000_000, bytes_accessed=4_000_000, transcendentals=0),
        name="whiten",
    )(source, band, inverse, archive, marks)


def sort_kernel(source_ref, got_ref, out_ref, *piece_refs):
    rows = out_ref.shape[1]

    def move(unit, carry):
        place = source_ref[unit]
        start = pl.multiple_of((place & 1) * rows, TILE)
        out_ref[unit] = got_ref[place >> 1, pl.ds(start, rows), :]
        return carry

    lax.fori_loop(0, UNITS, move, 0, unroll=8)
    for n, ref in enumerate(piece_refs):
        ref[...] = out_ref[n * PIECE : (n + 1) * PIECE]


def sort_units(source, got, rows, pieces):
    shapes = [(UNITS, rows, LANES)] + [(PIECE, rows, LANES)] * pieces
    return pl.pallas_call(
        sort_kernel,
        in_specs=[SMEM, VMEM],
        out_specs=[VMEM for _ in shapes],
        out_shape=[jax.ShapeDtypeStruct(shape, jnp.bfloat16) for shape in shapes],
        compiler_params=pltpu.CompilerParams(vmem_limit_bytes=6 * 1024 * 1024),
        cost_estimate=pl.CostEstimate(flops=0, bytes_accessed=3_000_000, transcendentals=0),
        name="sort_units",
    )(source, got)


def choose_kernel(plane_ref, block_ref, *refs):
    pieces, piece_ref = refs[:-1], refs[-1]
    last = len(pieces)
    for plane, ref in enumerate(pieces):

        @pl.when(plane_ref[0] == plane)
        def _(ref=ref):
            piece_ref[...] = ref[...]

    @pl.when(plane_ref[0] == last)
    def _():
        piece_ref[...] = block_ref[last * PIECE :]


def choose(plane, block, pieces):
    return pl.pallas_call(
        choose_kernel,
        in_specs=[SMEM] + [VMEM] * (1 + len(pieces)),
        out_specs=VMEM,
        out_shape=jax.ShapeDtypeStruct(pieces[0].shape, jnp.bfloat16),
        compiler_params=pltpu.CompilerParams(vmem_limit_bytes=6 * 1024 * 1024),
        cost_estimate=pl.CostEstimate(flops=20_000_000_000, bytes_accessed=2_000_000, transcendentals=0),
        name="choose_piece",
    )(plane.reshape(1), block, *pieces)


def relay_kernel(piece_ref, *refs):
    refs[-1][...] = piece_ref[...]


def relay(piece, *after):
    return pl.pallas_call(
        relay_kernel,
        in_specs=[VMEM] + [pl.BlockSpec(memory_space=pl.ANY)] * len(after),
        out_specs=VMEM,
        out_shape=jax.ShapeDtypeStruct(piece.shape, jnp.bfloat16),
        compiler_params=pltpu.CompilerParams(vmem_limit_bytes=4 * 1024 * 1024),
        cost_estimate=pl.CostEstimate(flops=20_000_000_000, bytes_accessed=400_000, transcendentals=0),
        name="relay_piece",
    )(piece, *after)


def products(left_block, right_block, chunk, store):
    pairs = pairs_of(chunk)

    def load(block, base, m, component):
        which, at = place_of(component)
        pieces = block[which]
        if len(pieces) > 1:
            ref, unit = pieces[base // PIECE], m
        else:
            ref, unit = pieces[0], base + m
        tile = ref[unit, at * TILE : (at + 1) * TILE, :].astype(jnp.float32)
        return tile[:FH], tile[FH:]

    firsts = sorted({c for c, _ in pairs})
    seconds = sorted({d for _, d in pairs})
    for i in range(SB):
        for j in range(SB):
            zero = jnp.zeros((FH, LANES), jnp.float32)
            sums = tuple((zero, zero) for _ in pairs)
            for start in range(0, SEGS, PIECE):

                def step(m, sums, start=start):
                    left = {c: load(left_block, i * SEGS + start, m, c) for c in firsts}
                    right = {d: load(right_block, j * SEGS + start, m, d) for d in seconds}
                    new = []
                    for n, (c, d) in enumerate(pairs):
                        real, imag = sums[n]
                        (ar, ai), (br, bi) = left[c], right[d]
                        new.append((real + ar * br + ai * bi, imag + ai * br - ar * bi))
                    return tuple(new)

                sums = lax.fori_loop(0, PIECE, step, sums, unroll=2)
            for n, (real, imag) in enumerate(sums):
                store(i, j, n, jnp.concatenate([real, imag], axis=0).astype(jnp.bfloat16))


def cross_kernel(chunk, plan, counts, carried, flag_ref, *refs):
    blocks, at = [], 0
    for count in counts:
        block = []
        for _ in range(chunk + 1):
            block.append(refs[at : at + count])
            at += count
        blocks.append(block)
    out = refs[-1]
    size = SB * SB
    for slot in range(carried):
        out[slot * size : (slot + 1) * size] = refs[at + slot][...]
    for slot, (when_zero, when_one) in enumerate(plan, carried):

        def store(i, j, n, tile, slot=slot):
            out[slot * size + i * SB + j, n] = tile

        if when_zero == when_one:
            products(blocks[when_zero[0]], blocks[when_zero[1]], chunk, store)
        else:
            for value, (left, right) in ((0, when_zero), (1, when_one)):

                @pl.when(flag_ref[0] == value)
                def _(right=right, left=left, store=store):
                    products(blocks[left], blocks[right], chunk, store)


def cross(chunk, plan, flag, blocks, carried=(), after=()):
    count = len(pairs_of(chunk))
    shape = ((len(carried) + len(plan)) * SB * SB, count, TILE, LANES)
    flat = [piece for block in blocks for part in block[: chunk + 1] for piece in part]
    flat += carried
    return pl.pallas_call(
        functools.partial(
            cross_kernel, chunk, plan, tuple(len(block[0]) for block in blocks), len(carried)
        ),
        in_specs=[SMEM]
        + [VMEM] * len(flat)
        + [pl.BlockSpec(memory_space=pl.ANY)] * len(after),
        out_specs=VMEM,
        out_shape=jax.ShapeDtypeStruct(shape, jnp.bfloat16),
        compiler_params=pltpu.CompilerParams(vmem_limit_bytes=8 * 1024 * 1024),
        cost_estimate=pl.CostEstimate(
            flops=len(plan) * 40_000_000, bytes_accessed=len(plan) * 1_500_000, transcendentals=0
        ),
        name="cross",
    )(flag.reshape(1), *flat, *after)


COLUMNS = 256
CYCLE_ROWS = SB * STEPS * 9 * SB
ALL_ROWS = CYCLE_ROWS + SB * 9 * SB


def series_kernel(core_ref, table_ref, one_ref, two_ref, kept_ref, got_ref, across_ref, *refs):
    cycle_ref, region_ref, wide_ref, rows_ref, held_ref, sems = refs
    step = pl.program_id(0)
    size = SB * SB

    def fetch(n):
        return pltpu.make_async_copy(table_ref.at[n], held_ref.at[n], sems.at[n])

    def place(k, source, first):
        for i in range(SB):
            for j in range(SB):
                for n, (c, d) in enumerate(pairs_of(0)):
                    if k < STEPS:
                        row = ((i * STEPS + k) * 9 + 3 * c + d) * SB + j
                    else:
                        row = CYCLE_ROWS + (i * 9 + 3 * c + d) * SB + j
                    wide_ref[row * TILE : (row + 1) * TILE, :] = source[
                        first + i * SB + j, n
                    ].astype(jnp.float32)

    @pl.when(step == 0)
    def _():
        for n in range(LAGS // COLUMNS):
            fetch(n).start()
        place(0, one_ref, 0)
        place(1, two_ref, 0)
        place(3, got_ref, 0)
        place(4, across_ref, 0)

        @pl.when(core_ref[0] == 0)
        def _():
            place(2, got_ref, size)

        @pl.when(core_ref[0] == 1)
        def _():
            place(2, kept_ref, size)

        for piece in range(TILE):
            rows_ref[:, piece * LANES : (piece + 1) * LANES] = wide_ref[
                pl.ds(piece, ALL_ROWS, stride=TILE), :
            ].astype(jnp.bfloat16)

    fetch(step).wait()
    series = jnp.dot(rows_ref[...], held_ref[step], preferred_element_type=jnp.float32)
    series = (series * (1.0 / math.sqrt(F * SEGS))).astype(jnp.bfloat16)
    for i in range(SB):
        for k in range(STEPS):
            for n in range(9):
                row = ((i * STEPS + k) * 9 + n) * SB
                cycle_ref[i, k, n] = series[row : row + SB]
        for n in range(9):
            row = CYCLE_ROWS + (i * 9 + n) * SB
            region_ref[i, n] = series[row : row + SB]


def lag_series(core, table, *sources):
    return pl.pallas_call(
        series_kernel,
        grid=(LAGS // COLUMNS,),
        in_specs=[SMEM, pl.BlockSpec(memory_space=pl.ANY)] + [VMEM] * len(sources),
        out_specs=[
            pl.BlockSpec((SB, STEPS, 9, SB, COLUMNS), lambda n: (0, 0, 0, 0, n)),
            pl.BlockSpec((SB, 9, SB, COLUMNS), lambda n: (0, 0, 0, n)),
        ],
        out_shape=[
            jax.ShapeDtypeStruct((SB, STEPS, 9, SB, LAGS), jnp.bfloat16),
            jax.ShapeDtypeStruct((SB, 9, SB, LAGS), jnp.bfloat16),
        ],
        scratch_shapes=[
            pltpu.VMEM((ALL_ROWS * TILE, LANES), jnp.float32),
            pltpu.VMEM((ALL_ROWS, 2 * F), jnp.bfloat16),
            pltpu.VMEM((LAGS // COLUMNS, 2 * F, COLUMNS), jnp.bfloat16),
            pltpu.SemaphoreType.DMA((LAGS // COLUMNS,)),
        ],
        compiler_params=pltpu.CompilerParams(vmem_limit_bytes=18 * 1024 * 1024),
        cost_estimate=pl.CostEstimate(
            flops=2 * ALL_ROWS * 2 * F * LAGS, bytes_accessed=12_000_000, transcendentals=0
        ),
        name="lag_series",
    )(core.reshape(1), pltpu.with_memory_space_constraint(table, pltpu.HBM), *sources)


def table_kernel(fine_ref, coarse_ref, out_ref):
    step = pl.program_id(0)
    for high in range(FH):
        cos_high = coarse_ref[0, high : high + 1, :]
        sin_high = coarse_ref[1, high : high + 1, :]
        cos_low, sin_low = fine_ref[0], fine_ref[1]

        @pl.when(step == 0)
        def _(high=high):
            out_ref[0, high * LANES : (high + 1) * LANES, :] = (
                cos_low * cos_high - sin_low * sin_high
            ).astype(jnp.bfloat16)

        @pl.when(step == 1)
        def _(high=high):
            out_ref[0, high * LANES : (high + 1) * LANES, :] = (
                -(sin_low * cos_high + cos_low * sin_high)
            ).astype(jnp.bfloat16)


def make_table():
    lag_index = jnp.arange(LAGS, dtype=jnp.int32) - LAGS // 2

    def angles(bins):
        phase = bins[:, None] * lag_index[None, :] % (2 * F)
        angle = phase.astype(jnp.float32) * (math.pi / F)
        return jnp.stack([jnp.cos(angle), jnp.sin(angle)])

    fine = angles(jnp.arange(LANES, dtype=jnp.int32))
    coarse = angles(LANES * jnp.arange(FH, dtype=jnp.int32))
    return pl.pallas_call(
        table_kernel,
        grid=(2, LAGS // COLUMNS),
        in_specs=[
            pl.BlockSpec((2, LANES, COLUMNS), lambda s, n: (0, 0, n)),
            pl.BlockSpec((2, FH, COLUMNS), lambda s, n: (0, 0, n)),
        ],
        out_specs=pl.BlockSpec((1, F, COLUMNS), lambda s, n: (n, s, 0)),
        out_shape=pltpu.HBM((LAGS // COLUMNS, 2 * F, COLUMNS), jnp.bfloat16),
        compiler_params=pltpu.CompilerParams(vmem_limit_bytes=8 * 1024 * 1024),
        cost_estimate=pl.CostEstimate(flops=16_000_000, bytes_accessed=12_000_000, transcendentals=0),
        name="lag_table",
    )(fine, coarse)


def shifted(block, axis, by):
    size = lax.axis_size(axis)
    return lax.ppermute(block, axis, [(i, (i + by) % size) for i in range(size)])


def swapped(block):
    return lax.ppermute(block, "blk", [(i, i ^ 1) for i in range(lax.axis_size("blk"))])


def spread(pieces):
    planes = len(pieces) + 1
    starts = range(0, lax.axis_size("region"), planes)
    return [
        lax.ppermute(piece, "region", [(n + planes - 1, n + plane) for n in starts])
        for plane, piece in enumerate(pieces)
    ]


def from_previous_region(block, piece, planes, *after):
    regions = lax.axis_size("region")
    near = lax.ppermute(
        block, "region", [(i, i + 1) for i in range(regions) if (i + 1) % planes]
    )
    piece = lax.ppermute(piece, "region", [(i, (i + planes) % regions) for i in range(regions)])
    far = [piece]
    piece = relay(piece)
    for plane in range(1, planes):
        far.append(
            lax.ppermute(piece, "region", [(n + plane, n) for n in range(0, regions, planes)])
        )
    return near, far, piece


def body(archive, unit_of, row_counts):
    blocks = lax.axis_size("blk")
    slot = jnp.arange(CAP, dtype=jnp.int32)
    ids = jnp.where(slot < row_counts[0], unit_of, -1)
    owners = jnp.arange(blocks, dtype=jnp.int32)
    sent = (ids >> 6)[None, :] == owners[:, None]
    key = slot * UNITS + (ids & (UNITS - 1))
    none = CAP * UNITS
    first = jnp.min(jnp.where(sent, key, none), axis=1)
    last = jnp.max(jnp.where(sent, key, -1), axis=1)
    source = jnp.clip(jnp.stack([first, last], axis=1) >> 6, 0, CAP - 1).reshape(2 * blocks)
    first_id = jnp.where(first < none, first & (UNITS - 1), -1).astype(jnp.bfloat16)
    last_id = jnp.where(last > first, last & (UNITS - 1), -1).astype(jnp.bfloat16)
    lane = jnp.arange(LANES, dtype=jnp.int32)
    marks = jnp.broadcast_to(
        jnp.where(lane[None, :] < LANES // 2, first_id[:, None], last_id[:, None])[:, None, :],
        (blocks, MARK, LANES),
    )
    send = whiten(source, archive.reshape(CAP, 3 * TILE, LANES), marks)
    got = [
        lax.all_to_all(part, "blk", split_axis=0, concat_axis=0, tiled=True) for part in send
    ]

    table = make_table()
    got[0], table = lax.optimization_barrier((got[0], table))
    found = got[0][:, 2 * len(CHUNKS[0]) * TILE, :].astype(jnp.int32)
    units = jnp.arange(UNITS, dtype=jnp.int32)[:, None]
    place = jnp.sum(
        jnp.where(found[:, 0][None, :] == units, 2 * owners[None, :], 0)
        + jnp.where(found[:, LANES - 1][None, :] == units, 2 * owners[None, :] + 1, 0),
        axis=1,
    )
    place = jnp.clip(place, 0, 2 * blocks - 1)

    planes = 4
    plane = lax.axis_index("region") % planes
    edge = (plane == 0).astype(jnp.int32)
    core = lax.axis_index("blk") & 1
    block, *pieces = sort_units(place, got[0], 3 * TILE, planes - 1)
    piece = choose(plane, block, spread(pieces))
    twin = swapped(block)
    near, far, passed = from_previous_region(block, piece, planes, twin)
    two = shifted(block, "blk", 2)
    ahead = shifted(block, "blk", -2)
    beside = swapped(two)
    own, twin, two, ahead, beside, near, far = (
        [block] for block in ([block], [twin], [two], [ahead], [beside], [near], far)
    )
    by_four = cross(0, (((0, 1), (0, 1)),), core, (ahead, two), (), (passed,))
    sent = cross(0, (((1, 2), (0, 2)),), core, (own, ahead, beside), (by_four,))
    got_two = shifted(sent, "blk", 2)
    by_two = cross(0, (((0, 1), (0, 1)),), core, (own, two), (), (sent,))
    by_one = cross(0, (((0, 2), (0, 1)),), core, (own, twin, beside), (), (by_two,))
    by_region = cross(0, (((0, 1), (0, 2)),), edge, (own, near, far), (), (by_one,))
    cycle_series, region_series = lag_series(
        core, table, by_one, by_two, sent, got_two, by_region
    )
    return jnp.swapaxes(cycle_series, 2, 3), jnp.swapaxes(region_series, 1, 2)


def solution(mesh):
    placed = (P(("region", "blk"), None, None), P(("region", "blk")), P(("region", "blk")))
    return jax.shard_map(
        body,
        mesh=mesh,
        in_specs=placed,
        out_specs=(
            P(("region", "blk"), None, None, None, None),
            P(("region", "blk"), None, None, None),
        ),
        check_vma=False,
    )
```
